32 devices in a mesh: ctx: 8 (over y, x, core), head: 4 (over z).
Axes of the slice: x: 2, y: 2, z: 4, core: 2. Of those that a mesh axis runs over, the one named last changes fastest.
Arguments:
- inputs: bfloat16 [4096, 4096], P('ctx'), may hold values from -8 to 8
- query_weight: bfloat16 [4096, 2048], P(None, 'head'), may hold values from -0.09375 to 0.09375
- key_weight: bfloat16 [4096, 512], P(None, 'head'), may hold values from -0.09375 to 0.09375
- value_weight: bfloat16 [4096, 512], P(None, 'head'), may hold values from -0.09375 to 0.09375
- out_grad: bfloat16 [4096, 2048], P('ctx', 'head'), may hold values from -6 to 6
- doc_lengths: int32 [8], replicated, may hold values from 128 to 1536, as said below
Outputs:
- attn_out: bfloat16 [4096, 2048], P('ctx', 'head')
- input_grad: bfloat16 [4096, 4096], P('ctx', 'head')
- query_weight_grad: float32 [4096, 2048], P('ctx', 'head')
- key_weight_grad: float32 [4096, 512], P('ctx', 'head')
- value_weight_grad: float32 [4096, 512], P('ctx', 'head')
The draws below stay inside these ranges and needn't reach their ends.
Inputs may be any that keep to these rules, and one draw needn't show every extreme that they name: `doc_lengths`: each length is a positive multiple of 128; the lengths sum to 4096; the largest is exactly 1536.
All inputs are finite; a program needn't handle non-finite values.
Results may differ from the reference program's by a relative error of at most 0.018.
The reference program's roundings to bfloat16 on the way count: a program that leaves them out, or rounds other values in their place, can miss the bound.
Values may be sent and summed in bfloat16 or wider, within the bound.
No kernel may reach another device: no remote copies, remote signals or barrier semaphores. Data moves between devices by JAX's collectives and lax.ppermute only.
A program may use at most 128 MiB of HBM per device.

```python
import jax
import jax.numpy as jnp
from jax import lax

D = 4096
HD = 128
GROUP = 4
KV_DEV = 1
TOK_DEV = 512
GRAIN = 128
SPAN = 3
KVH = 4
HEADS = 16
TOKENS = 4096
MAXDOC = 1536
NDOCS = 8
N_CTX = 8
N_HEAD = 4


def draw_inputs(key, part):
    base_key, scale_key = jax.random.split(jax.random.fold_in(key, 11))
    base = jax.random.truncated_normal(base_key, -4.0, 4.0, (TOKENS, D), jnp.float32)
    row_scale = jnp.exp(jax.random.uniform(scale_key, (TOKENS, 1), jnp.float32, jnp.log(0.5), jnp.log(2.0)))
    return (base * row_scale).astype(jnp.bfloat16)


def draw_doc_lengths(key, part):
    grain_total = TOKENS // GRAIN
    most_grains = MAXDOC // GRAIN
    other_docs = NDOCS - 1
    extra_grains = grain_total - most_grains - other_docs
    pick_key, place_key, order_key = jax.random.split(jax.random.fold_in(key, 23), 3)
    picks_one = jax.random.randint(jax.random.fold_in(pick_key, 1), (extra_grains,), 0, other_docs)
    picks_two = jax.random.randint(jax.random.fold_in(pick_key, 2), (extra_grains,), 0, other_docs)
    picks = jnp.minimum(picks_one, picks_two).astype(jnp.int32)

    def add_one(step_idx, counts):
        target = picks[step_idx]
        has_room = counts < most_grains - 1
        fallback = jnp.argmax(has_room.astype(jnp.int32)).astype(jnp.int32)
        chosen = jnp.where(has_room[target], target, fallback)
        return counts.at[chosen].add(1)
    counts = lax.fori_loop(0, extra_grains, add_one, jnp.zeros((other_docs,), jnp.int32))
    counts = jax.random.permutation(order_key, counts + 1)
    spot = jax.random.randint(place_key, (), 0, NDOCS).astype(jnp.int32)
    index_all = jnp.arange(NDOCS, dtype=jnp.int32)
    before = counts[jnp.clip(index_all, 0, other_docs - 1)]
    after = counts[jnp.clip(index_all - 1, 0, other_docs - 1)]
    grains = jnp.where(index_all < spot, before, jnp.where(index_all == spot, most_grains, after))
    return (grains * GRAIN).astype(jnp.int32)


def block_scale(stream_key, shape, pieces, smallest, high):
    factor_of = 1.0
    for position, blocks in pieces:
        heights = jax.random.uniform(jax.random.fold_in(jax.random.fold_in(stream_key, 6), position), (blocks,), jnp.float32, smallest / len(pieces), high / len(pieces))
        factor_of = factor_of * jnp.repeat(jnp.exp(heights), shape[position] // blocks).reshape((-1,) + (1,) * (len(shape) - 1 - position))
    return factor_of


def gaussian(stream_key, extent, scale, limit, cuts=(), kind=jnp.bfloat16):
    values = jax.random.normal(stream_key, extent, jnp.float32) * scale
    if len(cuts) > 0:
        values = block_scale(stream_key, extent, cuts, -0.22, 0.18) * values
    return jnp.clip(values, min=-limit, max=limit).astype(kind)


def setup_inputs(seed: int = 0) -> dict:
    seeds = jax.random.split(jax.random.key(seed), 7)
    return {
        "inputs": draw_inputs(jax.random.fold_in(seeds[6], 71), 0),
        "query_weight": gaussian(seeds[1], (D, HEADS * HD), D ** -0.5, 0.09375, ((1, 4),)),
        "key_weight": gaussian(seeds[2], (D, KVH * HD), D ** -0.5, 0.09375, ((1, 4),)),
        "value_weight": gaussian(seeds[3], (D, KVH * HD), D ** -0.5, 0.09375, ((1, 4),)),
        "out_grad": gaussian(seeds[4], (TOKENS, HEADS * HD), 1.0, 6.0, ((0, 8), (1, 4))),
        "doc_lengths": draw_doc_lengths(jax.random.fold_in(seeds[6], 71), 0),
    }


NEG = -1.0e30


def visible(query_pos, query_start, key_pos):
    return (key_pos[None, :] >= query_start[:, None]) & (key_pos[None, :] <= query_pos[:, None])


def block_scores(query_blk, key_blk):
    return jnp.einsum("qkgd,skd->kgqs", query_blk.astype(jnp.float32), key_blk.astype(jnp.float32)) * (HD ** -0.5)


def take_rows(array, start, count):
    return lax.dynamic_slice_in_dim(array, start, count, 0)


def keep_carry(carry, *others):
    return carry


def stats_live(carry, query_blk, key_blk, mask):
    run_top, run_total = carry
    score = jnp.where(mask, block_scores(query_blk, key_blk), NEG)
    new_top = jnp.maximum(run_top, jnp.max(score, axis=-1))
    weight = jnp.where(mask, jnp.exp(score - new_top[..., None]), 0.0)
    return new_top, run_total * jnp.exp(run_top - new_top) + jnp.sum(weight, axis=-1)


def output_live(accum, query_blk, key_blk, value_blk, mask, lse_blk):
    prob = jnp.where(mask, jnp.exp(block_scores(query_blk, key_blk) - lse_blk[..., None]), 0.0)
    prob_low = lax.optimization_barrier(prob.astype(jnp.bfloat16)).astype(jnp.float32)
    return accum + jnp.einsum("kgqs,skd->qkgd", prob_low, value_blk.astype(jnp.float32))


def grads_live(carry, query_blk, key_blk, value_blk, grad_blk, mask, lse_blk, delta_blk, key_at):
    query_acc, key_acc, value_acc = carry
    scale = HD ** -0.5
    prob = jnp.where(mask, jnp.exp(block_scores(query_blk, key_blk) - lse_blk[..., None]), 0.0)
    prob_low = lax.optimization_barrier(prob.astype(jnp.bfloat16)).astype(jnp.float32)
    grad_f = grad_blk.astype(jnp.float32)
    dprob = jnp.einsum("qkgd,skd->kgqs", grad_f, value_blk.astype(jnp.float32))
    dscore = lax.optimization_barrier((prob * (dprob - delta_blk[..., None])).astype(jnp.bfloat16)).astype(jnp.float32)
    query_acc = query_acc + scale * jnp.einsum("kgqs,skd->qkgd", dscore, key_blk.astype(jnp.float32))
    key_part = scale * jnp.einsum("kgqs,qkgd->skd", dscore, query_blk.astype(jnp.float32))
    value_part = jnp.einsum("kgqs,qkgd->skd", prob_low, grad_f)
    key_acc = lax.dynamic_update_slice_in_dim(key_acc, take_rows(key_acc, key_at, TOK_DEV) + key_part, key_at, 0)
    value_acc = lax.dynamic_update_slice_in_dim(value_acc, take_rows(value_acc, key_at, TOK_DEV) + value_part, key_at, 0)
    return query_acc, key_acc, value_acc


def dot_nt(left_mat, right_mat):
    return lax.dot_general(left_mat, right_mat, (((1,), (1,)), ((), ())), preferred_element_type=jnp.float32)


def reference(inputs, query_weight, key_weight, value_weight, out_grad, doc_lengths):
    n_tok = inputs.shape[0]
    kv_heads = KV_DEV * N_HEAD
    query = lax.optimization_barrier(jnp.dot(inputs, query_weight, preferred_element_type=jnp.float32).astype(jnp.bfloat16))
    keys_all = lax.optimization_barrier(jnp.dot(inputs, key_weight, preferred_element_type=jnp.float32).astype(jnp.bfloat16))
    values_all = lax.optimization_barrier(jnp.dot(inputs, value_weight, preferred_element_type=jnp.float32).astype(jnp.bfloat16))
    query4 = query.reshape(n_tok, kv_heads, GROUP, HD)
    keys3 = keys_all.reshape(n_tok, kv_heads, HD)
    values3 = values_all.reshape(n_tok, kv_heads, HD)
    positions = jnp.arange(n_tok, dtype=jnp.int32)
    doc_ends = jnp.cumsum(doc_lengths).astype(jnp.int32)
    starts = jnp.sum(jnp.where(doc_ends[None, :] <= positions[:, None], doc_lengths[None, :], 0), axis=1).astype(jnp.int32)
    local_pos = jnp.arange(TOK_DEV, dtype=jnp.int32)

    def forward_shard(shard):
        first = shard * TOK_DEV
        query_blk = take_rows(query4, first, TOK_DEV)
        query_pos = first + local_pos
        query_start = take_rows(starts, first, TOK_DEV)
        carry = (jnp.full((kv_heads, GROUP, TOK_DEV), NEG, jnp.float32), jnp.zeros((kv_heads, GROUP, TOK_DEV), jnp.float32))
        for distance in range(SPAN + 1):
            key_first = (shard - distance) * TOK_DEV
            mask = visible(query_pos, query_start, key_first + local_pos)
            key_blk = take_rows(keys3, jnp.maximum(key_first, 0), TOK_DEV)
            carry = lax.cond(jnp.any(mask), stats_live, keep_carry, carry, query_blk, key_blk, mask)
        lse_blk = carry[0] + jnp.log(carry[1])
        accum = jnp.zeros((TOK_DEV, kv_heads, GROUP, HD), jnp.float32)
        for distance in range(SPAN + 1):
            key_first = (shard - distance) * TOK_DEV
            mask = visible(query_pos, query_start, key_first + local_pos)
            key_at = jnp.maximum(key_first, 0)
            accum = lax.cond(jnp.any(mask), output_live, keep_carry, accum, query_blk,
                             take_rows(keys3, key_at, TOK_DEV), take_rows(values3, key_at, TOK_DEV), mask, lse_blk)
        return lax.optimization_barrier(accum.astype(jnp.bfloat16)), lse_blk

    outs, lse_all = lax.map(forward_shard, jnp.arange(N_CTX, dtype=jnp.int32))
    attn4 = outs.reshape(n_tok, kv_heads, GROUP, HD)
    attn_out = attn4.reshape(n_tok, kv_heads * GROUP * HD)
    grad4 = out_grad.reshape(n_tok, kv_heads, GROUP, HD)
    delta_all = jnp.sum(grad4.astype(jnp.float32) * attn4.astype(jnp.float32), axis=-1)

    def backward_shard(carry, shard):
        key_acc, value_acc = carry
        first = shard * TOK_DEV
        query_blk = take_rows(query4, first, TOK_DEV)
        grad_blk = take_rows(grad4, first, TOK_DEV)
        query_pos = first + local_pos
        query_start = take_rows(starts, first, TOK_DEV)
        lse_blk = lax.dynamic_index_in_dim(lse_all, shard, 0, keepdims=False)
        delta_blk = jnp.transpose(take_rows(delta_all, first, TOK_DEV), (1, 2, 0))
        state = (jnp.zeros((TOK_DEV, kv_heads, GROUP, HD), jnp.float32), key_acc, value_acc)
        for distance in range(SPAN + 1):
            key_first = (shard - distance) * TOK_DEV
            mask = visible(query_pos, query_start, key_first + local_pos)
            key_at = jnp.maximum(key_first, 0)
            state = lax.cond(jnp.any(mask), grads_live, keep_carry, state, query_blk,
                             take_rows(keys3, key_at, TOK_DEV), take_rows(values3, key_at, TOK_DEV),
                             grad_blk, mask, lse_blk, delta_blk, key_at)
        return (state[1], state[2]), state[0]

    zero_kv = jnp.zeros((n_tok, kv_heads, HD), jnp.float32)
    (key_acc, value_acc), query_grads = lax.scan(backward_shard, (zero_kv, zero_kv), jnp.arange(N_CTX, dtype=jnp.int32))
    dq_low = lax.optimization_barrier(query_grads.reshape(n_tok, kv_heads * GROUP * HD).astype(jnp.bfloat16))
    dk_low = lax.optimization_barrier(key_acc.reshape(n_tok, kv_heads * HD).astype(jnp.bfloat16))
    dv_low = lax.optimization_barrier(value_acc.reshape(n_tok, kv_heads * HD).astype(jnp.bfloat16))
    q_cols = GROUP * KV_DEV * HD
    k_cols = KV_DEV * HD
    total_grad = jnp.zeros((n_tok, inputs.shape[1]), jnp.float32)
    for group_idx in range(N_HEAD):
        qa, qb = group_idx * q_cols, (group_idx + 1) * q_cols
        ka, kb = group_idx * k_cols, (group_idx + 1) * k_cols
        piece = dot_nt(dq_low[:, qa:qb], query_weight[:, qa:qb]) + dot_nt(dk_low[:, ka:kb], key_weight[:, ka:kb]) + dot_nt(dv_low[:, ka:kb], value_weight[:, ka:kb])
        total_grad = total_grad + lax.optimization_barrier(piece.astype(jnp.bfloat16)).astype(jnp.float32)
    input_grad = total_grad.astype(jnp.bfloat16)
    joined = jnp.concatenate([dq_low, dk_low, dv_low], axis=1)
    weight_grad = lax.dot_general(inputs, joined, (((0,), (0,)), ((), ())), preferred_element_type=jnp.float32)
    all_q = kv_heads * GROUP * HD
    all_k = kv_heads * HD
    return (attn_out, input_grad, weight_grad[:, :all_q], weight_grad[:, all_q:all_q + all_k], weight_grad[:, all_q + all_k:])
```

```python
from functools import partial

import jax
import jax.numpy as jnp
from jax import lax
from jax.experimental import pallas as pl
from jax.experimental.pallas import tpu as pltpu
from jax.sharding import PartitionSpec as P

HD = 128
GROUP = 4
SPAN = 3
GRAIN = 128
TILE = 256

NEG = -1e30
LOG2E = 1.4426950408889634


def dot_nt(left_mat, right_mat):
    return lax.dot_general(
        left_mat, right_mat, (((1,), (1,)), ((), ())), preferred_element_type=jnp.float32
    )


def dot_tn(left_mat, right_mat):
    return lax.dot_general(
        left_mat, right_mat, (((0,), (0,)), ((), ())), preferred_element_type=jnp.float32
    )


def dot_nn(left_mat, right_mat):
    return jnp.dot(left_mat, right_mat, preferred_element_type=jnp.float32)


def attention_kernel(
    first_ref, query_ref, grad_ref, kv0, kv1, kv2, kv3,
    out_ref, dq_ref, d0, d1, d2, d3,
    kv_ref, acc_ref, score_ref,
):
    rows = query_ref.shape[0]
    for slot, block in enumerate((kv3, kv2, kv1, kv0)):
        kv_ref[pl.ds(slot * rows, rows), :] = block[...]
    acc_ref[...] = jnp.zeros_like(acc_ref)
    factor = HD ** (-0.5)
    wide = GROUP * GRAIN
    for granule in range(rows // GRAIN):
        here = pl.ds(granule * GRAIN, GRAIN)
        heads = [slice(h * HD, (h + 1) * HD) for h in range(GROUP)]
        query = jnp.concatenate([query_ref[here, cols] for cols in heads], axis=0)
        grad = jnp.concatenate([grad_ref[here, cols] for cols in heads], axis=0)
        own = SPAN * rows + granule * GRAIN
        last = own // TILE
        first_key = first_ref[granule]
        low = first_key // TILE

        def tile_rows(tile):
            return pl.ds(pl.multiple_of(tile * TILE, TILE), TILE)

        def score_tile(tile, top, diagonal):
            score = dot_nt(kv_ref[tile_rows(tile), :HD], query) * (factor * LOG2E)
            key_pos = tile * TILE + lax.broadcasted_iota(jnp.int32, (TILE, wide), 0)
            keep = key_pos >= first_key
            if diagonal:
                query_pos = own + lax.broadcasted_iota(jnp.int32, (TILE, wide), 1) % GRAIN
                keep = keep & (key_pos <= query_pos)
            score = jnp.where(keep, score, NEG)
            score_ref[tile_rows(tile), :] = score
            return jnp.maximum(top, jnp.max(score.reshape(TILE // 8, 8, wide), axis=0))

        top = lax.fori_loop(
            low, last, lambda tile, top: score_tile(tile, top, False),
            jnp.full((8, wide), NEG, jnp.float32),
        )
        top = score_tile(last, top, True)
        top = jnp.max(top, axis=0, keepdims=True)

        def weight_tile(tile, total):
            weight = jnp.exp2(score_ref[tile_rows(tile), :] - top)
            score_ref[tile_rows(tile), :] = weight
            return total + jnp.sum(weight.reshape(TILE // 8, 8, wide), axis=0)

        total = lax.fori_loop(low, last + 1, weight_tile, jnp.zeros((8, wide), jnp.float32))
        inverse = 1.0 / jnp.sum(total, axis=0, keepdims=True)

        def output_tile(tile, accum):
            prob = (score_ref[tile_rows(tile), :] * inverse).astype(jnp.bfloat16)
            acc_ref[tile_rows(tile), HD:] += dot_nn(prob, grad)
            return accum + dot_tn(kv_ref[tile_rows(tile), HD:], prob)

        accum = lax.fori_loop(low, last + 1, output_tile, jnp.zeros((HD, wide), jnp.float32))
        out = accum.T.astype(jnp.bfloat16)
        delta = jnp.sum(
            (out.astype(jnp.float32) * grad.astype(jnp.float32)).T, axis=0, keepdims=True
        )

        def grad_tile(tile, accum):
            prob = score_ref[tile_rows(tile), :] * inverse
            dprob = dot_nt(kv_ref[tile_rows(tile), HD:], grad)
            dscore = (prob * (dprob - delta)).astype(jnp.bfloat16)
            acc_ref[tile_rows(tile), :HD] += dot_nn(dscore, query)
            return accum + dot_tn(kv_ref[tile_rows(tile), :HD], dscore)

        accum = lax.fori_loop(low, last + 1, grad_tile, jnp.zeros((HD, wide), jnp.float32))
        dquery = (accum * factor).T.astype(jnp.bfloat16)
        for head, cols in enumerate(heads):
            part = slice(head * GRAIN, (head + 1) * GRAIN)
            out_ref[here, cols] = out[part]
            dq_ref[here, cols] = dquery[part]
    for slot, block in enumerate((d3, d2, d1, d0)):
        place = pl.ds(slot * rows, rows)
        block[:, :HD] = acc_ref[place, :HD] * factor
        block[:, HD:] = acc_ref[place, HD:]


def attention(first, query, grad, kv_list):
    rows, cols = query.shape
    window = (SPAN + 1) * rows
    low = jax.ShapeDtypeStruct((rows, cols), jnp.bfloat16)
    high = jax.ShapeDtypeStruct((rows, 2 * HD), jnp.float32)
    vmem = pl.BlockSpec(memory_space=pltpu.VMEM)
    return pl.pallas_call(
        attention_kernel,
        out_shape=(low, low) + (high,) * (SPAN + 1),
        in_specs=[pl.BlockSpec(memory_space=pltpu.SMEM)] + [vmem] * (SPAN + 3),
        out_specs=(vmem,) * (SPAN + 3),
        scratch_shapes=[
            pltpu.VMEM((window, 2 * HD), jnp.bfloat16),
            pltpu.VMEM((window, 2 * HD), jnp.float32),
            pltpu.VMEM((window, GROUP * GRAIN), jnp.float32),
        ],
        compiler_params=pltpu.CompilerParams(vmem_limit_bytes=32 * 1024 * 1024),
        cost_estimate=pl.CostEstimate(
            flops=6 * 2 * rows * window * cols, bytes_accessed=6 * 2**20, transcendentals=0
        ),
        name="attention",
    )(first, query, grad, *kv_list)


def shift(value, axis, steps):
    count = lax.axis_size(axis)
    pairs = [(i, i + steps) for i in range(count) if 0 <= i + steps < count]
    return lax.ppermute(value, axis, pairs)


def swap(value, axis, mask):
    return lax.ppermute(value, axis, [(i, i ^ mask) for i in range(lax.axis_size(axis))])


def rotate(value, axis, steps):
    count = lax.axis_size(axis)
    return lax.ppermute(value, axis, [(i, (i + steps) % count) for i in range(count)])


def body(inputs, query_weight, key_weight, value_weight, out_grad, doc_lengths):
    tok_rows, width = inputs.shape
    n_ctx = lax.axis_size("ctx")
    n_head = lax.axis_size("head")
    chips = n_ctx // 2
    ctx = lax.axis_index("ctx")
    head = lax.axis_index("head")
    q_cols = query_weight.shape[1]
    k_cols = key_weight.shape[1]
    weights = (query_weight, key_weight, value_weight)

    kv_loc = jnp.concatenate(
        [dot_nn(inputs, key_weight).astype(jnp.bfloat16), dot_nn(inputs, value_weight).astype(jnp.bfloat16)],
        axis=1,
    )
    kv_list = [kv_loc] + [shift(kv_loc, "ctx", distance) for distance in range(1, SPAN + 1)]
    query = dot_nn(inputs, query_weight).astype(jnp.bfloat16)

    out_width = width // n_head
    piece = out_width // n_ctx
    weight_rows = []
    for step in range(n_head):
        if step == 0:
            start = head * out_width
            rows = [lax.dynamic_slice_in_dim(w, start, out_width, 0) for w in weights]
            weight_rows.append(jnp.concatenate(rows, axis=1))
            continue
        start = (head + step) % n_head * out_width + ctx * piece
        rows = [lax.dynamic_slice_in_dim(w, start, piece, 0) for w in weights]
        moved = rotate(jnp.concatenate(rows, axis=1), "head", step)
        weight_rows.append(lax.all_gather(moved, "ctx", axis=0, tiled=True))

    split = inputs.reshape(tok_rows, chips, 2, width // n_ctx)
    core = ctx % 2
    own_part = lax.dynamic_index_in_dim(split, core, 2, keepdims=False)
    other_part = lax.dynamic_index_in_dim(split, 1 - core, 2, keepdims=False)
    pair_inputs = jnp.concatenate([own_part, swap(other_part, "ctx", 1)], axis=0)

    granules = tok_rows // GRAIN
    window_start = (ctx - SPAN) * tok_rows
    positions = ctx * tok_rows + GRAIN * jnp.arange(granules, dtype=jnp.int32)
    doc_ends = jnp.cumsum(doc_lengths)
    starts = jnp.sum(
        jnp.where(doc_ends[None, :] <= positions[:, None], doc_lengths[None, :], 0), axis=1
    )
    attn_out, dq_low, *kv_grads = attention(starts - window_start, query, out_grad, kv_list)

    kv_total = kv_grads[0]
    for distance in range(1, SPAN + 1):
        kv_total = kv_total + shift(kv_grads[distance], "ctx", -distance)
    dkv_low = kv_total.astype(jnp.bfloat16)

    grad_sum = jnp.zeros((tok_rows, out_width), jnp.float32)
    moving = (dq_low, dkv_low)
    for step in range(n_head):
        if step > 0:
            moving = tuple(rotate(part, "head", 1) for part in moving)
        rows = weight_rows[step]
        term = dot_nt(moving[0], rows[:, :q_cols]) + dot_nt(moving[1], rows[:, q_cols:])
        grad_sum = grad_sum + term.astype(jnp.bfloat16).astype(jnp.float32)
    input_grad = grad_sum.astype(jnp.bfloat16)

    sums = []
    for low in (dq_low, dkv_low):
        pair = jnp.concatenate([low, swap(low, "ctx", 1)], axis=0)
        total = None
        for chip in range(chips):
            block = lax.dynamic_index_in_dim(pair_inputs, (ctx // 2) ^ chip, 1, keepdims=False)
            term = dot_tn(block, pair)
            if chip > 0:
                term = swap(term.astype(jnp.bfloat16), "ctx", 2 * chip).astype(jnp.float32)
            total = term if total is None else total + term
        sums.append(total)
    return (attn_out, input_grad, sums[0], sums[1][:, :k_cols], sums[1][:, k_cols:])


def solution(mesh):
    return jax.shard_map(
        body,
        mesh=mesh,
        in_specs=(
            P("ctx", None),
            P(None, "head"),
            P(None, "head"),
            P(None, "head"),
            P("ctx", "head"),
            P(),
        ),
        out_specs=(P("ctx", "head"),) * 5,
        check_vma=False,
    )
```

```python
from functools import partial

import jax
import jax.numpy as jnp
from jax import lax
from jax.experimental import pallas as pl
from jax.experimental.pallas import tpu as pltpu
from jax.sharding import PartitionSpec as P

HD = 128
GROUP = 4
SPAN = 3
GRAIN = 128
TILE = 256
CHUNK = 512
MIB = 2**20

NEG = -1e30
LOG2E = 1.4426950408889634


def dot_nt(left_mat, right_mat):
    return lax.dot_general(
        left_mat, right_mat, (((1,), (1,)), ((), ())), preferred_element_type=jnp.float32
    )


def dot_tn(left_mat, right_mat):
    return lax.dot_general(
        left_mat, right_mat, (((0,), (0,)), ((), ())), preferred_element_type=jnp.float32
    )


def dot_nn(left_mat, right_mat):
    return jnp.dot(left_mat, right_mat, preferred_element_type=jnp.float32)


def in_hbm(*arrays):
    return [pltpu.with_memory_space_constraint(array, pltpu.HBM) for array in arrays]


def project_kernel(place_ref, x_ref, wq_ref, wk_ref, wv_ref, q_ref, kv_ref, *refs):
    piece_refs, acc_ref = refs[:-1], refs[-1]
    step = pl.program_id(0)
    at = 0
    for weight_ref in (wq_ref, wk_ref, wv_ref):
        cols = slice(at, at + weight_ref.shape[1])
        at = cols.stop
        term = dot_nn(x_ref[...], weight_ref[...])

        @pl.when(step == 0)
        def _():
            acc_ref[:, cols] = term

        @pl.when(step > 0)
        def _():
            acc_ref[:, cols] += term

    n_head = len(piece_refs) + 1
    per_head = pl.num_programs(0) // n_head
    piece = piece_refs[0].shape[0]
    chunk = x_ref.shape[1]
    group = step // per_head
    first = place_ref[1] - step % per_head * chunk
    here = (first >= 0) & (first < chunk)
    for distance, piece_ref in enumerate(piece_refs, 1):

        @pl.when(here & (group == (place_ref[0] + distance) % n_head))
        def _():
            rows = pl.ds(pl.multiple_of(first, piece), piece)
            at = 0
            for weight_ref in (wq_ref, wk_ref, wv_ref):
                cols = slice(at, at + weight_ref.shape[1])
                at = cols.stop
                piece_ref[:, cols] = weight_ref[rows, :]

    @pl.when(step == pl.num_programs(0) - 1)
    def _():
        q_cols = q_ref.shape[1]
        q_ref[...] = acc_ref[:, :q_cols].astype(q_ref.dtype)
        kv_ref[...] = acc_ref[:, q_cols:].astype(kv_ref.dtype)


def project(place, inputs, weights, n_head, piece):
    rows, width = inputs.shape
    widths = [weight.shape[1] for weight in weights]
    cols = sum(widths)

    def fixed(shape):
        return pl.BlockSpec(shape, lambda i, place: (0, 0))

    shapes = [(rows, widths[0]), (rows, cols - widths[0])] + [(piece, cols)] * (n_head - 1)
    return pl.pallas_call(
        project_kernel,
        grid_spec=pltpu.PrefetchScalarGridSpec(
            num_scalar_prefetch=1,
            grid=(width // CHUNK,),
            in_specs=[pl.BlockSpec((rows, CHUNK), lambda i, place: (0, i))]
            + [pl.BlockSpec((CHUNK, cols), lambda i, place: (i, 0)) for cols in widths],
            out_specs=tuple(fixed(shape) for shape in shapes),
            scratch_shapes=[pltpu.VMEM((rows, cols), jnp.float32)],
        ),
        out_shape=tuple(jax.ShapeDtypeStruct(shape, jnp.bfloat16) for shape in shapes),
        compiler_params=pltpu.CompilerParams(vmem_limit_bytes=32 * MIB),
        cost_estimate=pl.CostEstimate(
            flops=2 * rows * width * cols, bytes_accessed=2 * width * (rows + cols), transcendentals=0
        ),
        name="project",
    )(place, *in_hbm(inputs, *weights))


def combine_kernel(own_ref, *refs):
    back_refs, (dq_ref, dq_t_ref, low_ref, joined_ref, turned_ref) = refs[:-5], refs[-5:]
    total = own_ref[...]
    for back_ref in back_refs:
        total = total + back_ref[...].astype(jnp.float32)
    low = total.astype(jnp.bfloat16)
    q_cols = dq_ref.shape[1]
    low_ref[...] = low
    joined_ref[:, :q_cols] = dq_ref[...]
    joined_ref[:, q_cols:] = low
    turned_ref[:q_cols, :] = dq_t_ref[...]
    turned_ref[q_cols:, :] = total.T.astype(jnp.bfloat16)


def combine(own, back, dq, dq_turned):
    rows, cols = own.shape
    wide = dq.shape[1] + cols
    vmem = pl.BlockSpec(memory_space=pltpu.VMEM)
    shapes = ((rows, cols), (rows, wide), (wide, rows))
    return pl.pallas_call(
        combine_kernel,
        out_shape=tuple(jax.ShapeDtypeStruct(shape, jnp.bfloat16) for shape in shapes),
        in_specs=[vmem] * (len(back) + 3),
        out_specs=(vmem,) * 3,
        compiler_params=pltpu.CompilerParams(vmem_limit_bytes=16 * MIB),
        cost_estimate=pl.CostEstimate(flops=rows * cols * 4, bytes_accessed=4 * MIB, transcendentals=0),
        name="combine",
    )(own, *back, dq, dq_turned)


def terms_kernel(index_ref, joined_ref, other_joined_ref, x_ref, other_x_ref, *out_refs):
    step = pl.program_id(0)
    term = dot_nn(joined_ref[...], x_ref[...]) + dot_nn(other_joined_ref[...], other_x_ref[...])
    for chip, out_ref in enumerate(out_refs):

        @pl.when(step == chip)
        def _():
            out_ref[...] = term.astype(out_ref.dtype)


def weight_terms(index, joined, other_joined, inputs, other_inputs, n_ctx):
    cols, rows = joined.shape
    kept = inputs.shape[1] // n_ctx
    chips = n_ctx // 2
    whole = pl.BlockSpec((cols, rows), lambda i, index: (0, 0))
    part = pl.BlockSpec((rows, kept), lambda i, index: (0, index[i]))
    return pl.pallas_call(
        terms_kernel,
        grid_spec=pltpu.PrefetchScalarGridSpec(
            num_scalar_prefetch=1,
            grid=(chips,),
            in_specs=[whole, whole, part, part],
            out_specs=(pl.BlockSpec((cols, kept), lambda i, index: (0, 0)),) * chips,
        ),
        out_shape=tuple(
            jax.ShapeDtypeStruct((cols, kept), jnp.float32 if chip == 0 else jnp.bfloat16)
            for chip in range(chips)
        ),
        compiler_params=pltpu.CompilerParams(vmem_limit_bytes=32 * MIB),
        cost_estimate=pl.CostEstimate(
            flops=4 * cols * rows * kept * chips, bytes_accessed=10 * MIB, transcendentals=0
        ),
        name="weight_terms",
    )(index, joined, other_joined, inputs, other_inputs)


def rows_kernel(*refs):
    in_refs, out_refs = refs[:-3], refs[-3:]
    total = in_refs[0][...]
    for in_ref in in_refs[1:]:
        total = total + in_ref[...].astype(jnp.float32)
    at = 0
    for out_ref in out_refs:
        cols = slice(at, at + out_ref.shape[1])
        at = cols.stop
        out_ref[...] = total[cols, :].T


def weight_rows(terms, widths):
    kept = terms[0].shape[1]
    vmem = pl.BlockSpec(memory_space=pltpu.VMEM)
    return pl.pallas_call(
        rows_kernel,
        out_shape=tuple(jax.ShapeDtypeStruct((kept, width), jnp.float32) for width in widths),
        in_specs=[vmem] * len(terms),
        out_specs=(vmem,) * 3,
        compiler_params=pltpu.CompilerParams(vmem_limit_bytes=32 * MIB),
        cost_estimate=pl.CostEstimate(flops=4 * MIB, bytes_accessed=6 * MIB, transcendentals=0),
        name="weight_rows",
    )(*terms)


def products_kernel(firsts, has_base, *refs):
    refs = refs[1:]
    out_ref = refs[-1]
    n_terms = len(firsts)
    total = refs[2 * n_terms][...] if has_base else None
    for at, first in enumerate(firsts):
        rows = refs[n_terms + at][...]
        rows = rows.reshape(-1, rows.shape[-1])
        term = dot_nt(refs[at][:, first : first + rows.shape[1]], rows)
        total = term if total is None else total + term
    out_ref[...] = total.astype(out_ref.dtype)


def products(lefts, rights, base, out_width, head, dtype, name):
    rows = lefts[0].shape[0]
    block = 256
    n_blocks = out_width // block
    left_specs = [pl.BlockSpec(left.shape, lambda i, head: (0, 0)) for left in lefts]
    right_specs = []
    firsts = []
    flops = 0
    for left, (array, *place) in zip(lefts, rights):
        cols = array.shape[1] if len(place) == 1 else place[2]
        flops += 2 * rows * cols * out_width
        if len(place) == 1:
            firsts.append(place[0])
            right_specs.append(
                pl.BlockSpec((block, cols), lambda i, head: (head[0] * n_blocks + i, 0))
            )
        else:
            step, first, cols = place
            piece = array.shape[2]
            firsts.append(0)
            right_specs.append(
                pl.BlockSpec(
                    (block // piece, 1, piece, cols),
                    partial(lambda step, at, i, head: (i, step, 0, at), step, first // cols),
                )
            )
    out_spec = pl.BlockSpec((rows, block), lambda i, head: (0, i))
    extra = [] if base is None else [base]
    return pl.pallas_call(
        partial(products_kernel, tuple(firsts), base is not None),
        grid_spec=pltpu.PrefetchScalarGridSpec(
            num_scalar_prefetch=1,
            grid=(n_blocks,),
            in_specs=left_specs + right_specs + [out_spec] * len(extra),
            out_specs=out_spec,
        ),
        out_shape=jax.ShapeDtypeStruct((rows, out_width), dtype),
        compiler_params=pltpu.CompilerParams(vmem_limit_bytes=32 * MIB),
        cost_estimate=pl.CostEstimate(flops=flops, bytes_accessed=8 * MIB, transcendentals=0),
        name=name,
    )(head, *lefts, *in_hbm(*[array for array, *place in rights]), *extra)


def attention_kernel(
    first_ref, query_ref, grad_ref, kv0, kv1, kv2, kv3,
    out_ref, dq_ref, dq_t_ref, d0, d1, d2, d3,
    kv_ref, acc_ref, score_ref, sems,
):
    rows = query_ref.shape[0]
    copies = [
        pltpu.make_async_copy(block, kv_ref.at[pl.ds(slot * rows, rows), :], sems.at[slot])
        for slot, block in enumerate((kv3, kv2, kv1, kv0))
    ]
    for copy in copies:
        copy.start()
    acc_ref[...] = jnp.zeros_like(acc_ref)
    for copy in copies:
        copy.wait()
    factor = HD ** (-0.5)
    wide = GROUP * GRAIN
    for granule in range(rows // GRAIN):
        here = pl.ds(granule * GRAIN, GRAIN)
        heads = [slice(h * HD, (h + 1) * HD) for h in range(GROUP)]
        query = jnp.concatenate([query_ref[here, cols] for cols in heads], axis=0)
        grad = jnp.concatenate([grad_ref[here, cols] for cols in heads], axis=0)
        own = SPAN * rows + granule * GRAIN
        last = own // TILE
        first_key = first_ref[granule]
        low = first_key // TILE

        def tile_rows(tile):
            return pl.ds(pl.multiple_of(tile * TILE, TILE), TILE)

        def score_tile(tile, top, diagonal):
            score = dot_nt(kv_ref[tile_rows(tile), :HD], query) * (factor * LOG2E)
            key_pos = tile * TILE + lax.broadcasted_iota(jnp.int32, (TILE, wide), 0)
            keep = key_pos >= first_key
            if diagonal:
                query_pos = own + lax.broadcasted_iota(jnp.int32, (TILE, wide), 1) % GRAIN
                keep = keep & (key_pos <= query_pos)
            score = jnp.where(keep, score, NEG)
            score_ref[tile_rows(tile), :] = score
            return jnp.maximum(top, jnp.max(score.reshape(TILE // 8, 8, wide), axis=0))

        top = lax.fori_loop(
            low, last, lambda tile, top: score_tile(tile, top, False),
            jnp.full((8, wide), NEG, jnp.float32),
        )
        top = score_tile(last, top, True)
        top = jnp.max(top, axis=0, keepdims=True)

        def weight_tile(tile, total):
            weight = jnp.exp2(score_ref[tile_rows(tile), :] - top)
            score_ref[tile_rows(tile), :] = weight
            return total + jnp.sum(weight.reshape(TILE // 8, 8, wide), axis=0)

        total = lax.fori_loop(low, last + 1, weight_tile, jnp.zeros((8, wide), jnp.float32))
        inverse = 1.0 / jnp.sum(total, axis=0, keepdims=True)

        def output_tile(tile, accum):
            prob = (score_ref[tile_rows(tile), :] * inverse).astype(jnp.bfloat16)
            acc_ref[tile_rows(tile), HD:] += dot_nn(prob, grad)
            return accum + dot_tn(kv_ref[tile_rows(tile), HD:], prob)

        accum = lax.fori_loop(low, last + 1, output_tile, jnp.zeros((HD, wide), jnp.float32))
        out = accum.T.astype(jnp.bfloat16)
        delta = jnp.sum(
            (out.astype(jnp.float32) * grad.astype(jnp.float32)).T, axis=0, keepdims=True
        )

        def grad_tile(tile, accum):
            prob = score_ref[tile_rows(tile), :] * inverse
            dprob = dot_nt(kv_ref[tile_rows(tile), HD:], grad)
            dscore = (prob * (dprob - delta)).astype(jnp.bfloat16)
            acc_ref[tile_rows(tile), :HD] += dot_nn(dscore, query)
            return accum + dot_tn(kv_ref[tile_rows(tile), :HD], dscore)

        accum = lax.fori_loop(low, last + 1, grad_tile, jnp.zeros((HD, wide), jnp.float32))
        accum = accum * factor
        dquery = accum.T.astype(jnp.bfloat16)
        for head, cols in enumerate(heads):
            part = slice(head * GRAIN, (head + 1) * GRAIN)
            out_ref[here, cols] = out[part]
            dq_ref[here, cols] = dquery[part]
            dq_t_ref[cols, here] = accum[:, part].astype(jnp.bfloat16)
    for slot, block in enumerate((d3, d2, d1, d0)):
        place = pl.ds(slot * rows, rows)
        block[:, :HD] = (acc_ref[place, :HD] * factor).astype(block.dtype)
        block[:, HD:] = acc_ref[place, HD:].astype(block.dtype)


def attention(first, query, grad, kv_list):
    rows, cols = query.shape
    window = (SPAN + 1) * rows
    low = jax.ShapeDtypeStruct((rows, cols), jnp.bfloat16)
    turned = jax.ShapeDtypeStruct((cols, rows), jnp.bfloat16)
    own = jax.ShapeDtypeStruct((rows, 2 * HD), jnp.float32)
    sent = jax.ShapeDtypeStruct((rows, 2 * HD), jnp.bfloat16)
    vmem = pl.BlockSpec(memory_space=pltpu.VMEM)
    anywhere = pl.BlockSpec(memory_space=pl.ANY)
    return pl.pallas_call(
        attention_kernel,
        out_shape=(low, low, turned, own) + (sent,) * SPAN,
        in_specs=[pl.BlockSpec(memory_space=pltpu.SMEM), vmem, vmem] + [anywhere] * (SPAN + 1),
        out_specs=(vmem,) * (SPAN + 4),
        scratch_shapes=[
            pltpu.VMEM((window, 2 * HD), jnp.bfloat16),
            pltpu.VMEM((window, 2 * HD), jnp.float32),
            pltpu.VMEM((window, GROUP * GRAIN), jnp.float32),
            pltpu.SemaphoreType.DMA((SPAN + 1,)),
        ],
        compiler_params=pltpu.CompilerParams(vmem_limit_bytes=32 * MIB),
        cost_estimate=pl.CostEstimate(
            flops=6 * 2 * rows * window * cols, bytes_accessed=6 * MIB, transcendentals=0
        ),
        name="attention",
    )(first, query, grad, *kv_list)


def shift(value, axis, steps):
    count = lax.axis_size(axis)
    pairs = [(i, i + steps) for i in range(count) if 0 <= i + steps < count]
    return lax.ppermute(value, axis, pairs)


def swap(value, axis, mask):
    return lax.ppermute(value, axis, [(i, i ^ mask) for i in range(lax.axis_size(axis))])


def rotate(value, axis, steps):
    count = lax.axis_size(axis)
    return lax.ppermute(value, axis, [(i, (i + steps) % count) for i in range(count)])


def body(inputs, query_weight, key_weight, value_weight, out_grad, doc_lengths):
    tok_rows, width = inputs.shape
    n_ctx = lax.axis_size("ctx")
    n_head = lax.axis_size("head")
    chips = n_ctx // 2
    ctx = lax.axis_index("ctx")
    head = lax.axis_index("head")
    q_cols = query_weight.shape[1]
    k_cols = key_weight.shape[1]

    weights = (query_weight, key_weight, value_weight)
    out_width = width // n_head
    piece = out_width // n_ctx
    place = jnp.stack([head, ctx * piece]).astype(jnp.int32)
    query, kv_loc, *pieces = project(place, inputs, weights, n_head, piece)

    kv_list = [kv_loc] + [shift(kv_loc, "ctx", distance) for distance in range(1, SPAN + 1)]
    pieces = [rotate(rows, "head", step) for step, rows in enumerate(pieces, 1)]
    query, kv_list, pieces, inputs = lax.optimization_barrier((query, kv_list, pieces, inputs))
    gathered = lax.all_gather(jnp.concatenate(pieces, axis=0), "ctx", axis=0, tiled=True)
    gathered = gathered.reshape(n_ctx, n_head - 1, piece, q_cols + 2 * k_cols)

    other_inputs = swap(inputs, "ctx", 1)

    granules = tok_rows // GRAIN
    window_start = (ctx - SPAN) * tok_rows
    positions = ctx * tok_rows + GRAIN * jnp.arange(granules, dtype=jnp.int32)
    doc_ends = jnp.cumsum(doc_lengths)
    starts = jnp.sum(
        jnp.where(doc_ends[None, :] <= positions[:, None], doc_lengths[None, :], 0), axis=1
    )
    attn_out, dq_low, dq_turned, own_grads, *sent_grads = attention(
        starts - window_start, query, out_grad, kv_list
    )

    dq_up = rotate(dq_low, "head", 1)
    back = [shift(sent_grads[distance - 1], "ctx", -distance) for distance in range(1, SPAN + 1)]
    back, dq_up, dq_low, dq_turned = lax.optimization_barrier((back, dq_up, dq_low, dq_turned))
    dkv_low, joined, turned = combine(own_grads, back, dq_low, dq_turned)
    joined_down = rotate(joined, "head", -1)
    dkv_up = rotate(dkv_low, "head", 1)

    other_turned = swap(turned, "ctx", 1)
    index = ((ctx // 2) ^ jnp.arange(chips, dtype=jnp.int32)) * 2 + ctx % 2
    terms = weight_terms(index, turned, other_turned, inputs, other_inputs, n_ctx)
    moved = [swap(term, "ctx", 2 * chip) for chip, term in enumerate(terms) if chip > 0]
    dq_far = rotate(dq_up, "head", 1)
    dkv_far = rotate(dkv_up, "head", 1)

    head_index = jnp.reshape(head, (1,)).astype(jnp.int32)
    q_place, kv_place, place = (0, q_cols), (q_cols, 2 * k_cols), (0, q_cols + 2 * k_cols)
    dq_up, dkv_up, joined_down, terms = lax.optimization_barrier((dq_up, dkv_up, joined_down, terms))
    grad_sum = products(
        (joined, joined, joined, dq_up, dkv_up, joined_down),
        (
            (query_weight, 0), (key_weight, q_cols), (value_weight, q_cols + k_cols),
            (gathered, 0, *q_place), (gathered, 0, *kv_place), (gathered, 2, *place),
        ),
        None, out_width, head_index, jnp.float32, "products_near",
    )
    input_grad = products(
        (dq_far, dkv_far), ((gathered, 1, *q_place), (gathered, 1, *kv_place)),
        grad_sum, out_width, head_index, jnp.bfloat16, "products_far",
    )
    weight_grads = weight_rows([terms[0], *moved], (q_cols, k_cols, k_cols))
    return (attn_out, input_grad, *weight_grads)


def solution(mesh):
    return jax.shard_map(
        body,
        mesh=mesh,
        in_specs=(
            P("ctx", None),
            P(None, "head"),
            P(None, "head"),
            P(None, "head"),
            P("ctx", "head"),
            P(),
        ),
        out_specs=(P("ctx", "head"),) * 5,
        check_vma=False,
    )
```

```python
from functools import partial

import jax
import jax.numpy as jnp
from jax import lax
from jax.experimental import pallas as pl
from jax.experimental.pallas import tpu as pltpu
from jax.sharding import PartitionSpec as P

HD = 128
GROUP = 4
SPAN = 3
GRAIN = 128
TILE = 256
CHUNK = 1024
MIB = 2**20

NEG = -1e30
LOG2E = 1.4426950408889634


def dot_nt(left_mat, right_mat):
    return lax.dot_general(
        left_mat, right_mat, (((1,), (1,)), ((), ())), preferred_element_type=jnp.float32
    )


def dot_tn(left_mat, right_mat):
    return lax.dot_general(
        left_mat, right_mat, (((0,), (0,)), ((), ())), preferred_element_type=jnp.float32
    )


def dot_nn(left_mat, right_mat):
    return jnp.dot(left_mat, right_mat, preferred_element_type=jnp.float32)


def in_hbm(*arrays):
    return [pltpu.with_memory_space_constraint(array, pltpu.HBM) for array in arrays]


def cut_kernel(*refs):
    weight_refs, piece_refs, sems = refs[:3], refs[3:-1], refs[-1]
    head, ctx = lax.axis_index("head"), lax.axis_index("ctx")
    n_head = len(piece_refs) + 1
    piece = piece_refs[0].shape[0]
    copies = []
    for distance, piece_ref in enumerate(piece_refs, 1):
        group = lax.rem(head + distance, n_head)
        first = group * (weight_refs[0].shape[0] // n_head) + ctx * piece
        at = 0
        for number, weight_ref in enumerate(weight_refs):
            cols = weight_ref.shape[1]
            copies.append(
                pltpu.make_async_copy(
                    weight_ref.at[pl.ds(pl.multiple_of(first, piece), piece), :],
                    piece_ref.at[:, pl.ds(at, cols)],
                    sems.at[distance - 1, number],
                )
            )
            at += cols
    for copy in copies:
        copy.start()
    for copy in copies:
        copy.wait()


def cut_rows(weights, n_head, piece):
    cols = sum(weight.shape[1] for weight in weights)
    anywhere = pl.BlockSpec(memory_space=pl.ANY)
    return pl.pallas_call(
        cut_kernel,
        out_shape=(jax.ShapeDtypeStruct((piece, cols), jnp.bfloat16),) * (n_head - 1),
        in_specs=[anywhere] * 3,
        out_specs=(anywhere,) * (n_head - 1),
        scratch_shapes=[pltpu.SemaphoreType.DMA((n_head - 1, 3))],
        cost_estimate=pl.CostEstimate(flops=0, bytes_accessed=2 * MIB, transcendentals=0),
        name="cut_rows",
    )(*in_hbm(*weights))


def project_kernel(x_ref, *refs):
    weight_refs, (out_ref, joined_ref, acc_ref) = refs[:-3], refs[-3:]
    step = pl.program_id(0)

    @pl.when(step == 0)
    def _():
        acc_ref[...] = jnp.zeros_like(acc_ref)

    if len(weight_refs) == 1:
        joined_ref = weight_refs[0]
    else:
        at = 0
        for weight_ref in weight_refs:
            joined_ref[:, at : at + weight_ref.shape[1]] = weight_ref[...]
            at += weight_ref.shape[1]
    acc_ref[...] += dot_nn(x_ref[...], joined_ref[...])

    @pl.when(step == pl.num_programs(0) - 1)
    def _():
        out_ref[...] = acc_ref[...].astype(out_ref.dtype)


def project(inputs, weights, name):
    rows, width = inputs.shape
    widths = [weight.shape[1] for weight in weights]
    cols = sum(widths)
    return pl.pallas_call(
        project_kernel,
        grid=(width // CHUNK,),
        in_specs=[pl.BlockSpec((rows, CHUNK), lambda i: (0, i))]
        + [pl.BlockSpec((CHUNK, cols), lambda i: (i, 0)) for cols in widths],
        out_specs=pl.BlockSpec((rows, cols), lambda i: (0, 0)),
        out_shape=jax.ShapeDtypeStruct((rows, cols), jnp.bfloat16),
        scratch_shapes=[pltpu.VMEM((CHUNK, cols), jnp.bfloat16), pltpu.VMEM((rows, cols), jnp.float32)],
        compiler_params=pltpu.CompilerParams(vmem_limit_bytes=32 * MIB),
        cost_estimate=pl.CostEstimate(
            flops=2 * rows * width * cols, bytes_accessed=2 * width * (rows + cols), transcendentals=0
        ),
        name=name,
    )(*in_hbm(inputs, *weights))


def combine_kernel(own_ref, *refs):
    back_refs, (low_ref, turned_ref) = refs[:-2], refs[-2:]
    total = own_ref[...]
    for back_ref in back_refs:
        total = total + back_ref[...].astype(jnp.float32)
    low_ref[...] = total.astype(jnp.bfloat16)
    turned_ref[...] = total.T.astype(jnp.bfloat16)


def combine(own, back):
    rows, cols = own.shape
    vmem = pl.BlockSpec(memory_space=pltpu.VMEM)
    shapes = ((rows, cols), (cols, rows))
    return pl.pallas_call(
        combine_kernel,
        out_shape=tuple(jax.ShapeDtypeStruct(shape, jnp.bfloat16) for shape in shapes),
        in_specs=[vmem] * (len(back) + 1),
        out_specs=(vmem,) * 2,
        compiler_params=pltpu.CompilerParams(vmem_limit_bytes=16 * MIB),
        cost_estimate=pl.CostEstimate(flops=rows * cols * 4, bytes_accessed=2 * MIB, transcendentals=0),
        name="combine",
    )(own, *back)


def terms_kernel(index_ref, joined_ref, other_joined_ref, x_ref, other_x_ref, *out_refs):
    step = pl.program_id(0)
    term = dot_nn(joined_ref[...], x_ref[...]) + dot_nn(other_joined_ref[...], other_x_ref[...])
    for chip, out_ref in enumerate(out_refs):

        @pl.when(step == chip)
        def _():
            out_ref[...] = term.astype(out_ref.dtype)


def weight_terms(index, joined, other_joined, inputs, other_inputs, n_ctx, name):
    cols, rows = joined.shape
    kept = inputs.shape[1] // n_ctx
    chips = n_ctx // 2
    whole = pl.BlockSpec((cols, rows), lambda i, index: (0, 0))
    part = pl.BlockSpec((rows, kept), lambda i, index: (0, index[i]))
    return pl.pallas_call(
        terms_kernel,
        grid_spec=pltpu.PrefetchScalarGridSpec(
            num_scalar_prefetch=1,
            grid=(chips,),
            in_specs=[whole, whole, part, part],
            out_specs=(pl.BlockSpec((cols, kept), lambda i, index: (0, 0)),) * chips,
        ),
        out_shape=tuple(
            jax.ShapeDtypeStruct((cols, kept), jnp.float32 if chip == 0 else jnp.bfloat16)
            for chip in range(chips)
        ),
        compiler_params=pltpu.CompilerParams(vmem_limit_bytes=32 * MIB),
        cost_estimate=pl.CostEstimate(
            flops=4 * cols * rows * kept * chips, bytes_accessed=10 * MIB, transcendentals=0
        ),
        name=name,
    )(index, joined, other_joined, inputs, other_inputs)


def rows_kernel(n_in, *refs):
    in_refs, out_refs = refs[:n_in], refs[n_in:]
    total = in_refs[0][...]
    for in_ref in in_refs[1:]:
        total = total + in_ref[...].astype(jnp.float32)
    at = 0
    for out_ref in out_refs:
        cols = slice(at, at + out_ref.shape[1])
        at = cols.stop
        out_ref[...] = total[cols, :].T


def weight_rows(terms, widths, name):
    kept = terms[0].shape[1]
    vmem = pl.BlockSpec(memory_space=pltpu.VMEM)
    return pl.pallas_call(
        partial(rows_kernel, len(terms)),
        out_shape=tuple(jax.ShapeDtypeStruct((kept, width), jnp.float32) for width in widths),
        in_specs=[vmem] * len(terms),
        out_specs=(vmem,) * len(widths),
        compiler_params=pltpu.CompilerParams(vmem_limit_bytes=32 * MIB),
        cost_estimate=pl.CostEstimate(flops=4 * MIB, bytes_accessed=6 * MIB, transcendentals=0),
        name=name,
    )(*terms)


def products_kernel(firsts, has_base, *refs):
    refs = refs[1:]
    out_ref = refs[-1]
    n_terms = len(firsts)
    total = refs[2 * n_terms][...] if has_base else None
    for at, first in enumerate(firsts):
        rows = refs[n_terms + at][...]
        rows = rows.reshape(-1, rows.shape[-1])
        term = dot_nt(refs[at][:, first : first + rows.shape[1]], rows)
        total = term if total is None else total + term
    out_ref[...] = total.astype(out_ref.dtype)


def products(lefts, rights, base, out_width, head, dtype, name):
    rows = lefts[0].shape[0]
    block = 256
    n_blocks = out_width // block
    left_specs = [pl.BlockSpec(left.shape, lambda i, head: (0, 0)) for left in lefts]
    right_specs = []
    firsts = []
    flops = 0
    for left, (array, *place) in zip(lefts, rights):
        cols = array.shape[1] if len(place) == 1 else place[2]
        flops += 2 * rows * cols * out_width
        if len(place) == 1:
            firsts.append(place[0])
            right_specs.append(
                pl.BlockSpec((block, cols), lambda i, head: (head[0] * n_blocks + i, 0))
            )
        else:
            step, first, cols = place
            piece = array.shape[2]
            firsts.append(0)
            right_specs.append(
                pl.BlockSpec(
                    (block // piece, 1, piece, cols),
                    partial(lambda step, at, i, head: (i, step, 0, at), step, first // cols),
                )
            )
    out_spec = pl.BlockSpec((rows, block), lambda i, head: (0, i))
    extra = [] if base is None else [base]
    return pl.pallas_call(
        partial(products_kernel, tuple(firsts), base is not None),
        grid_spec=pltpu.PrefetchScalarGridSpec(
            num_scalar_prefetch=1,
            grid=(n_blocks,),
            in_specs=left_specs + right_specs + [out_spec] * len(extra),
            out_specs=out_spec,
        ),
        out_shape=jax.ShapeDtypeStruct((rows, out_width), dtype),
        compiler_params=pltpu.CompilerParams(vmem_limit_bytes=32 * MIB),
        cost_estimate=pl.CostEstimate(flops=flops, bytes_accessed=8 * MIB, transcendentals=0),
        name=name,
    )(head, *lefts, *in_hbm(*[array for array, *place in rights]), *extra)


def attention_kernel(
    first_ref, query_ref, grad_ref, kv0, kv1, kv2, kv3,
    out_ref, dq_ref, dq_t_ref, d0, d1, d2, d3,
    kv_ref, acc_ref, score_ref, sum_ref, sems,
):
    rows = query_ref.shape[0]
    copies = [
        pltpu.make_async_copy(block, kv_ref.at[pl.ds(slot * rows, rows), :], sems.at[slot])
        for slot, block in enumerate((kv3, kv2, kv1, kv0))
    ]
    for copy in copies:
        copy.start()
    acc_ref[...] = jnp.zeros_like(acc_ref)
    for copy in copies:
        copy.wait()
    factor = HD ** (-0.5)
    wide = GROUP * GRAIN
    streams = range(TILE // GRAIN)
    key_local = lax.broadcasted_iota(jnp.int32, (TILE, wide), 0)
    query_local = lax.broadcasted_iota(jnp.int32, (TILE, wide), 1) % GRAIN
    heads = [slice(h * HD, (h + 1) * HD) for h in range(GROUP)]

    def tile_rows(tile):
        return pl.ds(pl.multiple_of(tile * TILE, TILE), TILE)

    for pair in range(rows // TILE):
        places = [pl.ds(pair * TILE + g * GRAIN, GRAIN) for g in streams]
        query = [jnp.concatenate([query_ref[here, cols] for cols in heads], axis=0) for here in places]
        grad = [jnp.concatenate([grad_ref[here, cols] for cols in heads], axis=0) for here in places]
        first = [first_ref[pair * len(places) + g] for g in streams]
        last = (SPAN * rows) // TILE + pair
        low = first[0] // TILE
        sum_ref[...] = jnp.zeros_like(sum_ref)

        def score_tile(tile, carry, diagonal):
            here = tile_rows(tile)
            following = []
            for g in streams:
                top, total = carry[g]
                score = dot_nt(kv_ref[here, :HD], query[g]) * (factor * LOG2E)
                keep = key_local >= first[g] - tile * TILE
                if diagonal:
                    keep = keep & (key_local <= query_local + g * GRAIN)
                score = jnp.where(keep, score, NEG)
                score_ref[g, here, :] = score
                new_top = jnp.maximum(top, jnp.max(score, axis=0, keepdims=True))
                weight = jnp.sum(jnp.exp2(score - new_top), axis=0, keepdims=True)
                following.append((new_top, total * jnp.exp2(top - new_top) + weight))
            return tuple(following)

        state = tuple(
            (jnp.full((1, wide), NEG, jnp.float32), jnp.zeros((1, wide), jnp.float32)) for g in streams
        )
        state = lax.fori_loop(low, last, lambda tile, carry: score_tile(tile, carry, False), state)
        state = score_tile(last, state, True)
        lse = [top + jnp.log2(total) for top, total in state]

        def output_tile(tile, carry):
            here = tile_rows(tile)
            value_grad = acc_ref[here, HD:]
            for g in streams:
                prob = jnp.exp2(score_ref[g, here, :] - lse[g])
                score_ref[g, here, :] = prob
                prob = prob.astype(jnp.bfloat16)
                sum_ref[g] += dot_tn(kv_ref[here, HD:], prob)
                value_grad = value_grad + dot_nn(prob, grad[g])
            acc_ref[here, HD:] = value_grad
            return carry

        lax.fori_loop(low, last + 1, output_tile, 0)
        delta = []
        for g in streams:
            turned = sum_ref[g].astype(jnp.bfloat16).astype(jnp.float32)
            delta.append(
                jnp.sum(turned * grad[g].astype(jnp.float32).T, axis=0, keepdims=True)
            )
            out_rows = turned.T.astype(jnp.bfloat16)
            for head, cols in enumerate(heads):
                out_ref[places[g], cols] = out_rows[head * GRAIN : (head + 1) * GRAIN]
        sum_ref[...] = jnp.zeros_like(sum_ref)

        def gradient_tile(tile, carry):
            here = tile_rows(tile)
            key_grad = acc_ref[here, :HD]
            for g in streams:
                dprob = dot_nt(kv_ref[here, HD:], grad[g])
                dscore = (score_ref[g, here, :] * (dprob - delta[g])).astype(jnp.bfloat16)
                key_grad = key_grad + dot_nn(dscore, query[g])
                sum_ref[g] += dot_tn(kv_ref[here, :HD], dscore)
            acc_ref[here, :HD] = key_grad
            return carry

        lax.fori_loop(low, last + 1, gradient_tile, 0)
        for g in streams:
            turned = sum_ref[g] * factor
            dquery = turned.T.astype(jnp.bfloat16)
            for head, cols in enumerate(heads):
                part = slice(head * GRAIN, (head + 1) * GRAIN)
                dq_ref[places[g], cols] = dquery[part]
                dq_t_ref[cols, places[g]] = turned[:, part].astype(jnp.bfloat16)
    for slot, block in enumerate((d3, d2, d1, d0)):
        place = pl.ds(slot * rows, rows)
        block[:, :HD] = (acc_ref[place, :HD] * factor).astype(block.dtype)
        block[:, HD:] = acc_ref[place, HD:].astype(block.dtype)


def attention(first, query, grad, kv_list):
    rows, cols = query.shape
    window = (SPAN + 1) * rows
    low = jax.ShapeDtypeStruct((rows, cols), jnp.bfloat16)
    turned = jax.ShapeDtypeStruct((cols, rows), jnp.bfloat16)
    own = jax.ShapeDtypeStruct((rows, 2 * HD), jnp.float32)
    sent = jax.ShapeDtypeStruct((rows, 2 * HD), jnp.bfloat16)
    vmem = pl.BlockSpec(memory_space=pltpu.VMEM)
    anywhere = pl.BlockSpec(memory_space=pl.ANY)
    return pl.pallas_call(
        attention_kernel,
        out_shape=(low, low, turned, own) + (sent,) * SPAN,
        in_specs=[pl.BlockSpec(memory_space=pltpu.SMEM), vmem, vmem] + [anywhere] * (SPAN + 1),
        out_specs=(vmem,) * (SPAN + 4),
        scratch_shapes=[
            pltpu.VMEM((window, 2 * HD), jnp.bfloat16),
            pltpu.VMEM((window, 2 * HD), jnp.float32),
            pltpu.VMEM((TILE // GRAIN, window, GROUP * GRAIN), jnp.float32),
            pltpu.VMEM((TILE // GRAIN, HD, GROUP * GRAIN), jnp.float32),
            pltpu.SemaphoreType.DMA((SPAN + 1,)),
        ],
        compiler_params=pltpu.CompilerParams(vmem_limit_bytes=32 * MIB),
        cost_estimate=pl.CostEstimate(
            flops=6 * 2 * rows * window * cols, bytes_accessed=6 * MIB, transcendentals=0
        ),
        name="attention",
    )(first, query, grad, *kv_list)


def shift(value, axis, steps):
    count = lax.axis_size(axis)
    pairs = [(i, i + steps) for i in range(count) if 0 <= i + steps < count]
    return lax.ppermute(value, axis, pairs)


def swap(value, axis, mask):
    return lax.ppermute(value, axis, [(i, i ^ mask) for i in range(lax.axis_size(axis))])


def rotate(value, axis, steps):
    count = lax.axis_size(axis)
    return lax.ppermute(value, axis, [(i, (i + steps) % count) for i in range(count)])


def body(inputs, query_weight, key_weight, value_weight, out_grad, doc_lengths):
    tok_rows, width = inputs.shape
    n_ctx = lax.axis_size("ctx")
    n_head = lax.axis_size("head")
    chips = n_ctx // 2
    ctx = lax.axis_index("ctx")
    head = lax.axis_index("head")
    q_cols = query_weight.shape[1]
    k_cols = key_weight.shape[1]

    weights = (query_weight, key_weight, value_weight)
    out_width = width // n_head
    piece = out_width // n_ctx
    pieces = cut_rows(weights, n_head, piece)
    pieces, inputs = lax.optimization_barrier((pieces, inputs))
    pieces = [rotate(rows, "head", step) for step, rows in enumerate(pieces, 1)]

    kv_loc = project(inputs, (key_weight, value_weight), "project_kv")
    kv_list = [kv_loc] + [shift(kv_loc, "ctx", distance) for distance in range(1, SPAN + 1)]
    late_inputs, kv_loc = lax.optimization_barrier((inputs, kv_loc))
    query = project(late_inputs, (query_weight,), "project_query")
    query, kv_list, pieces, inputs = lax.optimization_barrier((query, kv_list, pieces, inputs))
    gathered = lax.all_gather(jnp.concatenate(pieces, axis=0), "ctx", axis=0, tiled=True)
    gathered = gathered.reshape(n_ctx, n_head - 1, piece, q_cols + 2 * k_cols)

    other_inputs = swap(inputs, "ctx", 1)

    granules = tok_rows // GRAIN
    window_start = (ctx - SPAN) * tok_rows
    positions = ctx * tok_rows + GRAIN * jnp.arange(granules, dtype=jnp.int32)
    doc_ends = jnp.cumsum(doc_lengths)
    starts = jnp.sum(
        jnp.where(doc_ends[None, :] <= positions[:, None], doc_lengths[None, :], 0), axis=1
    )
    attn_out, dq_low, dq_turned, own_grads, *sent_grads = attention(
        starts - window_start, query, out_grad, kv_list
    )

    back = [shift(sent_grads[distance - 1], "ctx", -distance) for distance in range(1, SPAN + 1)]
    dq_up = rotate(dq_low, "head", 1)

    index = ((ctx // 2) ^ jnp.arange(chips, dtype=jnp.int32)) * 2 + ctx % 2
    other_dq = swap(dq_turned, "ctx", 1)
    q_terms = weight_terms(index, dq_turned, other_dq, inputs, other_inputs, n_ctx, "query_terms")
    q_terms, back = lax.optimization_barrier((q_terms, back))
    q_moved = [swap(term, "ctx", 2 * chip) for chip, term in enumerate(q_terms) if chip > 0]
    dkv_low, dkv_turned = combine(own_grads, back)
    other_dkv = swap(dkv_turned, "ctx", 1)
    dkv_up = rotate(dkv_low, "head", 1)
    kv_terms = weight_terms(index, dkv_turned, other_dkv, inputs, other_inputs, n_ctx, "key_terms")
    dq_up, kv_terms, dkv_low, dq_low = lax.optimization_barrier((dq_up, kv_terms, dkv_low, dq_low))
    dq_far = rotate(dq_up, "head", 1)
    dq_down = rotate(dq_low, "head", -1)
    kv_moved = [swap(term, "ctx", 2 * chip) for chip, term in enumerate(kv_terms) if chip > 0]
    dkv_down = rotate(dkv_low, "head", -1)
    dkv_far = rotate(dkv_up, "head", 1)

    head_index = jnp.reshape(head, (1,)).astype(jnp.int32)
    q_place, kv_place = (0, q_cols), (q_cols, 2 * k_cols)
    grad_sum = products(
        (dq_low, dkv_low, dkv_low, dq_up, dkv_up),
        (
            (query_weight, 0), (key_weight, 0), (value_weight, k_cols),
            (gathered, 0, *q_place), (gathered, 0, *kv_place),
        ),
        None, out_width, head_index, jnp.float32, "products_near",
    )
    grad_sum, q_moved, dq_down = lax.optimization_barrier((grad_sum, q_moved, dq_down))
    q_grad, = weight_rows([q_terms[0], *q_moved], (q_cols,), "query_rows")
    grad_sum = products(
        (dq_far, dq_down, dkv_down),
        ((gathered, 1, *q_place), (gathered, 2, *q_place), (gathered, 2, *kv_place)),
        grad_sum, out_width, head_index, jnp.float32, "products_mid",
    )
    grad_sum, kv_moved = lax.optimization_barrier((grad_sum, kv_moved))
    k_grad, v_grad = weight_rows([kv_terms[0], *kv_moved], (k_cols, k_cols), "key_rows")
    grad_sum, q_grad, k_grad, v_grad = lax.optimization_barrier((grad_sum, q_grad, k_grad, v_grad))
    input_grad = products(
        (dkv_far,), ((gathered, 1, *kv_place),),
        grad_sum, out_width, head_index, jnp.bfloat16, "products_far",
    )
    return (attn_out, input_grad, q_grad, k_grad, v_grad)


def solution(mesh):
    return jax.shard_map(
        body,
        mesh=mesh,
        in_specs=(
            P("ctx", None),
            P(None, "head"),
            P(None, "head"),
            P(None, "head"),
            P("ctx", "head"),
            P(),
        ),
        out_specs=(P("ctx", "head"),) * 5,
        check_vma=False,
    )
```

```python
from functools import partial

import jax
import jax.numpy as jnp
from jax import lax
from jax.experimental import pallas as pl
from jax.experimental.pallas import tpu as pltpu
from jax.sharding import PartitionSpec as P

HD = 128
GROUP = 4
SPAN = 3
GRAIN = 128
TILE = 256
CHUNK = 1024
MIB = 2**20

NEG = -1e30
LOG2E = 1.4426950408889634


def dot_nt(left_mat, right_mat):
    return lax.dot_general(
        left_mat, right_mat, (((1,), (1,)), ((), ())), preferred_element_type=jnp.float32
    )


def dot_tn(left_mat, right_mat):
    return lax.dot_general(
        left_mat, right_mat, (((0,), (0,)), ((), ())), preferred_element_type=jnp.float32
    )


def dot_nn(left_mat, right_mat):
    return jnp.dot(left_mat, right_mat, preferred_element_type=jnp.float32)


def in_hbm(*arrays):
    return [pltpu.with_memory_space_constraint(array, pltpu.HBM) for array in arrays]


def cut_kernel(*refs):
    weight_refs, piece_refs, sems = refs[:3], refs[3:-1], refs[-1]
    head, ctx = lax.axis_index("head"), lax.axis_index("ctx")
    n_head = len(piece_refs) + 1
    piece = piece_refs[0].shape[0]
    copies = []
    for distance, piece_ref in enumerate(piece_refs, 1):
        group = lax.rem(head + distance, n_head)
        first = group * (weight_refs[0].shape[0] // n_head) + ctx * piece
        at = 0
        for number, weight_ref in enumerate(weight_refs):
            cols = weight_ref.shape[1]
            copies.append(
                pltpu.make_async_copy(
                    weight_ref.at[pl.ds(pl.multiple_of(first, piece), piece), :],
                    piece_ref.at[:, pl.ds(at, cols)],
                    sems.at[distance - 1, number],
                )
            )
            at += cols
    for copy in copies:
        copy.start()
    for copy in copies:
        copy.wait()


def cut_rows(weights, n_head, piece):
    cols = sum(weight.shape[1] for weight in weights)
    anywhere = pl.BlockSpec(memory_space=pl.ANY)
    return pl.pallas_call(
        cut_kernel,
        out_shape=(jax.ShapeDtypeStruct((piece, cols), jnp.bfloat16),) * (n_head - 1),
        in_specs=[anywhere] * 3,
        out_specs=(pl.BlockSpec(memory_space=pltpu.VMEM),) * (n_head - 1),
        scratch_shapes=[pltpu.SemaphoreType.DMA((n_head - 1, 3))],
        cost_estimate=pl.CostEstimate(flops=0, bytes_accessed=2 * MIB, transcendentals=0),
        name="cut_rows",
    )(*in_hbm(*weights))


def project_kernel(x_ref, *refs):
    weight_refs, (out_ref, joined_ref, acc_ref) = refs[:-3], refs[-3:]
    step = pl.program_id(0)

    @pl.when(step == 0)
    def _():
        acc_ref[...] = jnp.zeros_like(acc_ref)

    if len(weight_refs) == 1:
        joined_ref = weight_refs[0]
    else:
        at = 0
        for weight_ref in weight_refs:
            joined_ref[:, at : at + weight_ref.shape[1]] = weight_ref[...]
            at += weight_ref.shape[1]
    acc_ref[...] += dot_nn(x_ref[...], joined_ref[...])

    @pl.when(step == pl.num_programs(0) - 1)
    def _():
        out_ref[...] = acc_ref[...].astype(out_ref.dtype)


def project(inputs, weights, name):
    rows, width = inputs.shape
    widths = [weight.shape[1] for weight in weights]
    cols = sum(widths)
    return pl.pallas_call(
        project_kernel,
        grid=(width // CHUNK,),
        in_specs=[pl.BlockSpec((rows, CHUNK), lambda i: (0, i))]
        + [pl.BlockSpec((CHUNK, cols), lambda i: (i, 0)) for cols in widths],
        out_specs=pl.BlockSpec((rows, cols), lambda i: (0, 0)),
        out_shape=jax.ShapeDtypeStruct((rows, cols), jnp.bfloat16),
        scratch_shapes=[pltpu.VMEM((CHUNK, cols), jnp.bfloat16), pltpu.VMEM((rows, cols), jnp.float32)],
        compiler_params=pltpu.CompilerParams(vmem_limit_bytes=32 * MIB),
        cost_estimate=pl.CostEstimate(
            flops=2 * rows * width * cols, bytes_accessed=2 * width * (rows + cols), transcendentals=0
        ),
        name=name,
    )(*in_hbm(inputs, *weights))


def combine_kernel(own_ref, *refs):
    back_refs, (low_ref, turned_ref) = refs[:-2], refs[-2:]
    total = own_ref[...]
    for back_ref in back_refs:
        total = total + back_ref[...].astype(jnp.float32)
    low_ref[...] = total.astype(jnp.bfloat16)
    turned_ref[...] = total.T.astype(jnp.bfloat16)


def combine(own, back):
    rows, cols = own.shape
    vmem = pl.BlockSpec(memory_space=pltpu.VMEM)
    shapes = ((rows, cols), (cols, rows))
    return pl.pallas_call(
        combine_kernel,
        out_shape=tuple(jax.ShapeDtypeStruct(shape, jnp.bfloat16) for shape in shapes),
        in_specs=[vmem] * (len(back) + 1),
        out_specs=(vmem,) * 2,
        compiler_params=pltpu.CompilerParams(vmem_limit_bytes=16 * MIB),
        cost_estimate=pl.CostEstimate(flops=rows * cols * 4, bytes_accessed=2 * MIB, transcendentals=0),
        name="combine",
    )(own, *back)


def terms_kernel(joined_ref, other_joined_ref, x_ref, other_x_ref, *out_refs):
    step = pl.program_id(0)
    term = dot_nn(joined_ref[...], x_ref[...]) + dot_nn(other_joined_ref[...], other_x_ref[...])
    for chip, out_ref in enumerate(out_refs):

        @pl.when(step == chip)
        def _():
            out_ref[...] = term.astype(out_ref.dtype)


def weight_terms(joined, other_joined, inputs, other_inputs, n_ctx, name):
    cols, rows = joined.shape
    kept = inputs.shape[1] // n_ctx
    chips = n_ctx // 2

    def place(i):
        ctx = lax.axis_index("ctx")
        return 0, ((ctx // 2) ^ i) * 2 + ctx % 2

    whole = pl.BlockSpec((cols, rows), lambda i: (0, 0))
    part = pl.BlockSpec((rows, kept), place)
    return pl.pallas_call(
        terms_kernel,
        grid=(chips,),
        in_specs=[whole, whole, part, part],
        out_specs=(pl.BlockSpec((cols, kept), lambda i: (0, 0)),) * chips,
        out_shape=tuple(
            jax.ShapeDtypeStruct((cols, kept), jnp.float32 if chip == 0 else jnp.bfloat16)
            for chip in range(chips)
        ),
        compiler_params=pltpu.CompilerParams(vmem_limit_bytes=32 * MIB),
        cost_estimate=pl.CostEstimate(
            flops=4 * cols * rows * kept * chips, bytes_accessed=10 * MIB, transcendentals=0
        ),
        name=name,
    )(joined, other_joined, inputs, other_inputs)


def rows_kernel(n_in, *refs):
    in_refs, out_refs = refs[:n_in], refs[n_in:]
    total = in_refs[0][...]
    for in_ref in in_refs[1:]:
        total = total + in_ref[...].astype(jnp.float32)
    at = 0
    for out_ref in out_refs:
        cols = slice(at, at + out_ref.shape[1])
        at = cols.stop
        out_ref[...] = total[cols, :].T


def weight_rows(terms, widths, name):
    kept = terms[0].shape[1]
    vmem = pl.BlockSpec(memory_space=pltpu.VMEM)
    return pl.pallas_call(
        partial(rows_kernel, len(terms)),
        out_shape=tuple(jax.ShapeDtypeStruct((kept, width), jnp.float32) for width in widths),
        in_specs=[vmem] * len(terms),
        out_specs=(vmem,) * len(widths),
        compiler_params=pltpu.CompilerParams(vmem_limit_bytes=32 * MIB),
        cost_estimate=pl.CostEstimate(flops=4 * MIB, bytes_accessed=6 * MIB, transcendentals=0),
        name=name,
    )(*terms)


def own_products_kernel(dq_ref, dkv_ref, query_ref, key_ref, value_ref, out_ref):
    k_cols = key_ref.shape[1]
    out_ref[...] = (
        dot_nt(dq_ref[...], query_ref[...])
        + dot_nt(dkv_ref[:, :k_cols], key_ref[...])
        + dot_nt(dkv_ref[:, k_cols:], value_ref[...])
    )


def own_products(dq, dkv, weights, out_width):
    rows = dq.shape[0]
    block = 512
    n_blocks = out_width // block

    def fixed(array):
        return pl.BlockSpec(array.shape, lambda i: (0, 0))

    return pl.pallas_call(
        own_products_kernel,
        grid=(n_blocks,),
        in_specs=[fixed(dq), fixed(dkv)]
        + [
            pl.BlockSpec((block, w.shape[1]), lambda i: (lax.axis_index("head") * n_blocks + i, 0))
            for w in weights
        ],
        out_specs=pl.BlockSpec((rows, block), lambda i: (0, i)),
        out_shape=jax.ShapeDtypeStruct((rows, out_width), jnp.float32),
        compiler_params=pltpu.CompilerParams(vmem_limit_bytes=32 * MIB),
        cost_estimate=pl.CostEstimate(
            flops=2 * rows * out_width * (dq.shape[1] + dkv.shape[1]), bytes_accessed=4 * MIB, transcendentals=0
        ),
        name="products_own",
    )(dq, dkv, *in_hbm(*weights))


def products_kernel(steps, first, block, base_ref, *refs):
    left_refs, (rows_ref, out_ref) = refs[:-2], refs[-2:]
    n_rows, cols = left_refs[0].shape[0], left_refs[0].shape[1]
    piece = rows_ref.shape[2]
    for at in range(out_ref.shape[1] // block):
        total = base_ref[:, at * block : (at + 1) * block]
        for left_ref, step in zip(left_refs, steps):
            rows = rows_ref[at * block // piece : (at + 1) * block // piece, step - 1, :, first : first + cols]
            total = total + dot_nt(left_ref[...], rows.reshape(block, cols))
        out_ref[:, at * block : (at + 1) * block] = total.astype(out_ref.dtype)


def products(base, lefts, steps, gathered, first, dtype, name):
    rows, out_width = base.shape
    cols = lefts[0].shape[1]
    vmem = pl.BlockSpec(memory_space=pltpu.VMEM)
    return pl.pallas_call(
        partial(products_kernel, steps, first, 256),
        in_specs=[vmem] * (len(lefts) + 2),
        out_specs=vmem,
        out_shape=jax.ShapeDtypeStruct((rows, out_width), dtype),
        compiler_params=pltpu.CompilerParams(vmem_limit_bytes=32 * MIB),
        cost_estimate=pl.CostEstimate(
            flops=2 * rows * out_width * cols * len(lefts), bytes_accessed=8 * MIB, transcendentals=0
        ),
        name=name,
    )(base, *lefts, gathered)


def attention_kernel(
    first_ref, query_ref, grad_ref, kv0, kv1, kv2, kv3,
    out_ref, dq_ref, dq_t_ref, d0, d1, d2, d3,
    kv_ref, acc_ref, score_ref, sum_ref, sems,
):
    rows = query_ref.shape[0]
    copies = [
        pltpu.make_async_copy(block, kv_ref.at[pl.ds(slot * rows, rows), :], sems.at[slot])
        for slot, block in enumerate((kv3, kv2, kv1, kv0))
    ]
    for copy in copies:
        copy.start()
    acc_ref[...] = jnp.zeros_like(acc_ref)
    for copy in copies:
        copy.wait()
    factor = HD ** (-0.5)
    wide = GROUP * GRAIN
    streams = range(TILE // GRAIN)
    key_local = lax.broadcasted_iota(jnp.int32, (TILE, wide), 0)
    query_local = lax.broadcasted_iota(jnp.int32, (TILE, wide), 1) % GRAIN
    heads = [slice(h * HD, (h + 1) * HD) for h in range(GROUP)]

    def tile_rows(tile):
        return pl.ds(pl.multiple_of(tile * TILE, TILE), TILE)

    for pair in range(rows // TILE):
        places = [pl.ds(pair * TILE + g * GRAIN, GRAIN) for g in streams]
        query = [jnp.concatenate([query_ref[here, cols] for cols in heads], axis=0) for here in places]
        grad = [jnp.concatenate([grad_ref[here, cols] for cols in heads], axis=0) for here in places]
        first = [first_ref[pair * len(places) + g] for g in streams]
        last = (SPAN * rows) // TILE + pair
        low = first[0] // TILE
        sum_ref[...] = jnp.zeros_like(sum_ref)

        def score_tile(tile, carry, diagonal):
            here = tile_rows(tile)
            following = []
            for g in streams:
                top, total = carry[g]
                score = dot_nt(kv_ref[here, :HD], query[g]) * (factor * LOG2E)
                keep = key_local >= first[g] - tile * TILE
                if diagonal:
                    keep = keep & (key_local <= query_local + g * GRAIN)
                score = jnp.where(keep, score, NEG)
                score_ref[g, here, :] = score
                new_top = jnp.maximum(top, jnp.max(score, axis=0, keepdims=True))
                weight = jnp.sum(jnp.exp2(score - new_top), axis=0, keepdims=True)
                following.append((new_top, total * jnp.exp2(top - new_top) + weight))
            return tuple(following)

        state = tuple(
            (jnp.full((1, wide), NEG, jnp.float32), jnp.zeros((1, wide), jnp.float32)) for g in streams
        )
        state = lax.fori_loop(low, last, lambda tile, carry: score_tile(tile, carry, False), state)
        state = score_tile(last, state, True)
        lse = [top + jnp.log2(total) for top, total in state]

        def output_tile(tile, carry):
            here = tile_rows(tile)
            value_grad = acc_ref[here, HD:]
            for g in streams:
                prob = jnp.exp2(score_ref[g, here, :] - lse[g])
                score_ref[g, here, :] = prob
                prob = prob.astype(jnp.bfloat16)
                sum_ref[g] += dot_tn(kv_ref[here, HD:], prob)
                value_grad = value_grad + dot_nn(prob, grad[g])
            acc_ref[here, HD:] = value_grad
            return carry

        lax.fori_loop(low, last + 1, output_tile, 0)
        delta = []
        for g in streams:
            turned = sum_ref[g].astype(jnp.bfloat16).astype(jnp.float32)
            delta.append(
                jnp.sum(turned * grad[g].astype(jnp.float32).T, axis=0, keepdims=True)
            )
            out_rows = turned.T.astype(jnp.bfloat16)
            for head, cols in enumerate(heads):
                out_ref[places[g], cols] = out_rows[head * GRAIN : (head + 1) * GRAIN]
        sum_ref[...] = jnp.zeros_like(sum_ref)

        def gradient_tile(tile, carry):
            here = tile_rows(tile)
            key_grad = acc_ref[here, :HD]
            for g in streams:
                dprob = dot_nt(kv_ref[here, HD:], grad[g])
                dscore = (score_ref[g, here, :] * (dprob - delta[g])).astype(jnp.bfloat16)
                key_grad = key_grad + dot_nn(dscore, query[g])
                sum_ref[g] += dot_tn(kv_ref[here, :HD], dscore)
            acc_ref[here, :HD] = key_grad
            return carry

        lax.fori_loop(low, last + 1, gradient_tile, 0)
        for g in streams:
            turned = sum_ref[g] * factor
            dquery = turned.T.astype(jnp.bfloat16)
            for head, cols in enumerate(heads):
                part = slice(head * GRAIN, (head + 1) * GRAIN)
                dq_ref[places[g], cols] = dquery[part]
                dq_t_ref[cols, places[g]] = turned[:, part].astype(jnp.bfloat16)
    for slot, block in enumerate((d3, d2, d1, d0)):
        place = pl.ds(slot * rows, rows)
        block[:, :HD] = (acc_ref[place, :HD] * factor).astype(block.dtype)
        block[:, HD:] = acc_ref[place, HD:].astype(block.dtype)


def attention(first, query, grad, kv_list):
    rows, cols = query.shape
    window = (SPAN + 1) * rows
    low = jax.ShapeDtypeStruct((rows, cols), jnp.bfloat16)
    turned = jax.ShapeDtypeStruct((cols, rows), jnp.bfloat16)
    own = jax.ShapeDtypeStruct((rows, 2 * HD), jnp.float32)
    sent = jax.ShapeDtypeStruct((rows, 2 * HD), jnp.bfloat16)
    vmem = pl.BlockSpec(memory_space=pltpu.VMEM)
    anywhere = pl.BlockSpec(memory_space=pl.ANY)
    return pl.pallas_call(
        attention_kernel,
        out_shape=(low, low, turned, own) + (sent,) * SPAN,
        in_specs=[pl.BlockSpec(memory_space=pltpu.SMEM), vmem, vmem] + [anywhere] * (SPAN + 1),
        out_specs=(vmem,) * (SPAN + 4),
        scratch_shapes=[
            pltpu.VMEM((window, 2 * HD), jnp.bfloat16),
            pltpu.VMEM((window, 2 * HD), jnp.float32),
            pltpu.VMEM((TILE // GRAIN, window, GROUP * GRAIN), jnp.float32),
            pltpu.VMEM((TILE // GRAIN, HD, GROUP * GRAIN), jnp.float32),
            pltpu.SemaphoreType.DMA((SPAN + 1,)),
        ],
        compiler_params=pltpu.CompilerParams(vmem_limit_bytes=32 * MIB),
        cost_estimate=pl.CostEstimate(
            flops=6 * 2 * rows * window * cols, bytes_accessed=6 * MIB, transcendentals=0
        ),
        name="attention",
    )(first, query, grad, *kv_list)


def shift(value, axis, steps):
    count = lax.axis_size(axis)
    pairs = [(i, i + steps) for i in range(count) if 0 <= i + steps < count]
    return lax.ppermute(value, axis, pairs)


def swap(value, axis, mask):
    return lax.ppermute(value, axis, [(i, i ^ mask) for i in range(lax.axis_size(axis))])


def rotate(value, axis, steps):
    count = lax.axis_size(axis)
    return lax.ppermute(value, axis, [(i, (i + steps) % count) for i in range(count)])


def body(inputs, query_weight, key_weight, value_weight, out_grad, doc_lengths):
    tok_rows, width = inputs.shape
    n_ctx = lax.axis_size("ctx")
    n_head = lax.axis_size("head")
    chips = n_ctx // 2
    ctx = lax.axis_index("ctx")
    head = lax.axis_index("head")
    q_cols = query_weight.shape[1]
    k_cols = key_weight.shape[1]

    weights = (query_weight, key_weight, value_weight)
    out_width = width // n_head
    piece = out_width // n_ctx
    pieces = cut_rows(weights, n_head, piece)
    pieces, inputs = lax.optimization_barrier((pieces, inputs))
    pieces = [rotate(rows, "head", step) for step, rows in enumerate(pieces, 1)]

    kv_loc = project(inputs, (key_weight, value_weight), "project_kv")
    kv_list = [kv_loc] + [shift(kv_loc, "ctx", distance) for distance in range(1, SPAN + 1)]
    late_inputs, kv_loc = lax.optimization_barrier((inputs, kv_loc))
    query = project(late_inputs, (query_weight,), "project_query")
    query, kv_list, pieces, inputs = lax.optimization_barrier((query, kv_list, pieces, inputs))
    gathered = lax.all_gather(jnp.concatenate(pieces, axis=0), "ctx", axis=0, tiled=True)
    gathered = gathered.reshape(n_ctx, n_head - 1, piece, q_cols + 2 * k_cols)

    other_inputs = swap(inputs, "ctx", 1)

    granules = tok_rows // GRAIN
    window_start = (ctx - SPAN) * tok_rows
    positions = ctx * tok_rows + GRAIN * jnp.arange(granules, dtype=jnp.int32)
    doc_ends = jnp.cumsum(doc_lengths)
    starts = jnp.sum(
        jnp.where(doc_ends[None, :] <= positions[:, None], doc_lengths[None, :], 0), axis=1
    )
    attn_out, dq_low, dq_turned, own_grads, *sent_grads = attention(
        starts - window_start, query, out_grad, kv_list
    )

    back = [shift(sent_grads[distance - 1], "ctx", -distance) for distance in range(1, SPAN + 1)]
    dq_up = rotate(dq_low, "head", 1)

    other_dq = swap(dq_turned, "ctx", 1)
    q_terms = weight_terms(dq_turned, other_dq, inputs, other_inputs, n_ctx, "query_terms")
    q_moved = [swap(term, "ctx", 2 * chip) for chip, term in enumerate(q_terms) if chip > 0]
    _, dq_low, back, dq_up = lax.optimization_barrier((q_terms, dq_low, back, dq_up))
    dq_far = rotate(dq_up, "head", 1)
    dq_down = rotate(dq_low, "head", -1)
    dkv_low, dkv_turned = combine(own_grads, back)
    dkv_all = lax.all_gather(dkv_low, "head", axis=0, tiled=True)
    other_dkv = swap(dkv_turned, "ctx", 1)
    kv_terms = weight_terms(dkv_turned, other_dkv, inputs, other_inputs, n_ctx, "key_terms")
    kv_terms, dq_far, dq_down, dkv_low = lax.optimization_barrier((kv_terms, dq_far, dq_down, dkv_low))
    kv_moved = [swap(term, "ctx", 2 * chip) for chip, term in enumerate(kv_terms) if chip > 0]

    grad_sum = own_products(dq_low, dkv_low, weights, out_width)
    grad_sum = products(
        grad_sum, (dq_up, dq_far, dq_down), (1, 2, 3), gathered, 0, jnp.float32, "products_query"
    )
    grad_sum, q_moved = lax.optimization_barrier((grad_sum, q_moved))
    q_grad, = weight_rows([q_terms[0], *q_moved], (q_cols,), "query_rows")
    q_grad, kv_moved, dkv_all = lax.optimization_barrier((q_grad, kv_moved, dkv_all))
    k_grad, v_grad = weight_rows([kv_terms[0], *kv_moved], (k_cols, k_cols), "key_rows")
    steps = tuple(range(1, n_head))
    dkv_others = [
        lax.dynamic_slice_in_dim(dkv_all, (head - step) % n_head * tok_rows, tok_rows, 0) for step in steps
    ]
    input_grad = products(grad_sum, dkv_others, steps, gathered, q_cols, jnp.bfloat16, "products_key")
    return (attn_out, input_grad, q_grad, k_grad, v_grad)


def solution(mesh):
    return jax.shard_map(
        body,
        mesh=mesh,
        in_specs=(
            P("ctx", None),
            P(None, "head"),
            P(None, "head"),
            P(None, "head"),
            P("ctx", "head"),
            P(),
        ),
        out_specs=(P("ctx", "head"),) * 5,
        check_vma=False,
    )
```

```python
from functools import partial

import jax
import jax.numpy as jnp
from jax import lax
from jax.experimental import pallas as pl
from jax.experimental.pallas import tpu as pltpu
from jax.sharding import PartitionSpec as P

HD = 128
GROUP = 4
SPAN = 3
GRAIN = 128
TILE = 256
CHUNK = 512
MIB = 2**20
VMEM = 32 * MIB

NEG = -1e30
LOG2E = 1.4426950408889634


def dot_nt(left_mat, right_mat):
    return lax.dot_general(
        left_mat, right_mat, (((1,), (1,)), ((), ())), preferred_element_type=jnp.float32
    )


def dot_tn(left_mat, right_mat):
    return lax.dot_general(
        left_mat, right_mat, (((0,), (0,)), ((), ())), preferred_element_type=jnp.float32
    )


def dot_nn(left_mat, right_mat):
    return jnp.dot(left_mat, right_mat, preferred_element_type=jnp.float32)


def in_hbm(*arrays):
    return [pltpu.with_memory_space_constraint(array, pltpu.HBM) for array in arrays]


def cut_kernel(*refs):
    weight_refs, piece_refs, sems = refs[:3], refs[3:-1], refs[-1]
    head, ctx = lax.axis_index("head"), lax.axis_index("ctx")
    n_head = len(piece_refs) + 1
    piece = piece_refs[0].shape[0]
    copies = []
    for distance, piece_ref in enumerate(piece_refs, 1):
        group = lax.rem(head + distance, n_head)
        first = group * (weight_refs[0].shape[0] // n_head) + ctx * piece
        at = 0
        for number, weight_ref in enumerate(weight_refs):
            cols = weight_ref.shape[1]
            copies.append(
                pltpu.make_async_copy(
                    weight_ref.at[pl.ds(pl.multiple_of(first, piece), piece), :],
                    piece_ref.at[:, pl.ds(at, cols)],
                    sems.at[distance - 1, number],
                )
            )
            at += cols
    for copy in copies:
        copy.start()
    for copy in copies:
        copy.wait()


def cut_rows(weights, n_head, piece):
    cols = sum(weight.shape[1] for weight in weights)
    anywhere = pl.BlockSpec(memory_space=pl.ANY)
    return pl.pallas_call(
        cut_kernel,
        out_shape=(jax.ShapeDtypeStruct((piece, cols), jnp.bfloat16),) * (n_head - 1),
        in_specs=[anywhere] * 3,
        out_specs=(pl.BlockSpec(memory_space=pltpu.VMEM),) * (n_head - 1),
        scratch_shapes=[pltpu.SemaphoreType.DMA((n_head - 1, 3))],
        cost_estimate=pl.CostEstimate(flops=0, bytes_accessed=2 * MIB, transcendentals=0),
        name="cut_rows",
    )(*in_hbm(*weights))


def project_kernel(x_ref, *refs):
    n = len(refs) - 4
    weight_refs, (out_ref, x_here, weight_here, sems) = refs[:n], refs[n:]
    rows = x_ref.shape[0]
    chunks = []
    for step in range(x_ref.shape[1] // CHUNK):
        part = pl.ds(step * CHUNK, CHUNK)
        copies = [pltpu.make_async_copy(x_ref.at[:, part], x_here.at[:, part], sems.at[step, 0])]
        at = 0
        for number, weight_ref in enumerate(weight_refs):
            cols = pl.ds(at, weight_ref.shape[1])
            at += weight_ref.shape[1]
            copies.append(
                pltpu.make_async_copy(
                    weight_ref.at[part, :], weight_here.at[part, cols], sems.at[step, 1 + number]
                )
            )
        for copy in copies:
            copy.start()
        chunks.append((part, copies))
    total = jnp.zeros((rows, weight_here.shape[1]), jnp.float32)
    for part, copies in chunks:
        for copy in copies:
            copy.wait()
        total = total + dot_nn(x_here[:, part], weight_here[part, :])
    out_ref[...] = total.astype(out_ref.dtype)


def project(inputs, weights, name):
    rows, width = inputs.shape
    cols = sum(weight.shape[1] for weight in weights)
    anywhere = pl.BlockSpec(memory_space=pl.ANY)
    return pl.pallas_call(
        project_kernel,
        in_specs=[anywhere] * (len(weights) + 1),
        out_specs=pl.BlockSpec(memory_space=pltpu.VMEM),
        out_shape=jax.ShapeDtypeStruct((rows, cols), jnp.bfloat16),
        scratch_shapes=[
            pltpu.VMEM((rows, width), jnp.bfloat16),
            pltpu.VMEM((width, cols), jnp.bfloat16),
            pltpu.SemaphoreType.DMA((width // CHUNK, len(weights) + 1)),
        ],
        compiler_params=pltpu.CompilerParams(vmem_limit_bytes=VMEM),
        cost_estimate=pl.CostEstimate(
            flops=2 * rows * width * cols, bytes_accessed=2 * width * (rows + cols), transcendentals=0
        ),
        name=name,
    )(*in_hbm(inputs, *weights))


def combine_kernel(own_ref, *refs):
    back_refs, (dq_t_ref, low_ref, turned_ref) = refs[:-3], refs[-3:]
    total = own_ref[...]
    for back_ref in back_refs:
        total = total + back_ref[...].astype(jnp.float32)
    low_ref[...] = total.astype(jnp.bfloat16)
    q_cols = dq_t_ref.shape[0]
    turned_ref[:q_cols, :] = dq_t_ref[...]
    turned_ref[q_cols:, :] = total.T.astype(jnp.bfloat16)


def combine(own, back, dq_turned):
    rows, cols = own.shape
    q_cols = dq_turned.shape[0]
    whole = pl.BlockSpec((rows, cols), lambda i: (0, 0))
    shapes = ((rows, cols), (q_cols + cols, rows))
    return pl.pallas_call(
        combine_kernel,
        grid=(1,),
        out_shape=tuple(jax.ShapeDtypeStruct(shape, jnp.bfloat16) for shape in shapes),
        in_specs=[whole] * (len(back) + 1) + [pl.BlockSpec((q_cols, rows), lambda i: (0, 0))],
        out_specs=tuple(pl.BlockSpec(shape, lambda i: (0, 0)) for shape in shapes),
        compiler_params=pltpu.CompilerParams(vmem_limit_bytes=VMEM),
        cost_estimate=pl.CostEstimate(flops=rows * cols * 4, bytes_accessed=2 * MIB, transcendentals=0),
        name="combine",
    )(own, *back, dq_turned)


def terms_kernel(chips, turned_ref, other_turned_ref, x_ref, other_x_ref, *refs):
    out_refs, (x_here, sum_here, low_here, in_sems, out_sems) = refs[:chips], refs[chips:]
    kept = out_refs[0].shape[1]
    ctx = lax.axis_index("ctx")
    order = [*range(1, chips), 0]
    coming = {}
    for chip in order:
        first = pl.multiple_of((((ctx // 2) ^ chip) * 2 + ctx % 2) * kept, kept)
        coming[chip] = [
            pltpu.make_async_copy(ref.at[:, pl.ds(first, kept)], x_here.at[chip, side], in_sems.at[chip, side])
            for side, ref in enumerate((x_ref, other_x_ref))
        ]
        for copy in coming[chip]:
            copy.start()
    going = []
    for chip in order:
        for copy in coming[chip]:
            copy.wait()
        term = dot_nn(turned_ref[...], x_here[chip, 0]) + dot_nn(other_turned_ref[...], x_here[chip, 1])
        here = sum_here if chip == 0 else low_here.at[chip]
        here[...] = term.astype(here.dtype)
        copy = pltpu.make_async_copy(here, out_refs[chip], out_sems.at[chip])
        copy.start()
        going.append(copy)
    for copy in going:
        copy.wait()


def weight_terms(turned, other_turned, inputs, other_inputs, n_ctx, name):
    cols, rows = turned.shape
    kept = inputs.shape[1] // n_ctx
    chips = n_ctx // 2
    vmem = pl.BlockSpec(memory_space=pltpu.VMEM)
    anywhere = pl.BlockSpec(memory_space=pl.ANY)
    return pl.pallas_call(
        partial(terms_kernel, chips),
        in_specs=[vmem, vmem, anywhere, anywhere],
        out_specs=(anywhere,) * chips,
        out_shape=tuple(
            jax.ShapeDtypeStruct((cols, kept), jnp.float32 if chip == 0 else jnp.bfloat16)
            for chip in range(chips)
        ),
        scratch_shapes=[
            pltpu.VMEM((chips, 2, rows, kept), jnp.bfloat16),
            pltpu.VMEM((cols, kept), jnp.float32),
            pltpu.VMEM((chips, cols, kept), jnp.bfloat16),
            pltpu.SemaphoreType.DMA((chips, 2)),
            pltpu.SemaphoreType.DMA((chips,)),
        ],
        compiler_params=pltpu.CompilerParams(vmem_limit_bytes=VMEM),
        cost_estimate=pl.CostEstimate(
            flops=4 * cols * rows * kept * chips, bytes_accessed=10 * MIB, transcendentals=0
        ),
        name=name,
    )(turned, other_turned, inputs, other_inputs)


def rows_kernel(n_in, *refs):
    in_refs, out_refs = refs[:n_in], refs[n_in:]
    total = in_refs[0][...]
    for in_ref in in_refs[1:]:
        total = total + in_ref[...].astype(jnp.float32)
    at = 0
    for out_ref in out_refs:
        cols = slice(at, at + out_ref.shape[1])
        at = cols.stop
        out_ref[...] = total[cols, :].T


def weight_rows(terms, widths, name):
    cols, kept = terms[0].shape
    return pl.pallas_call(
        partial(rows_kernel, len(terms)),
        grid=(1,),
        out_shape=tuple(jax.ShapeDtypeStruct((kept, width), jnp.float32) for width in widths),
        in_specs=[pl.BlockSpec((cols, kept), lambda i: (0, 0))] * len(terms),
        out_specs=tuple(pl.BlockSpec((kept, width), lambda i: (0, 0)) for width in widths),
        compiler_params=pltpu.CompilerParams(vmem_limit_bytes=VMEM),
        cost_estimate=pl.CostEstimate(flops=4 * MIB, bytes_accessed=6 * MIB, transcendentals=0),
        name=name,
    )(*terms)


def own_products_kernel(dq_ref, dkv_ref, query_ref, key_ref, value_ref, out_ref):
    k_cols = key_ref.shape[1]
    out_ref[...] = (
        dot_nt(dq_ref[...], query_ref[...])
        + dot_nt(dkv_ref[:, :k_cols], key_ref[...])
        + dot_nt(dkv_ref[:, k_cols:], value_ref[...])
    )


def own_products(dq, dkv, weights, out_width):
    rows = dq.shape[0]
    block = 512
    n_blocks = out_width // block

    def fixed(array):
        return pl.BlockSpec(array.shape, lambda i: (0, 0))

    return pl.pallas_call(
        own_products_kernel,
        grid=(n_blocks,),
        in_specs=[fixed(dq), fixed(dkv)]
        + [
            pl.BlockSpec((block, w.shape[1]), lambda i: (lax.axis_index("head") * n_blocks + i, 0))
            for w in weights
        ],
        out_specs=pl.BlockSpec((rows, block), lambda i: (0, i)),
        out_shape=jax.ShapeDtypeStruct((rows, out_width), jnp.float32),
        compiler_params=pltpu.CompilerParams(vmem_limit_bytes=VMEM),
        cost_estimate=pl.CostEstimate(
            flops=2 * rows * out_width * (dq.shape[1] + dkv.shape[1]), bytes_accessed=4 * MIB, transcendentals=0
        ),
        name="products_own",
    )(dq, dkv, *in_hbm(*weights))


def products_kernel(base_ref, *refs):
    count = len(refs) // 2
    left_refs, rows_refs, out_ref = refs[:count], refs[count:-1], refs[-1]
    total = base_ref[...]
    for left_ref, rows_ref in zip(left_refs, rows_refs):
        rows = rows_ref[...]
        total = total + dot_nt(left_ref[...], rows.reshape(-1, rows.shape[-1]))
    out_ref[...] = total.astype(out_ref.dtype)


def products(base, lefts, gathered, first, dtype, name):
    rows, out_width = base.shape
    n_head = len(lefts) + 1
    block = 512
    piece = gathered.shape[2]
    cols = lefts[0].shape[1]

    def left_spec(left, step):
        if left.shape[0] == rows:
            return pl.BlockSpec((rows, cols), lambda i: (0, 0))
        return pl.BlockSpec((rows, cols), lambda i: ((lax.axis_index("head") + n_head - step) % n_head, 0))

    def rows_spec(step):
        return pl.BlockSpec((block // piece, 1, piece, cols), lambda i: (i, step - 1, 0, first // cols))

    part = pl.BlockSpec((rows, block), lambda i: (0, i))
    return pl.pallas_call(
        products_kernel,
        grid=(out_width // block,),
        in_specs=[part]
        + [left_spec(left, step) for step, left in enumerate(lefts, 1)]
        + [rows_spec(step) for step in range(1, n_head)],
        out_specs=part,
        out_shape=jax.ShapeDtypeStruct((rows, out_width), dtype),
        compiler_params=pltpu.CompilerParams(vmem_limit_bytes=VMEM),
        cost_estimate=pl.CostEstimate(
            flops=2 * rows * out_width * cols * len(lefts), bytes_accessed=8 * MIB, transcendentals=0
        ),
        name=name,
    )(base, *lefts, *in_hbm(*[gathered] * len(lefts)))


def attention_kernel(
    first_ref, query_ref, grad_ref, kv0, kv1, kv2, kv3,
    out_ref, dq_ref, dq_t_ref, d0, d1, d2, d3,
    kv_ref, acc_ref, score_ref, sum_ref, sems,
):
    rows = query_ref.shape[0]
    copies = [
        pltpu.make_async_copy(block, kv_ref.at[pl.ds(slot * rows, rows), :], sems.at[slot])
        for slot, block in enumerate((kv3, kv2, kv1, kv0))
    ]
    for copy in copies:
        copy.start()
    acc_ref[...] = jnp.zeros_like(acc_ref)
    for copy in copies:
        copy.wait()
    factor = HD ** (-0.5)
    wide = GROUP * GRAIN
    streams = range(TILE // GRAIN)
    key_local = lax.broadcasted_iota(jnp.int32, (TILE, wide), 0)
    query_local = lax.broadcasted_iota(jnp.int32, (TILE, wide), 1) % GRAIN
    heads = [slice(h * HD, (h + 1) * HD) for h in range(GROUP)]

    def tile_rows(tile):
        return pl.ds(pl.multiple_of(tile * TILE, TILE), TILE)

    for pair in range(rows // TILE):
        places = [pl.ds(pair * TILE + g * GRAIN, GRAIN) for g in streams]
        query = [jnp.concatenate([query_ref[here, cols] for cols in heads], axis=0) for here in places]
        grad = [jnp.concatenate([grad_ref[here, cols] for cols in heads], axis=0) for here in places]
        first = [first_ref[pair * len(places) + g] for g in streams]
        last = (SPAN * rows) // TILE + pair
        low = first[0] // TILE
        sum_ref[...] = jnp.zeros_like(sum_ref)

        def score_tile(tile, carry, diagonal):
            here = tile_rows(tile)
            following = []
            for g in streams:
                top, total = carry[g]
                score = dot_nt(kv_ref[here, :HD], query[g]) * (factor * LOG2E)
                keep = key_local >= first[g] - tile * TILE
                if diagonal:
                    keep = keep & (key_local <= query_local + g * GRAIN)
                score = jnp.where(keep, score, NEG)
                score_ref[g, here, :] = score
                new_top = jnp.maximum(top, jnp.max(score, axis=0, keepdims=True))
                weight = jnp.sum(jnp.exp2(score - new_top), axis=0, keepdims=True)
                following.append((new_top, total * jnp.exp2(top - new_top) + weight))
            return tuple(following)

        state = tuple(
            (jnp.full((1, wide), NEG, jnp.float32), jnp.zeros((1, wide), jnp.float32)) for g in streams
        )
        state = lax.fori_loop(low, last, lambda tile, carry: score_tile(tile, carry, False), state)
        state = score_tile(last, state, True)
        lse = [top + jnp.log2(total) for top, total in state]

        def output_tile(tile, carry):
            here = tile_rows(tile)
            value_grad = acc_ref[here, HD:]
            for g in streams:
                prob = jnp.exp2(score_ref[g, here, :] - lse[g])
                score_ref[g, here, :] = prob
                prob = prob.astype(jnp.bfloat16)
                sum_ref[g] += dot_tn(kv_ref[here, HD:], prob)
                value_grad = value_grad + dot_nn(prob, grad[g])
            acc_ref[here, HD:] = value_grad
            return carry

        lax.fori_loop(low, last + 1, output_tile, 0)
        delta = []
        for g in streams:
            turned = sum_ref[g].astype(jnp.bfloat16).astype(jnp.float32)
            delta.append(
                jnp.sum(turned * grad[g].astype(jnp.float32).T, axis=0, keepdims=True)
            )
            out_rows = turned.T.astype(jnp.bfloat16)
            for head, cols in enumerate(heads):
                out_ref[places[g], cols] = out_rows[head * GRAIN : (head + 1) * GRAIN]
        sum_ref[...] = jnp.zeros_like(sum_ref)

        def gradient_tile(tile, carry):
            here = tile_rows(tile)
            key_grad = acc_ref[here, :HD]
            for g in streams:
                dprob = dot_nt(kv_ref[here, HD:], grad[g])
                dscore = (score_ref[g, here, :] * (dprob - delta[g])).astype(jnp.bfloat16)
                key_grad = key_grad + dot_nn(dscore, query[g])
                sum_ref[g] += dot_tn(kv_ref[here, :HD], dscore)
            acc_ref[here, :HD] = key_grad
            return carry

        lax.fori_loop(low, last + 1, gradient_tile, 0)
        for g in streams:
            turned = sum_ref[g] * factor
            dquery = turned.T.astype(jnp.bfloat16)
            for head, cols in enumerate(heads):
                part = slice(head * GRAIN, (head + 1) * GRAIN)
                dq_ref[places[g], cols] = dquery[part]
                dq_t_ref[cols, places[g]] = turned[:, part].astype(jnp.bfloat16)
    for slot, block in enumerate((d3, d2, d1, d0)):
        place = pl.ds(slot * rows, rows)
        block[:, :HD] = (acc_ref[place, :HD] * factor).astype(block.dtype)
        block[:, HD:] = acc_ref[place, HD:].astype(block.dtype)


def attention(first, query, grad, kv_list):
    rows, cols = query.shape
    window = (SPAN + 1) * rows
    low = jax.ShapeDtypeStruct((rows, cols), jnp.bfloat16)
    turned = jax.ShapeDtypeStruct((cols, rows), jnp.bfloat16)
    own = jax.ShapeDtypeStruct((rows, 2 * HD), jnp.float32)
    sent = jax.ShapeDtypeStruct((rows, 2 * HD), jnp.bfloat16)
    vmem = pl.BlockSpec(memory_space=pltpu.VMEM)
    anywhere = pl.BlockSpec(memory_space=pl.ANY)
    return pl.pallas_call(
        attention_kernel,
        out_shape=(low, low, turned, own) + (sent,) * SPAN,
        in_specs=[pl.BlockSpec(memory_space=pltpu.SMEM), vmem, vmem] + [anywhere] * (SPAN + 1),
        out_specs=(vmem,) * (SPAN + 4),
        scratch_shapes=[
            pltpu.VMEM((window, 2 * HD), jnp.bfloat16),
            pltpu.VMEM((window, 2 * HD), jnp.float32),
            pltpu.VMEM((TILE // GRAIN, window, GROUP * GRAIN), jnp.float32),
            pltpu.VMEM((TILE // GRAIN, HD, GROUP * GRAIN), jnp.float32),
            pltpu.SemaphoreType.DMA((SPAN + 1,)),
        ],
        compiler_params=pltpu.CompilerParams(vmem_limit_bytes=VMEM),
        cost_estimate=pl.CostEstimate(
            flops=6 * 2 * rows * window * cols, bytes_accessed=6 * MIB, transcendentals=0
        ),
        name="attention",
    )(first, query, grad, *kv_list)


def shift(value, axis, steps):
    count = lax.axis_size(axis)
    pairs = [(i, i + steps) for i in range(count) if 0 <= i + steps < count]
    return lax.ppermute(value, axis, pairs)


def swap(value, axis, mask):
    return lax.ppermute(value, axis, [(i, i ^ mask) for i in range(lax.axis_size(axis))])


def rotate(value, axis, steps):
    count = lax.axis_size(axis)
    return lax.ppermute(value, axis, [(i, (i + steps) % count) for i in range(count)])


def body(inputs, query_weight, key_weight, value_weight, out_grad, doc_lengths):
    tok_rows, width = inputs.shape
    n_ctx = lax.axis_size("ctx")
    n_head = lax.axis_size("head")
    chips = n_ctx // 2
    ctx = lax.axis_index("ctx")
    head = lax.axis_index("head")
    q_cols = query_weight.shape[1]
    k_cols = key_weight.shape[1]

    weights = (query_weight, key_weight, value_weight)
    out_width = width // n_head
    piece = out_width // n_ctx
    pieces = cut_rows(weights, n_head, piece)
    pieces, inputs = lax.optimization_barrier((pieces, inputs))
    pieces = [rotate(rows, "head", step) for step, rows in enumerate(pieces, 1)]

    kv_loc = project(inputs, (key_weight, value_weight), "project_kv")
    kv_list = [kv_loc] + [shift(kv_loc, "ctx", distance) for distance in range(1, SPAN + 1)]
    late_inputs, kv_loc = lax.optimization_barrier((inputs, kv_loc))
    query = project(late_inputs, (query_weight,), "project_query")
    query, kv_list, pieces, inputs = lax.optimization_barrier((query, kv_list, pieces, inputs))
    gathered = lax.all_gather(jnp.concatenate(pieces, axis=0), "ctx", axis=0, tiled=True)
    gathered = gathered.reshape(n_ctx, n_head - 1, piece, q_cols + 2 * k_cols)

    other_inputs = swap(inputs, "ctx", 1)

    granules = tok_rows // GRAIN
    window_start = (ctx - SPAN) * tok_rows
    positions = ctx * tok_rows + GRAIN * jnp.arange(granules, dtype=jnp.int32)
    doc_ends = jnp.cumsum(doc_lengths)
    starts = jnp.sum(
        jnp.where(doc_ends[None, :] <= positions[:, None], doc_lengths[None, :], 0), axis=1
    )
    attn_out, dq_low, dq_turned, own_grads, *sent_grads = attention(
        starts - window_start, query, out_grad, kv_list
    )

    dq_up = rotate(dq_low, "head", 1)
    back = [shift(sent_grads[distance - 1], "ctx", -distance) for distance in range(1, SPAN + 1)]
    back, dq_up, dq_low = lax.optimization_barrier((back, dq_up, dq_low))
    dq_down = rotate(dq_low, "head", -1)
    dkv_low, turned = combine(own_grads, back, dq_turned)
    dkv_all = lax.all_gather(dkv_low, "head", axis=0, tiled=True)

    other_turned = swap(turned, "ctx", 1)
    terms = weight_terms(turned, other_turned, inputs, other_inputs, n_ctx, "weight_terms")
    moved = [swap(term, "ctx", 2 * chip) for chip, term in enumerate(terms) if chip > 0]
    dq_far = rotate(dq_up, "head", 1)
    _, dq_low, dkv_low = lax.optimization_barrier((terms, dq_low, dkv_low))

    grad_sum = own_products(dq_low, dkv_low, weights, out_width)
    grad_sum, dq_far = lax.optimization_barrier((grad_sum, dq_far))
    grad_sum = products(grad_sum, (dq_up, dq_far, dq_down), gathered, 0, jnp.float32, "products_query")
    grad_sum, dkv_all = lax.optimization_barrier((grad_sum, dkv_all))
    input_grad = products(
        grad_sum, (dkv_all,) * (n_head - 1), gathered, q_cols, jnp.bfloat16, "products_key"
    )
    input_grad, moved = lax.optimization_barrier((input_grad, moved))
    weight_grads = weight_rows([terms[0], *moved], (q_cols, k_cols, k_cols), "weight_rows")
    return (attn_out, input_grad, *weight_grads)


def solution(mesh):
    return jax.shard_map(
        body,
        mesh=mesh,
        in_specs=(
            P("ctx", None),
            P(None, "head"),
            P(None, "head"),
            P(None, "head"),
            P("ctx", "head"),
            P(),
        ),
        out_specs=(P("ctx", "head"),) * 5,
        check_vma=False,
    )
```

```python
from functools import partial

import jax
import jax.numpy as jnp
from jax import lax
from jax.experimental import pallas as pl
from jax.experimental.pallas import tpu as pltpu
from jax.sharding import PartitionSpec as P

HD = 128
GROUP = 4
SPAN = 3
GRAIN = 128
TILE = 256
CHUNK = 512
MIB = 2**20

NEG = -1e30
LOG2E = 1.4426950408889634


def dot_nt(left_mat, right_mat):
    return lax.dot_general(
        left_mat, right_mat, (((1,), (1,)), ((), ())), preferred_element_type=jnp.float32
    )


def dot_tn(left_mat, right_mat):
    return lax.dot_general(
        left_mat, right_mat, (((0,), (0,)), ((), ())), preferred_element_type=jnp.float32
    )


def dot_nn(left_mat, right_mat):
    return jnp.dot(left_mat, right_mat, preferred_element_type=jnp.float32)


def in_hbm(*arrays):
    return [pltpu.with_memory_space_constraint(array, pltpu.HBM) for array in arrays]


def cut_kernel(*refs):
    weight_refs, piece_refs, sems = refs[:3], refs[3:-1], refs[-1]
    head, ctx = lax.axis_index("head"), lax.axis_index("ctx")
    n_head = len(piece_refs) + 1
    piece = piece_refs[0].shape[0]
    copies = []
    for distance, piece_ref in enumerate(piece_refs, 1):
        group = lax.rem(head + distance, n_head)
        first = group * (weight_refs[0].shape[0] // n_head) + ctx * piece
        at = 0
        for number, weight_ref in enumerate(weight_refs):
            cols = weight_ref.shape[1]
            copies.append(
                pltpu.make_async_copy(
                    weight_ref.at[pl.ds(pl.multiple_of(first, piece), piece), :],
                    piece_ref.at[:, pl.ds(at, cols)],
                    sems.at[distance - 1, number],
                )
            )
            at += cols
    for copy in copies:
        copy.start()
    for copy in copies:
        copy.wait()


def cut_rows(weights, n_head, piece):
    cols = sum(weight.shape[1] for weight in weights)
    anywhere = pl.BlockSpec(memory_space=pl.ANY)
    return pl.pallas_call(
        cut_kernel,
        out_shape=(jax.ShapeDtypeStruct((piece, cols), jnp.bfloat16),) * (n_head - 1),
        in_specs=[anywhere] * 3,
        out_specs=(pl.BlockSpec(memory_space=pltpu.VMEM),) * (n_head - 1),
        scratch_shapes=[pltpu.SemaphoreType.DMA((n_head - 1, 3))],
        cost_estimate=pl.CostEstimate(flops=0, bytes_accessed=2 * MIB, transcendentals=0),
        name="cut_rows",
    )(*in_hbm(*weights))


def project_kernel(x_ref, *refs):
    n = len(refs) - 4
    weight_refs, (out_ref, x_here, weight_here, sems) = refs[:n], refs[n:]
    rows = x_ref.shape[0]
    chunks = []
    for step in range(x_ref.shape[1] // CHUNK):
        part = pl.ds(step * CHUNK, CHUNK)
        copies = [pltpu.make_async_copy(x_ref.at[:, part], x_here.at[:, part], sems.at[step, 0])]
        at = 0
        for number, weight_ref in enumerate(weight_refs):
            cols = pl.ds(at, weight_ref.shape[1])
            at += weight_ref.shape[1]
            copies.append(
                pltpu.make_async_copy(
                    weight_ref.at[part, :], weight_here.at[part, cols], sems.at[step, 1 + number]
                )
            )
        for copy in copies:
            copy.start()
        chunks.append((part, copies))
    total = jnp.zeros((rows, weight_here.shape[1]), jnp.float32)
    for part, copies in chunks:
        for copy in copies:
            copy.wait()
        total = total + dot_nn(x_here[:, part], weight_here[part, :])
    out_ref[...] = total.astype(out_ref.dtype)


def project(inputs, weights, name):
    rows, width = inputs.shape
    cols = sum(weight.shape[1] for weight in weights)
    anywhere = pl.BlockSpec(memory_space=pl.ANY)
    return pl.pallas_call(
        project_kernel,
        in_specs=[anywhere] * (len(weights) + 1),
        out_specs=pl.BlockSpec(memory_space=pltpu.VMEM),
        out_shape=jax.ShapeDtypeStruct((rows, cols), jnp.bfloat16),
        scratch_shapes=[
            pltpu.VMEM((rows, width), jnp.bfloat16),
            pltpu.VMEM((width, cols), jnp.bfloat16),
            pltpu.SemaphoreType.DMA((width // CHUNK, len(weights) + 1)),
        ],
        compiler_params=pltpu.CompilerParams(vmem_limit_bytes=24 * MIB),
        cost_estimate=pl.CostEstimate(
            flops=2 * rows * width * cols, bytes_accessed=2 * width * (rows + cols), transcendentals=0
        ),
        name=name,
    )(*in_hbm(inputs, *weights))


def merge_kernel(d2_ref, bundle_ref, out_ref):
    rows, cols = out_ref.shape
    core = lax.axis_index("ctx") % 2
    here = pl.ds(bundle_ref.shape[0] - rows, rows)
    near, far = bundle_ref[here, :cols], bundle_ref[here, cols:]
    other = jnp.where(core == 1, near.astype(jnp.float32), far.astype(jnp.float32))
    out_ref[...] = (d2_ref[...].astype(jnp.float32) + other).astype(out_ref.dtype)


def combine_kernel(own_ref, merged_ref, far_ref, bundle_ref, low_ref, turned_ref):
    rows, cols = own_ref.shape
    core = lax.axis_index("ctx") % 2
    near = bundle_ref[bundle_ref.shape[0] - rows :, :cols].astype(jnp.float32)
    total = own_ref[...] + merged_ref[...].astype(jnp.float32) + far_ref[...].astype(jnp.float32)
    total = total + jnp.where(core == 0, near, 0.0)
    low_ref[...] = total.astype(jnp.bfloat16)
    turned_ref[...] = total.T.astype(jnp.bfloat16)


def small_kernel(kernel, shapes, name, *operands):
    def whole(shape):
        return pl.BlockSpec(shape, lambda i: (0, 0))

    return pl.pallas_call(
        kernel,
        grid=(1,),
        out_shape=tuple(jax.ShapeDtypeStruct(shape, dtype) for shape, dtype in shapes),
        in_specs=[whole(operand.shape) for operand in operands],
        out_specs=tuple(whole(shape) for shape, dtype in shapes),
        compiler_params=pltpu.CompilerParams(vmem_limit_bytes=20 * MIB),
        cost_estimate=pl.CostEstimate(flops=4 * MIB, bytes_accessed=4 * MIB, transcendentals=0),
        name=name,
    )(*operands)


def terms_kernel(chips, turned_ref, other_turned_ref, x_ref, other_x_ref, *refs):
    out_refs, (x_here, sum_here, low_here, in_sems, out_sems) = refs[:chips], refs[chips:]
    cols, kept = out_refs[0].shape
    ctx = lax.axis_index("ctx")
    order = [*range(1, chips), 0]
    coming = {}
    for chip in order:
        first = pl.multiple_of((((ctx // 2) ^ chip) * 2 + ctx % 2) * kept, kept)
        coming[chip] = [
            pltpu.make_async_copy(ref.at[:, pl.ds(first, kept)], x_here.at[chip, side], in_sems.at[chip, side])
            for side, ref in enumerate((x_ref, other_x_ref))
        ]
        for copy in coming[chip]:
            copy.start()
    going = []
    for chip in order:
        for copy in coming[chip]:
            copy.wait()
        term = dot_nn(turned_ref[:cols, :], x_here[chip, 0]) + dot_nn(other_turned_ref[:cols, :], x_here[chip, 1])
        here = sum_here if chip == 0 else low_here.at[chip]
        here[...] = term.astype(here.dtype)
        copy = pltpu.make_async_copy(here, out_refs[chip], out_sems.at[chip])
        copy.start()
        going.append(copy)
    for copy in going:
        copy.wait()


def weight_terms(turned, other_turned, cols, inputs, other_inputs, n_ctx, name):
    rows = turned.shape[1]
    kept = inputs.shape[1] // n_ctx
    chips = n_ctx // 2
    vmem = pl.BlockSpec(memory_space=pltpu.VMEM)
    anywhere = pl.BlockSpec(memory_space=pl.ANY)
    return pl.pallas_call(
        partial(terms_kernel, chips),
        in_specs=[vmem, vmem, anywhere, anywhere],
        out_specs=(anywhere,) * chips,
        out_shape=tuple(
            jax.ShapeDtypeStruct((cols, kept), jnp.float32 if chip == 0 else jnp.bfloat16)
            for chip in range(chips)
        ),
        scratch_shapes=[
            pltpu.VMEM((chips, 2, rows, kept), jnp.bfloat16),
            pltpu.VMEM((cols, kept), jnp.float32),
            pltpu.VMEM((chips, cols, kept), jnp.bfloat16),
            pltpu.SemaphoreType.DMA((chips, 2)),
            pltpu.SemaphoreType.DMA((chips,)),
        ],
        compiler_params=pltpu.CompilerParams(vmem_limit_bytes=24 * MIB),
        cost_estimate=pl.CostEstimate(
            flops=4 * cols * rows * kept * chips, bytes_accessed=10 * MIB, transcendentals=0
        ),
        name=name,
    )(turned, other_turned, inputs, other_inputs)


def rows_kernel(n_in, *refs):
    in_refs, out_refs = refs[:n_in], refs[n_in:]
    total = in_refs[0][...]
    for in_ref in in_refs[1:]:
        total = total + in_ref[...].astype(jnp.float32)
    at = 0
    for out_ref in out_refs:
        cols = slice(at, at + out_ref.shape[1])
        at = cols.stop
        out_ref[...] = total[cols, :].T


def weight_rows(terms, widths, name):
    kept = terms[0].shape[1]
    shapes = [((kept, width), jnp.float32) for width in widths]
    return small_kernel(partial(rows_kernel, len(terms)), shapes, name, *terms)


def products_kernel(count, has_base, *refs):
    left_refs, rows_refs, out_ref = refs[:count], refs[count : 2 * count], refs[-1]
    total = refs[2 * count][...] if has_base else None
    for left_ref, rows_ref in zip(left_refs, rows_refs):
        rows = rows_ref[...]
        term = dot_nt(left_ref[...], rows.reshape(-1, rows.shape[-1]))
        total = term if total is None else total + term
    out_ref[...] = total.astype(out_ref.dtype)


def products(pairs, base, out_width, n_head, dtype, name):
    rows = base.shape[0] if base is not None else pairs[0][0][0].shape[0]
    block = 512
    n_blocks = out_width // block
    left_specs, right_specs, lefts, rights = [], [], [], []
    flops = 0
    for (left, *place), right in pairs:
        lefts.append(left)
        if len(place) == 2:
            column, cols = place
            left_specs.append(pl.BlockSpec((rows, cols), partial(lambda column, i: (0, column), column)))
        else:
            cols = left.shape[1]
            left_specs.append(
                pl.BlockSpec(
                    (rows, cols),
                    partial(
                        lambda steps, i: ((lax.axis_index("head") + n_head - steps) % n_head, 0), place[0]
                    ),
                )
            )
        flops += 2 * rows * cols * out_width
        if isinstance(right, tuple):
            gathered, steps, first = right
            piece = gathered.shape[2]
            rights.append(gathered)
            right_specs.append(
                pl.BlockSpec(
                    (block // piece, 1, piece, cols),
                    partial(lambda step, at, i: (i, step, 0, at), steps - 1, first // cols),
                )
            )
        else:
            rights.append(right)
            right_specs.append(
                pl.BlockSpec((block, cols), lambda i: (lax.axis_index("head") * n_blocks + i, 0))
            )
    part = pl.BlockSpec((rows, block), lambda i: (0, i))
    extra = [] if base is None else [base]
    return pl.pallas_call(
        partial(products_kernel, len(pairs), base is not None),
        grid=(n_blocks,),
        in_specs=left_specs + right_specs + [part] * len(extra),
        out_specs=part,
        out_shape=jax.ShapeDtypeStruct((rows, out_width), dtype),
        compiler_params=pltpu.CompilerParams(vmem_limit_bytes=20 * MIB),
        cost_estimate=pl.CostEstimate(flops=flops, bytes_accessed=8 * MIB, transcendentals=0),
        name=name,
    )(*lefts, *in_hbm(*rights), *extra)


def attention_kernel(
    first_ref, query_ref, grad_ref, kv0, kv1, kv2, kv3,
    out_ref, dq_ref, bundle_ref, d0, d2, d3,
    kv_ref, acc_ref, score_ref, sum_ref, sems,
):
    rows = query_ref.shape[0]
    copies = [
        pltpu.make_async_copy(block, kv_ref.at[pl.ds(slot * rows, rows), :], sems.at[slot])
        for slot, block in enumerate((kv3, kv2, kv1, kv0))
    ]
    for copy in copies:
        copy.start()
    acc_ref[...] = jnp.zeros_like(acc_ref)
    for copy in copies:
        copy.wait()
    factor = HD ** (-0.5)
    wide = GROUP * GRAIN
    streams = range(TILE // GRAIN)
    key_local = lax.broadcasted_iota(jnp.int32, (TILE, wide), 0)
    query_local = lax.broadcasted_iota(jnp.int32, (TILE, wide), 1) % GRAIN
    heads = [slice(h * HD, (h + 1) * HD) for h in range(GROUP)]

    def tile_rows(tile):
        return pl.ds(pl.multiple_of(tile * TILE, TILE), TILE)

    for pair in range(rows // TILE):
        places = [pl.ds(pair * TILE + g * GRAIN, GRAIN) for g in streams]
        query = [jnp.concatenate([query_ref[here, cols] for cols in heads], axis=0) for here in places]
        grad = [jnp.concatenate([grad_ref[here, cols] for cols in heads], axis=0) for here in places]
        first = [first_ref[pair * len(places) + g] for g in streams]
        last = (SPAN * rows) // TILE + pair
        low = first[0] // TILE
        sum_ref[...] = jnp.zeros_like(sum_ref)

        def score_tile(tile, carry, diagonal):
            here = tile_rows(tile)
            following = []
            for g in streams:
                top, total = carry[g]
                score = dot_nt(kv_ref[here, :HD], query[g]) * (factor * LOG2E)
                keep = key_local >= first[g] - tile * TILE
                if diagonal:
                    keep = keep & (key_local <= query_local + g * GRAIN)
                score = jnp.where(keep, score, NEG)
                score_ref[g, here, :] = score
                new_top = jnp.maximum(top, jnp.max(score, axis=0, keepdims=True))
                weight = jnp.sum(jnp.exp2(score - new_top), axis=0, keepdims=True)
                following.append((new_top, total * jnp.exp2(top - new_top) + weight))
            return tuple(following)

        state = tuple(
            (jnp.full((1, wide), NEG, jnp.float32), jnp.zeros((1, wide), jnp.float32)) for g in streams
        )
        state = lax.fori_loop(low, last, lambda tile, carry: score_tile(tile, carry, False), state)
        state = score_tile(last, state, True)
        lse = [top + jnp.log2(total) for top, total in state]

        def output_tile(tile, carry):
            here = tile_rows(tile)
            value_grad = acc_ref[here, HD:]
            for g in streams:
                prob = jnp.exp2(score_ref[g, here, :] - lse[g])
                score_ref[g, here, :] = prob
                prob = prob.astype(jnp.bfloat16)
                sum_ref[g] += dot_tn(kv_ref[here, HD:], prob)
                value_grad = value_grad + dot_nn(prob, grad[g])
            acc_ref[here, HD:] = value_grad
            return carry

        lax.fori_loop(low, last + 1, output_tile, 0)
        delta = []
        for g in streams:
            turned = sum_ref[g].astype(jnp.bfloat16).astype(jnp.float32)
            delta.append(
                jnp.sum(turned * grad[g].astype(jnp.float32).T, axis=0, keepdims=True)
            )
            out_rows = turned.T.astype(jnp.bfloat16)
            for head, cols in enumerate(heads):
                out_ref[places[g], cols] = out_rows[head * GRAIN : (head + 1) * GRAIN]
        sum_ref[...] = jnp.zeros_like(sum_ref)

        def gradient_tile(tile, carry):
            here = tile_rows(tile)
            key_grad = acc_ref[here, :HD]
            for g in streams:
                dprob = dot_nt(kv_ref[here, HD:], grad[g])
                dscore = (score_ref[g, here, :] * (dprob - delta[g])).astype(jnp.bfloat16)
                key_grad = key_grad + dot_nn(dscore, query[g])
                sum_ref[g] += dot_tn(kv_ref[here, :HD], dscore)
            acc_ref[here, :HD] = key_grad
            return carry

        lax.fori_loop(low, last + 1, gradient_tile, 0)
        for g in streams:
            turned = sum_ref[g] * factor
            dquery = turned.T.astype(jnp.bfloat16)
            for head, cols in enumerate(heads):
                part = slice(head * GRAIN, (head + 1) * GRAIN)
                dq_ref[places[g], cols] = dquery[part]
                bundle_ref[cols, places[g]] = turned[:, part].astype(jnp.bfloat16)
    cols = query_ref.shape[1]
    for distance, blocks in enumerate(
        ((d0,), (bundle_ref.at[cols:, : 2 * HD],), (d2,), (d3, bundle_ref.at[cols:, 2 * HD :]))
    ):
        place = pl.ds((SPAN - distance) * rows, rows)
        key_grad, value_grad = acc_ref[place, :HD] * factor, acc_ref[place, HD:]
        for block in blocks:
            block[:, :HD] = key_grad.astype(block.dtype)
            block[:, HD:] = value_grad.astype(block.dtype)


def attention(first, query, grad, kv_list):
    rows, cols = query.shape
    window = (SPAN + 1) * rows
    low = jax.ShapeDtypeStruct((rows, cols), jnp.bfloat16)
    bundle = jax.ShapeDtypeStruct((cols + rows, rows), jnp.bfloat16)
    own = jax.ShapeDtypeStruct((rows, 2 * HD), jnp.float32)
    sent = jax.ShapeDtypeStruct((rows, 2 * HD), jnp.bfloat16)
    vmem = pl.BlockSpec(memory_space=pltpu.VMEM)
    anywhere = pl.BlockSpec(memory_space=pl.ANY)
    return pl.pallas_call(
        attention_kernel,
        out_shape=(low, low, bundle, own, sent, sent),
        in_specs=[pl.BlockSpec(memory_space=pltpu.SMEM), vmem, vmem] + [anywhere] * (SPAN + 1),
        out_specs=(vmem,) * 6,
        scratch_shapes=[
            pltpu.VMEM((window, 2 * HD), jnp.bfloat16),
            pltpu.VMEM((window, 2 * HD), jnp.float32),
            pltpu.VMEM((TILE // GRAIN, window, GROUP * GRAIN), jnp.float32),
            pltpu.VMEM((TILE // GRAIN, HD, GROUP * GRAIN), jnp.float32),
            pltpu.SemaphoreType.DMA((SPAN + 1,)),
        ],
        compiler_params=pltpu.CompilerParams(vmem_limit_bytes=24 * MIB),
        cost_estimate=pl.CostEstimate(
            flops=6 * 2 * rows * window * cols, bytes_accessed=6 * MIB, transcendentals=0
        ),
        name="attention",
    )(first, query, grad, *kv_list)


def shift(value, axis, steps):
    count = lax.axis_size(axis)
    pairs = [(i, i + steps) for i in range(count) if 0 <= i + steps < count]
    return lax.ppermute(value, axis, pairs)


def swap(value, axis, mask):
    return lax.ppermute(value, axis, [(i, i ^ mask) for i in range(lax.axis_size(axis))])


def rotate(value, axis, steps):
    count = lax.axis_size(axis)
    return lax.ppermute(value, axis, [(i, (i + steps) % count) for i in range(count)])


def body(inputs, query_weight, key_weight, value_weight, out_grad, doc_lengths):
    tok_rows, width = inputs.shape
    n_ctx = lax.axis_size("ctx")
    n_head = lax.axis_size("head")
    chips = n_ctx // 2
    ctx = lax.axis_index("ctx")
    head = lax.axis_index("head")
    q_cols = query_weight.shape[1]
    k_cols = key_weight.shape[1]

    weights = (query_weight, key_weight, value_weight)
    out_width = width // n_head
    piece = out_width // n_ctx
    pieces = cut_rows(weights, n_head, piece)
    pieces, inputs = lax.optimization_barrier((pieces, inputs))
    pieces = [rotate(rows, "head", step) for step, rows in enumerate(pieces, 1)]

    kv_loc = project(inputs, (key_weight, value_weight), "project_kv")
    kv_list = [kv_loc] + [shift(kv_loc, "ctx", distance) for distance in range(1, SPAN + 1)]
    late_inputs, kv_loc = lax.optimization_barrier((inputs, kv_loc))
    query = project(late_inputs, (query_weight,), "project_query")
    query, kv_list, pieces, inputs = lax.optimization_barrier((query, kv_list, pieces, inputs))
    gathered = lax.all_gather(jnp.concatenate(pieces, axis=0), "ctx", axis=0, tiled=True)
    gathered = gathered.reshape(n_ctx, n_head - 1, piece, q_cols + 2 * k_cols)

    other_inputs = swap(inputs, "ctx", 1)

    granules = tok_rows // GRAIN
    window_start = (ctx - SPAN) * tok_rows
    positions = ctx * tok_rows + GRAIN * jnp.arange(granules, dtype=jnp.int32)
    doc_ends = jnp.cumsum(doc_lengths)
    starts = jnp.sum(
        jnp.where(doc_ends[None, :] <= positions[:, None], doc_lengths[None, :], 0), axis=1
    )
    attn_out, dq_low, bundle, own_grads, mid_grads, far_grads = attention(
        starts - window_start, query, out_grad, kv_list
    )

    other_bundle = swap(bundle, "ctx", 1)
    dq_up = rotate(dq_low, "head", 1)
    dq_down = rotate(dq_low, "head", -1)
    far = lax.ppermute(
        far_grads, "ctx", [(source, source - SPAN) for source in range(0, n_ctx, 2) if source >= SPAN]
    )
    kv_shape = (tok_rows, 2 * k_cols)
    merged, = small_kernel(merge_kernel, [(kv_shape, jnp.bfloat16)], "merge", mid_grads, other_bundle)
    merged = shift(merged, "ctx", -2)

    q_terms = weight_terms(bundle, other_bundle, q_cols, inputs, other_inputs, n_ctx, "query_terms")
    q_moved = [swap(q_terms[chips - 1], "ctx", 2 * (chips - 1))]
    far, merged, dq_up, dq_down, dq_low, q_moved, q_terms = lax.optimization_barrier(
        (far, merged, dq_up, dq_down, dq_low, q_moved, q_terms)
    )
    dkv_low, dkv_turned = small_kernel(
        combine_kernel, [(kv_shape, jnp.bfloat16), (kv_shape[::-1], jnp.bfloat16)], "combine",
        own_grads, merged, far, other_bundle,
    )
    dkv_all = lax.all_gather(dkv_low, "head", axis=0, tiled=True)
    dq_far = rotate(dq_up, "head", 1)
    other_dkv = swap(dkv_turned, "ctx", 1)
    q_moved += [swap(q_terms[chip], "ctx", 2 * chip) for chip in range(1, chips - 1)]
    kv_terms = weight_terms(
        dkv_turned, other_dkv, 2 * k_cols, inputs, other_inputs, n_ctx, "key_terms"
    )
    kv_moved = [swap(term, "ctx", 2 * chip) for chip, term in enumerate(kv_terms) if chip > 0]
    _, dq_low, dq_up, dq_down = lax.optimization_barrier((kv_terms, dq_low, dq_up, dq_down))

    grad_sum = products(
        (
            ((dq_low, 0, q_cols), query_weight),
            ((dq_up, 0, q_cols), (gathered, 1, 0)),
            ((dq_down, 0, q_cols), (gathered, 3, 0)),
        ),
        None, out_width, n_head, jnp.float32, "products_near",
    )
    grad_sum, q_moved, kv_moved = lax.optimization_barrier((grad_sum, q_moved, kv_moved))
    q_grad, = weight_rows([q_terms[0], *q_moved], (q_cols,), "query_rows")
    k_grad, v_grad = weight_rows([kv_terms[0], *kv_moved], (k_cols, k_cols), "key_rows")
    q_grad, k_grad, v_grad, grad_sum = lax.optimization_barrier((q_grad, k_grad, v_grad, grad_sum))
    input_grad = products(
        (
            ((dq_far, 0, q_cols), (gathered, 2, 0)),
            ((dkv_low, 0, k_cols), key_weight),
            ((dkv_low, 1, k_cols), value_weight),
            *(((dkv_all, step), (gathered, step, q_cols)) for step in range(1, n_head)),
        ),
        grad_sum, out_width, n_head, jnp.bfloat16, "products_far",
    )
    return (attn_out, input_grad, q_grad, k_grad, v_grad)


def solution(mesh):
    return jax.shard_map(
        body,
        mesh=mesh,
        in_specs=(
            P("ctx", None),
            P(None, "head"),
            P(None, "head"),
            P(None, "head"),
            P("ctx", "head"),
            P(),
        ),
        out_specs=(P("ctx", "head"),) * 5,
        check_vma=False,
    )
```

```python
from functools import partial

import jax
import jax.numpy as jnp
from jax import lax
from jax.experimental import pallas as pl
from jax.experimental.pallas import tpu as pltpu
from jax.sharding import PartitionSpec as P

HD = 128
GROUP = 4
SPAN = 3
GRAIN = 128
TILE = 256
CHUNK = 512
MIB = 2**20

NEG = -1e30
LOG2E = 1.4426950408889634


def dot_nt(left_mat, right_mat):
    return lax.dot_general(
        left_mat, right_mat, (((1,), (1,)), ((), ())), preferred_element_type=jnp.float32
    )


def dot_tn(left_mat, right_mat):
    return lax.dot_general(
        left_mat, right_mat, (((0,), (0,)), ((), ())), preferred_element_type=jnp.float32
    )


def dot_nn(left_mat, right_mat):
    return jnp.dot(left_mat, right_mat, preferred_element_type=jnp.float32)


def in_hbm(*arrays):
    return [pltpu.with_memory_space_constraint(array, pltpu.HBM) for array in arrays]


def cut_kernel(*refs):
    weight_refs, piece_refs, sems = refs[:3], refs[3:-1], refs[-1]
    head, ctx = lax.axis_index("head"), lax.axis_index("ctx")
    n_head = len(piece_refs) + 1
    piece = piece_refs[0].shape[0]
    copies = []
    for distance, piece_ref in enumerate(piece_refs, 1):
        group = lax.rem(head + distance, n_head)
        first = group * (weight_refs[0].shape[0] // n_head) + ctx * piece
        at = 0
        for number, weight_ref in enumerate(weight_refs):
            cols = weight_ref.shape[1]
            copies.append(
                pltpu.make_async_copy(
                    weight_ref.at[pl.ds(pl.multiple_of(first, piece), piece), :],
                    piece_ref.at[:, pl.ds(at, cols)],
                    sems.at[distance - 1, number],
                )
            )
            at += cols
    for copy in copies:
        copy.start()
    for copy in copies:
        copy.wait()


def cut_rows(weights, n_head, piece):
    cols = sum(weight.shape[1] for weight in weights)
    anywhere = pl.BlockSpec(memory_space=pl.ANY)
    return pl.pallas_call(
        cut_kernel,
        out_shape=(jax.ShapeDtypeStruct((piece, cols), jnp.bfloat16),) * (n_head - 1),
        in_specs=[anywhere] * 3,
        out_specs=(pl.BlockSpec(memory_space=pltpu.VMEM),) * (n_head - 1),
        scratch_shapes=[pltpu.SemaphoreType.DMA((n_head - 1, 3))],
        cost_estimate=pl.CostEstimate(flops=0, bytes_accessed=2 * MIB, transcendentals=0),
        name="cut_rows",
    )(*in_hbm(*weights))


def project_kernel(x_ref, *refs):
    n = len(refs) - 4
    weight_refs, (out_ref, x_here, weight_here, sems) = refs[:n], refs[n:]
    rows = x_ref.shape[0]
    chunks = []
    for step in range(x_ref.shape[1] // CHUNK):
        part = pl.ds(step * CHUNK, CHUNK)
        copies = [pltpu.make_async_copy(x_ref.at[:, part], x_here.at[:, part], sems.at[step, 0])]
        at = 0
        for number, weight_ref in enumerate(weight_refs):
            cols = pl.ds(at, weight_ref.shape[1])
            at += weight_ref.shape[1]
            copies.append(
                pltpu.make_async_copy(
                    weight_ref.at[part, :], weight_here.at[part, cols], sems.at[step, 1 + number]
                )
            )
        for copy in copies:
            copy.start()
        chunks.append((part, copies))
    total = jnp.zeros((rows, weight_here.shape[1]), jnp.float32)
    for part, copies in chunks:
        for copy in copies:
            copy.wait()
        total = total + dot_nn(x_here[:, part], weight_here[part, :])
    out_ref[...] = total.astype(out_ref.dtype)


def project(inputs, weights, name):
    rows, width = inputs.shape
    cols = sum(weight.shape[1] for weight in weights)
    anywhere = pl.BlockSpec(memory_space=pl.ANY)
    return pl.pallas_call(
        project_kernel,
        in_specs=[anywhere] * (len(weights) + 1),
        out_specs=pl.BlockSpec(memory_space=pltpu.VMEM),
        out_shape=jax.ShapeDtypeStruct((rows, cols), jnp.bfloat16),
        scratch_shapes=[
            pltpu.VMEM((rows, width), jnp.bfloat16),
            pltpu.VMEM((width, cols), jnp.bfloat16),
            pltpu.SemaphoreType.DMA((width // CHUNK, len(weights) + 1)),
        ],
        compiler_params=pltpu.CompilerParams(vmem_limit_bytes=24 * MIB),
        cost_estimate=pl.CostEstimate(
            flops=2 * rows * width * cols, bytes_accessed=2 * width * (rows + cols), transcendentals=0
        ),
        name=name,
    )(*in_hbm(inputs, *weights))


def merge_kernel(d2_ref, bundle_ref, out_ref):
    rows, cols = out_ref.shape
    core = lax.axis_index("ctx") % 2
    here = pl.ds(bundle_ref.shape[0] - rows, rows)
    near, far = bundle_ref[here, :cols], bundle_ref[here, cols:]
    other = jnp.where(core == 1, near.astype(jnp.float32), far.astype(jnp.float32))
    out_ref[...] = (d2_ref[...].astype(jnp.float32) + other).astype(out_ref.dtype)


def combine_kernel(own_ref, merged_ref, far_ref, bundle_ref, low_ref, turned_ref):
    rows, cols = own_ref.shape
    core = lax.axis_index("ctx") % 2
    near = bundle_ref[bundle_ref.shape[0] - rows :, :cols].astype(jnp.float32)
    total = own_ref[...] + merged_ref[...].astype(jnp.float32) + far_ref[...].astype(jnp.float32)
    total = total + jnp.where(core == 0, near, 0.0)
    low_ref[...] = total.astype(jnp.bfloat16)
    turned_ref[...] = total.T.astype(jnp.bfloat16)


def small_kernel(kernel, shapes, name, *operands):
    def whole(shape):
        return pl.BlockSpec(shape, lambda i: (0, 0))

    return pl.pallas_call(
        kernel,
        grid=(1,),
        out_shape=tuple(jax.ShapeDtypeStruct(shape, dtype) for shape, dtype in shapes),
        in_specs=[whole(operand.shape) for operand in operands],
        out_specs=tuple(whole(shape) for shape, dtype in shapes),
        compiler_params=pltpu.CompilerParams(vmem_limit_bytes=20 * MIB),
        cost_estimate=pl.CostEstimate(flops=4 * MIB, bytes_accessed=4 * MIB, transcendentals=0),
        name=name,
    )(*operands)


def terms_kernel(chips, turned_ref, other_turned_ref, x_ref, other_x_ref, *refs):
    out_refs, (x_here, sum_here, low_here, in_sems, out_sems) = refs[:chips], refs[chips:]
    cols, kept = out_refs[0].shape
    ctx = lax.axis_index("ctx")
    order = [*range(1, chips), 0]
    coming = {}
    for chip in order:
        first = pl.multiple_of((((ctx // 2) ^ chip) * 2 + ctx % 2) * kept, kept)
        coming[chip] = [
            pltpu.make_async_copy(ref.at[:, pl.ds(first, kept)], x_here.at[chip, side], in_sems.at[chip, side])
            for side, ref in enumerate((x_ref, other_x_ref))
        ]
        for copy in coming[chip]:
            copy.start()
    going = []
    for chip in order:
        for copy in coming[chip]:
            copy.wait()
        term = dot_nn(turned_ref[:cols, :], x_here[chip, 0]) + dot_nn(other_turned_ref[:cols, :], x_here[chip, 1])
        here = sum_here if chip == 0 else low_here.at[chip]
        here[...] = term.astype(here.dtype)
        copy = pltpu.make_async_copy(here, out_refs[chip], out_sems.at[chip])
        copy.start()
        going.append(copy)
    for copy in going:
        copy.wait()


def weight_terms(turned, other_turned, cols, inputs, other_inputs, n_ctx, name):
    rows = turned.shape[1]
    kept = inputs.shape[1] // n_ctx
    chips = n_ctx // 2
    vmem = pl.BlockSpec(memory_space=pltpu.VMEM)
    anywhere = pl.BlockSpec(memory_space=pl.ANY)
    return pl.pallas_call(
        partial(terms_kernel, chips),
        in_specs=[vmem, vmem, anywhere, anywhere],
        out_specs=(anywhere,) * chips,
        out_shape=tuple(
            jax.ShapeDtypeStruct((cols, kept), jnp.float32 if chip == 0 else jnp.bfloat16)
            for chip in range(chips)
        ),
        scratch_shapes=[
            pltpu.VMEM((chips, 2, rows, kept), jnp.bfloat16),
            pltpu.VMEM((cols, kept), jnp.float32),
            pltpu.VMEM((chips, cols, kept), jnp.bfloat16),
            pltpu.SemaphoreType.DMA((chips, 2)),
            pltpu.SemaphoreType.DMA((chips,)),
        ],
        compiler_params=pltpu.CompilerParams(vmem_limit_bytes=24 * MIB),
        cost_estimate=pl.CostEstimate(
            flops=4 * cols * rows * kept * chips, bytes_accessed=10 * MIB, transcendentals=0
        ),
        name=name,
    )(turned, other_turned, *in_hbm(inputs), other_inputs)


def rows_kernel(n_in, *refs):
    in_refs, out_refs = refs[:n_in], refs[n_in:]
    total = in_refs[0][...]
    for in_ref in in_refs[1:]:
        total += in_ref[...].astype(jnp.float32)
    at = 0
    for out_ref in out_refs:
        cols = slice(at, at + out_ref.shape[1])
        at = cols.stop
        out_ref[...] = total[cols, :].T


def weight_rows(terms, widths, name):
    kept = terms[0].shape[1]
    shapes = [((kept, width), jnp.float32) for width in widths]
    return small_kernel(partial(rows_kernel, len(terms)), shapes, name, *terms)


def products_kernel(count, has_base, *refs):
    left_refs, rows_refs, out_ref = refs[:count], refs[count : 2 * count], refs[-1]
    total = refs[2 * count][...] if has_base else None
    for left_ref, rows_ref in zip(left_refs, rows_refs):
        rows = rows_ref[...]
        term = dot_nt(left_ref[...], rows.reshape(-1, rows.shape[-1]))
        total = term if total is None else total + term
    out_ref[...] = total.astype(out_ref.dtype)


def products(pairs, base, out_width, n_head, dtype, name):
    rows = base.shape[0] if base is not None else pairs[0][0][0].shape[0]
    block = 512
    n_blocks = out_width // block
    left_specs, right_specs, lefts, rights = [], [], [], []
    flops = 0
    for (left, *place), right in pairs:
        lefts.append(left)
        if len(place) == 2:
            column, cols = place
            left_specs.append(pl.BlockSpec((rows, cols), partial(lambda column, i: (0, column), column)))
        else:
            cols = left.shape[1]
            left_specs.append(
                pl.BlockSpec(
                    (rows, cols),
                    partial(
                        lambda steps, i: ((lax.axis_index("head") + n_head - steps) % n_head, 0), place[0]
                    ),
                )
            )
        flops += 2 * rows * cols * out_width
        if isinstance(right, tuple):
            lefts[-1:] = in_hbm(left)
            gathered, steps, first = right
            piece = gathered.shape[2]
            rights.append(gathered)
            right_specs.append(
                pl.BlockSpec(
                    (block // piece, 1, piece, cols),
                    partial(lambda step, at, i: (i, step, 0, at), steps - 1, first // cols),
                )
            )
        else:
            rights.append(right)
            right_specs.append(
                pl.BlockSpec((block, cols), lambda i: (lax.axis_index("head") * n_blocks + i, 0))
            )
    part = pl.BlockSpec((rows, block), lambda i: (0, i))
    extra = [] if base is None else [base]
    return pl.pallas_call(
        partial(products_kernel, len(pairs), base is not None),
        grid=(n_blocks,),
        in_specs=left_specs + right_specs + [part] * len(extra),
        out_specs=part,
        out_shape=jax.ShapeDtypeStruct((rows, out_width), dtype),
        compiler_params=pltpu.CompilerParams(vmem_limit_bytes=20 * MIB),
        cost_estimate=pl.CostEstimate(flops=flops, bytes_accessed=8 * MIB, transcendentals=0),
        name=name,
    )(*lefts, *in_hbm(*rights), *extra)


def attention_kernel(
    first_ref, query_ref, grad_ref, kv0, kv1, kv2, kv3,
    out_ref, dq_ref, bundle_ref, d0, d2, d3,
    kv_ref, acc_ref, score_ref, sum_ref, sems,
):
    rows = query_ref.shape[0]
    copies = [
        pltpu.make_async_copy(block, kv_ref.at[pl.ds(slot * rows, rows), :], sems.at[slot])
        for slot, block in enumerate((kv3, kv2, kv1, kv0))
    ]
    for copy in copies:
        copy.start()
    acc_ref[...] = jnp.zeros_like(acc_ref)
    for copy in copies:
        copy.wait()
    factor = HD ** (-0.5)
    wide = GROUP * GRAIN
    streams = range(TILE // GRAIN)
    key_local = lax.broadcasted_iota(jnp.int32, (TILE, wide), 0)
    query_local = lax.broadcasted_iota(jnp.int32, (TILE, wide), 1) % GRAIN
    heads = [slice(h * HD, (h + 1) * HD) for h in range(GROUP)]

    def tile_rows(tile):
        return pl.ds(pl.multiple_of(tile * TILE, TILE), TILE)

    for pair in range(rows // TILE):
        places = [pl.ds(pair * TILE + g * GRAIN, GRAIN) for g in streams]
        query = [jnp.concatenate([query_ref[here, cols] for cols in heads], axis=0) for here in places]
        grad = [jnp.concatenate([grad_ref[here, cols] for cols in heads], axis=0) for here in places]
        first = [first_ref[pair * len(places) + g] for g in streams]
        last = (SPAN * rows) // TILE + pair
        low = first[0] // TILE
        sum_ref[...] = jnp.zeros_like(sum_ref)

        def score_tile(tile, carry, diagonal):
            here = tile_rows(tile)
            following = []
            for g in streams:
                top, total = carry[g]
                score = dot_nt(kv_ref[here, :HD], query[g]) * (factor * LOG2E)
                keep = key_local >= first[g] - tile * TILE
                if diagonal:
                    keep = keep & (key_local <= query_local + g * GRAIN)
                score = jnp.where(keep, score, NEG)
                score_ref[g, here, :] = score
                new_top = jnp.maximum(top, jnp.max(score, axis=0, keepdims=True))
                weight = jnp.sum(jnp.exp2(score - new_top), axis=0, keepdims=True)
                following.append((new_top, total * jnp.exp2(top - new_top) + weight))
            return tuple(following)

        state = tuple(
            (jnp.full((1, wide), NEG, jnp.float32), jnp.zeros((1, wide), jnp.float32)) for g in streams
        )
        state = lax.fori_loop(low, last, lambda tile, carry: score_tile(tile, carry, False), state)
        state = score_tile(last, state, True)
        lse = [top + jnp.log2(total) for top, total in state]

        def output_tile(tile, carry):
            here = tile_rows(tile)
            value_grad = acc_ref[here, HD:]
            for g in streams:
                prob = jnp.exp2(score_ref[g, here, :] - lse[g])
                score_ref[g, here, :] = prob
                prob = prob.astype(jnp.bfloat16)
                sum_ref[g] += dot_tn(kv_ref[here, HD:], prob)
                value_grad = value_grad + dot_nn(prob, grad[g])
            acc_ref[here, HD:] = value_grad
            return carry

        lax.fori_loop(low, last + 1, output_tile, 0)
        delta = []
        for g in streams:
            turned = sum_ref[g].astype(jnp.bfloat16).astype(jnp.float32)
            delta.append(
                jnp.sum(turned * grad[g].astype(jnp.float32).T, axis=0, keepdims=True)
            )
            out_rows = turned.T.astype(jnp.bfloat16)
            for head, cols in enumerate(heads):
                out_ref[places[g], cols] = out_rows[head * GRAIN : (head + 1) * GRAIN]
        sum_ref[...] = jnp.zeros_like(sum_ref)

        def gradient_tile(tile, carry):
            here = tile_rows(tile)
            key_grad = acc_ref[here, :HD]
            for g in streams:
                dprob = dot_nt(kv_ref[here, HD:], grad[g])
                dscore = (score_ref[g, here, :] * (dprob - delta[g])).astype(jnp.bfloat16)
                key_grad = key_grad + dot_nn(dscore, query[g])
                sum_ref[g] += dot_tn(kv_ref[here, :HD], dscore)
            acc_ref[here, :HD] = key_grad
            return carry

        lax.fori_loop(low, last + 1, gradient_tile, 0)
        for g in streams:
            turned = sum_ref[g] * factor
            dquery = turned.T.astype(jnp.bfloat16)
            for head, cols in enumerate(heads):
                part = slice(head * GRAIN, (head + 1) * GRAIN)
                dq_ref[places[g], cols] = dquery[part]
                bundle_ref[cols, places[g]] = turned[:, part].astype(jnp.bfloat16)
    cols = query_ref.shape[1]
    for distance, blocks in enumerate(
        ((d0,), (bundle_ref.at[cols:, : 2 * HD],), (d2,), (d3, bundle_ref.at[cols:, 2 * HD :]))
    ):
        place = pl.ds((SPAN - distance) * rows, rows)
        key_grad, value_grad = acc_ref[place, :HD] * factor, acc_ref[place, HD:]
        for block in blocks:
            block[:, :HD] = key_grad.astype(block.dtype)
            block[:, HD:] = value_grad.astype(block.dtype)


def attention(first, query, grad, kv_list):
    rows, cols = query.shape
    window = (SPAN + 1) * rows
    low = jax.ShapeDtypeStruct((rows, cols), jnp.bfloat16)
    bundle = jax.ShapeDtypeStruct((cols + rows, rows), jnp.bfloat16)
    own = jax.ShapeDtypeStruct((rows, 2 * HD), jnp.float32)
    sent = jax.ShapeDtypeStruct((rows, 2 * HD), jnp.bfloat16)
    vmem = pl.BlockSpec(memory_space=pltpu.VMEM)
    anywhere = pl.BlockSpec(memory_space=pl.ANY)
    return pl.pallas_call(
        attention_kernel,
        out_shape=(low, low, bundle, own, sent, sent),
        in_specs=[pl.BlockSpec(memory_space=pltpu.SMEM), vmem, vmem] + [anywhere] * (SPAN + 1),
        out_specs=(vmem,) * 6,
        scratch_shapes=[
            pltpu.VMEM((window, 2 * HD), jnp.bfloat16),
            pltpu.VMEM((window, 2 * HD), jnp.float32),
            pltpu.VMEM((TILE // GRAIN, window, GROUP * GRAIN), jnp.float32),
            pltpu.VMEM((TILE // GRAIN, HD, GROUP * GRAIN), jnp.float32),
            pltpu.SemaphoreType.DMA((SPAN + 1,)),
        ],
        compiler_params=pltpu.CompilerParams(vmem_limit_bytes=24 * MIB),
        cost_estimate=pl.CostEstimate(
            flops=6 * 2 * rows * window * cols, bytes_accessed=6 * MIB, transcendentals=0
        ),
        name="attention",
    )(first, query, grad, *kv_list)


def shift(value, axis, steps):
    count = lax.axis_size(axis)
    pairs = [(i, i + steps) for i in range(count) if 0 <= i + steps < count]
    return lax.ppermute(value, axis, pairs)


def swap(value, axis, mask):
    return lax.ppermute(value, axis, [(i, i ^ mask) for i in range(lax.axis_size(axis))])


def rotate(value, axis, steps):
    count = lax.axis_size(axis)
    return lax.ppermute(value, axis, [(i, (i + steps) % count) for i in range(count)])


def body(inputs, query_weight, key_weight, value_weight, out_grad, doc_lengths):
    tok_rows, width = inputs.shape
    n_ctx = lax.axis_size("ctx")
    n_head = lax.axis_size("head")
    chips = n_ctx // 2
    ctx = lax.axis_index("ctx")
    head = lax.axis_index("head")
    q_cols = query_weight.shape[1]
    k_cols = key_weight.shape[1]

    weights = (query_weight, key_weight, value_weight)
    out_width = width // n_head
    piece = out_width // n_ctx
    pieces = cut_rows(weights, n_head, piece)
    pieces, inputs = lax.optimization_barrier((pieces, inputs))
    pieces = [rotate(rows, "head", step) for step, rows in enumerate(pieces, 1)]

    kv_loc = project(inputs, (key_weight, value_weight), "project_kv")
    kv_list = [kv_loc] + [shift(kv_loc, "ctx", distance) for distance in range(1, SPAN + 1)]
    other_inputs = swap(inputs, "ctx", 1)
    late_inputs, other_inputs, kv_loc = lax.optimization_barrier((inputs, other_inputs, kv_loc))
    query = project(late_inputs, (query_weight,), "project_query")
    query, kv_list, pieces = lax.optimization_barrier((query, kv_list, pieces))
    gathered = lax.all_gather(jnp.concatenate(pieces, axis=0), "ctx", axis=0, tiled=True)
    gathered = gathered.reshape(n_ctx, n_head - 1, piece, q_cols + 2 * k_cols)

    granules = tok_rows // GRAIN
    window_start = (ctx - SPAN) * tok_rows
    positions = ctx * tok_rows + GRAIN * jnp.arange(granules, dtype=jnp.int32)
    doc_ends = jnp.cumsum(doc_lengths)
    starts = jnp.sum(
        jnp.where(doc_ends[None, :] <= positions[:, None], doc_lengths[None, :], 0), axis=1
    )
    attn_out, dq_low, bundle, own_grads, mid_grads, far_grads = attention(
        starts - window_start, query, out_grad, kv_list
    )

    other_bundle = swap(bundle, "ctx", 1)
    dq_up = rotate(dq_low, "head", 1)
    dq_down = rotate(dq_low, "head", -1)
    far = lax.ppermute(
        far_grads, "ctx", [(source, source - SPAN) for source in range(0, n_ctx, 2) if source >= SPAN]
    )
    kv_shape = (tok_rows, 2 * k_cols)
    merged, = small_kernel(merge_kernel, [(kv_shape, jnp.bfloat16)], "merge", mid_grads, other_bundle)
    merged, late_bundle = lax.optimization_barrier((merged, other_bundle))
    merged = shift(merged, "ctx", -2)

    q_terms = weight_terms(bundle, late_bundle, q_cols, inputs, other_inputs, n_ctx, "query_terms")
    q_moved = [swap(q_terms[chips - 1], "ctx", 2 * (chips - 1))]
    dq_far = rotate(dq_up, "head", 1)
    far, merged, dq_up, dq_down, dq_low, q_terms = lax.optimization_barrier(
        (far, merged, dq_up, dq_down, dq_low, q_terms)
    )
    dkv_low, dkv_turned = small_kernel(
        combine_kernel, [(kv_shape, jnp.bfloat16), (kv_shape[::-1], jnp.bfloat16)], "combine",
        own_grads, merged, far, other_bundle,
    )
    dkv_all = lax.all_gather(dkv_low, "head", axis=0, tiled=True)
    other_dkv = swap(dkv_turned, "ctx", 1)
    other_dkv, q_moved = lax.optimization_barrier((other_dkv, q_moved))
    q_moved += [swap(q_terms[chip], "ctx", 2 * chip) for chip in range(1, chips - 1)]
    kv_terms = weight_terms(
        dkv_turned, other_dkv, 2 * k_cols, inputs, other_inputs, n_ctx, "key_terms"
    )
    kv_moved = [swap(term, "ctx", 2 * chip) for chip, term in enumerate(kv_terms) if chip > 0]
    _, dq_low, dq_up, dq_down = lax.optimization_barrier((kv_terms, dq_low, dq_up, dq_down))

    grad_sum = products(
        (
            ((dq_low, 0, q_cols), query_weight),
            ((dq_up, 0, q_cols), (gathered, 1, 0)),
            ((dq_down, 0, q_cols), (gathered, 3, 0)),
        ),
        None, out_width, n_head, jnp.float32, "products_near",
    )
    grad_sum, q_moved, kv_moved = lax.optimization_barrier((grad_sum, q_moved, kv_moved))
    q_grad, = weight_rows([q_terms[0], *q_moved], (q_cols,), "query_rows")
    k_grad, v_grad = weight_rows([kv_terms[0], *kv_moved], (k_cols, k_cols), "key_rows")
    q_grad, k_grad, v_grad, grad_sum = lax.optimization_barrier((q_grad, k_grad, v_grad, grad_sum))
    input_grad = products(
        (
            ((dq_far, 0, q_cols), (gathered, 2, 0)),
            ((dkv_low, 0, k_cols), key_weight),
            ((dkv_low, 1, k_cols), value_weight),
            *(((dkv_all, step), (gathered, step, q_cols)) for step in range(1, n_head)),
        ),
        grad_sum, out_width, n_head, jnp.bfloat16, "products_far",
    )
    return (attn_out, input_grad, q_grad, k_grad, v_grad)


def solution(mesh):
    return jax.shard_map(
        body,
        mesh=mesh,
        in_specs=(
            P("ctx", None),
            P(None, "head"),
            P(None, "head"),
            P(None, "head"),
            P("ctx", "head"),
            P(),
        ),
        out_specs=(P("ctx", "head"),) * 5,
        check_vma=False,
    )
```

```python
from functools import partial

import jax
import jax.numpy as jnp
from jax import lax
from jax.experimental import pallas as pl
from jax.experimental.pallas import tpu as pltpu
from jax.sharding import PartitionSpec as P

HD = 128
GROUP = 4
SPAN = 3
GRAIN = 128
TILE = 256
CHUNK = 512
MIB = 2**20

NEG = -1e30
LOG2E = 1.4426950408889634


def dot_nt(left_mat, right_mat):
    return lax.dot_general(
        left_mat, right_mat, (((1,), (1,)), ((), ())), preferred_element_type=jnp.float32
    )


def dot_tn(left_mat, right_mat):
    return lax.dot_general(
        left_mat, right_mat, (((0,), (0,)), ((), ())), preferred_element_type=jnp.float32
    )


def dot_nn(left_mat, right_mat):
    return jnp.dot(left_mat, right_mat, preferred_element_type=jnp.float32)


def in_hbm(*arrays):
    return [pltpu.with_memory_space_constraint(array, pltpu.HBM) for array in arrays]


def cut_kernel(*refs):
    weight_refs, piece_refs, sems = refs[:3], refs[3:-1], refs[-1]
    head, ctx = lax.axis_index("head"), lax.axis_index("ctx")
    n_head = len(piece_refs) + 1
    piece = piece_refs[0].shape[0]
    copies = []
    for distance, piece_ref in enumerate(piece_refs, 1):
        group = lax.rem(head + distance, n_head)
        first = group * (weight_refs[0].shape[0] // n_head) + ctx * piece
        at = 0
        for number, weight_ref in enumerate(weight_refs):
            cols = weight_ref.shape[1]
            copies.append(
                pltpu.make_async_copy(
                    weight_ref.at[pl.ds(pl.multiple_of(first, piece), piece), :],
                    piece_ref.at[:, pl.ds(at, cols)],
                    sems.at[distance - 1, number],
                )
            )
            at += cols
    for copy in copies:
        copy.start()
    for copy in copies:
        copy.wait()


def cut_rows(weights, n_head, piece):
    cols = sum(weight.shape[1] for weight in weights)
    anywhere = pl.BlockSpec(memory_space=pl.ANY)
    return pl.pallas_call(
        cut_kernel,
        out_shape=(jax.ShapeDtypeStruct((piece, cols), jnp.bfloat16),) * (n_head - 1),
        in_specs=[anywhere] * 3,
        out_specs=(pl.BlockSpec(memory_space=pltpu.VMEM),) * (n_head - 1),
        scratch_shapes=[pltpu.SemaphoreType.DMA((n_head - 1, 3))],
        cost_estimate=pl.CostEstimate(flops=0, bytes_accessed=2 * MIB, transcendentals=0),
        name="cut_rows",
    )(*in_hbm(*weights))


def project_kernel(x_ref, *refs):
    n = len(refs) - 4
    weight_refs, (out_ref, x_here, weight_here, sems) = refs[:n], refs[n:]
    rows = x_ref.shape[0]
    chunks = []
    for step in range(x_ref.shape[1] // CHUNK):
        part = pl.ds(step * CHUNK, CHUNK)
        copies = [pltpu.make_async_copy(x_ref.at[:, part], x_here.at[:, part], sems.at[step, 0])]
        at = 0
        for number, weight_ref in enumerate(weight_refs):
            cols = pl.ds(at, weight_ref.shape[1])
            at += weight_ref.shape[1]
            copies.append(
                pltpu.make_async_copy(
                    weight_ref.at[part, :], weight_here.at[part, cols], sems.at[step, 1 + number]
                )
            )
        for copy in copies:
            copy.start()
        chunks.append((part, copies))
    total = jnp.zeros((rows, weight_here.shape[1]), jnp.float32)
    for part, copies in chunks:
        for copy in copies:
            copy.wait()
        total = total + dot_nn(x_here[:, part], weight_here[part, :])
    out_ref[...] = total.astype(out_ref.dtype)


def project(inputs, weights, name):
    rows, width = inputs.shape
    cols = sum(weight.shape[1] for weight in weights)
    anywhere = pl.BlockSpec(memory_space=pl.ANY)
    return pl.pallas_call(
        project_kernel,
        in_specs=[anywhere] * (len(weights) + 1),
        out_specs=pl.BlockSpec(memory_space=pltpu.VMEM),
        out_shape=jax.ShapeDtypeStruct((rows, cols), jnp.bfloat16),
        scratch_shapes=[
            pltpu.VMEM((rows, width), jnp.bfloat16),
            pltpu.VMEM((width, cols), jnp.bfloat16),
            pltpu.SemaphoreType.DMA((width // CHUNK, len(weights) + 1)),
        ],
        compiler_params=pltpu.CompilerParams(vmem_limit_bytes=24 * MIB),
        cost_estimate=pl.CostEstimate(
            flops=2 * rows * width * cols, bytes_accessed=2 * width * (rows + cols), transcendentals=0
        ),
        name=name,
    )(*in_hbm(inputs, *weights))


def merge_kernel(d2_ref, bundle_ref, out_ref):
    rows, cols = out_ref.shape
    core = lax.axis_index("ctx") % 2
    here = pl.ds(bundle_ref.shape[0] - rows, rows)
    near, far = bundle_ref[here, :cols], bundle_ref[here, cols:]
    other = jnp.where(core == 1, near.astype(jnp.float32), far.astype(jnp.float32))
    out_ref[...] = (d2_ref[...].astype(jnp.float32) + other).astype(out_ref.dtype)


def combine_kernel(own_ref, merged_ref, far_ref, bundle_ref, low_ref, turned_ref):
    rows, cols = own_ref.shape
    core = lax.axis_index("ctx") % 2
    near = bundle_ref[bundle_ref.shape[0] - rows :, :cols].astype(jnp.float32)
    total = own_ref[...] + merged_ref[...].astype(jnp.float32) + far_ref[...].astype(jnp.float32)
    total = total + jnp.where(core == 0, near, 0.0)
    low_ref[...] = total.astype(jnp.bfloat16)
    turned_ref[...] = total.T.astype(jnp.bfloat16)


def small_kernel(kernel, shapes, name, *operands):
    def whole(shape):
        return pl.BlockSpec(shape, lambda i: (0, 0))

    return pl.pallas_call(
        kernel,
        grid=(1,),
        out_shape=tuple(jax.ShapeDtypeStruct(shape, dtype) for shape, dtype in shapes),
        in_specs=[whole(operand.shape) for operand in operands],
        out_specs=tuple(whole(shape) for shape, dtype in shapes),
        compiler_params=pltpu.CompilerParams(vmem_limit_bytes=20 * MIB),
        cost_estimate=pl.CostEstimate(flops=4 * MIB, bytes_accessed=4 * MIB, transcendentals=0),
        name=name,
    )(*operands)


def terms_kernel(chips, turned_ref, other_turned_ref, x_ref, other_x_ref, *refs):
    out_refs, (x_here, sum_here, low_here, in_sems, out_sems) = refs[:chips], refs[chips:]
    cols, kept = out_refs[0].shape
    ctx = lax.axis_index("ctx")
    order = [*range(1, chips), 0]
    coming = {}
    for chip in order:
        first = pl.multiple_of((((ctx // 2) ^ chip) * 2 + ctx % 2) * kept, kept)
        coming[chip] = [
            pltpu.make_async_copy(ref.at[:, pl.ds(first, kept)], x_here.at[chip, side], in_sems.at[chip, side])
            for side, ref in enumerate((x_ref, other_x_ref))
        ]
        for copy in coming[chip]:
            copy.start()
    going = []
    for chip in order:
        for copy in coming[chip]:
            copy.wait()
        term = dot_nn(turned_ref[:cols, :], x_here[chip, 0]) + dot_nn(other_turned_ref[:cols, :], x_here[chip, 1])
        here = sum_here if chip == 0 else low_here.at[chip]
        here[...] = term.astype(here.dtype)
        copy = pltpu.make_async_copy(here, out_refs[chip], out_sems.at[chip])
        copy.start()
        going.append(copy)
    for copy in going:
        copy.wait()


def weight_terms(turned, other_turned, cols, inputs, other_inputs, n_ctx, name):
    rows = turned.shape[1]
    kept = inputs.shape[1] // n_ctx
    chips = n_ctx // 2
    vmem = pl.BlockSpec(memory_space=pltpu.VMEM)
    anywhere = pl.BlockSpec(memory_space=pl.ANY)
    return pl.pallas_call(
        partial(terms_kernel, chips),
        in_specs=[vmem, vmem, anywhere, anywhere],
        out_specs=(anywhere,) * chips,
        out_shape=tuple(
            jax.ShapeDtypeStruct((cols, kept), jnp.float32 if chip == 0 else jnp.bfloat16)
            for chip in range(chips)
        ),
        scratch_shapes=[
            pltpu.VMEM((chips, 2, rows, kept), jnp.bfloat16),
            pltpu.VMEM((cols, kept), jnp.float32),
            pltpu.VMEM((chips, cols, kept), jnp.bfloat16),
            pltpu.SemaphoreType.DMA((chips, 2)),
            pltpu.SemaphoreType.DMA((chips,)),
        ],
        compiler_params=pltpu.CompilerParams(vmem_limit_bytes=24 * MIB),
        cost_estimate=pl.CostEstimate(
            flops=4 * cols * rows * kept * chips, bytes_accessed=10 * MIB, transcendentals=0
        ),
        name=name,
    )(turned, other_turned, *in_hbm(inputs, other_inputs))


def rows_kernel(n_in, *refs):
    in_refs, out_refs = refs[:n_in], refs[n_in:]
    total = in_refs[0][...]
    for in_ref in in_refs[1:]:
        total += in_ref[...].astype(jnp.float32)
    at = 0
    for out_ref in out_refs:
        cols = slice(at, at + out_ref.shape[1])
        at = cols.stop
        out_ref[...] = total[cols, :].T


def weight_rows(terms, widths, name):
    kept = terms[0].shape[1]
    shapes = [((kept, width), jnp.float32) for width in widths]
    return small_kernel(partial(rows_kernel, len(terms)), shapes, name, *terms)


def products_kernel(count, has_base, *refs):
    left_refs, rows_refs, out_ref = refs[:count], refs[count : 2 * count], refs[-1]
    total = refs[2 * count][...] if has_base else None
    for left_ref, rows_ref in zip(left_refs, rows_refs):
        rows = rows_ref[...]
        term = dot_nt(left_ref[...], rows.reshape(-1, rows.shape[-1]))
        total = term if total is None else total + term
    out_ref[...] = total.astype(out_ref.dtype)


def products(pairs, base, out_width, n_head, dtype, name):
    rows = base.shape[0] if base is not None else pairs[0][0][0].shape[0]
    block = 512
    n_blocks = out_width // block
    left_specs, right_specs, lefts, rights = [], [], [], []
    flops = 0
    for (left, *place), right in pairs:
        lefts.append(left)
        if len(place) == 2:
            column, cols = place
            left_specs.append(pl.BlockSpec((rows, cols), partial(lambda column, i: (0, column), column)))
        else:
            cols = left.shape[1]
            left_specs.append(
                pl.BlockSpec(
                    (rows, cols),
                    partial(
                        lambda steps, i: ((lax.axis_index("head") + n_head - steps) % n_head, 0), place[0]
                    ),
                )
            )
        flops += 2 * rows * cols * out_width
        if isinstance(right, tuple):
            lefts[-1:] = in_hbm(left)
            gathered, steps, first = right
            piece = gathered.shape[2]
            rights.append(gathered)
            right_specs.append(
                pl.BlockSpec(
                    (block // piece, 1, piece, cols),
                    partial(lambda step, at, i: (i, step, 0, at), steps - 1, first // cols),
                )
            )
        else:
            rights.append(right)
            right_specs.append(
                pl.BlockSpec((block, cols), lambda i: (lax.axis_index("head") * n_blocks + i, 0))
            )
    part = pl.BlockSpec((rows, block), lambda i: (0, i))
    extra = [] if base is None else [base]
    return pl.pallas_call(
        partial(products_kernel, len(pairs), base is not None),
        grid=(n_blocks,),
        in_specs=left_specs + right_specs + [part] * len(extra),
        out_specs=part,
        out_shape=jax.ShapeDtypeStruct((rows, out_width), dtype),
        compiler_params=pltpu.CompilerParams(vmem_limit_bytes=20 * MIB),
        cost_estimate=pl.CostEstimate(flops=flops, bytes_accessed=8 * MIB, transcendentals=0),
        name=name,
    )(*lefts, *in_hbm(*rights), *extra)


def attention_kernel(
    first_ref, query_ref, grad_ref, kv0, kv1, kv2, kv3,
    out_ref, dq_ref, bundle_ref, d0, d2, d3,
    kv_ref, acc_ref, score_ref, sum_ref, sems,
):
    rows = query_ref.shape[0]
    copies = [
        pltpu.make_async_copy(block, kv_ref.at[pl.ds(slot * rows, rows), :], sems.at[slot])
        for slot, block in enumerate((kv3, kv2, kv1, kv0))
    ]
    for copy in copies:
        copy.start()
    acc_ref[...] = jnp.zeros_like(acc_ref)
    for copy in copies:
        copy.wait()
    factor = HD ** (-0.5)
    wide = GROUP * GRAIN
    streams = range(TILE // GRAIN)
    key_local = lax.broadcasted_iota(jnp.int32, (TILE, wide), 0)
    query_local = lax.broadcasted_iota(jnp.int32, (TILE, wide), 1) % GRAIN
    heads = [slice(h * HD, (h + 1) * HD) for h in range(GROUP)]

    def tile_rows(tile):
        return pl.ds(pl.multiple_of(tile * TILE, TILE), TILE)

    for pair in range(rows // TILE):
        places = [pl.ds(pair * TILE + g * GRAIN, GRAIN) for g in streams]
        query = [jnp.concatenate([query_ref[here, cols] for cols in heads], axis=0) for here in places]
        grad = [jnp.concatenate([grad_ref[here, cols] for cols in heads], axis=0) for here in places]
        first = [first_ref[pair * len(places) + g] for g in streams]
        last = (SPAN * rows) // TILE + pair
        low = first[0] // TILE
        sum_ref[...] = jnp.zeros_like(sum_ref)

        def score_tile(tile, carry, diagonal):
            here = tile_rows(tile)
            following = []
            for g in streams:
                top, total = carry[g]
                score = dot_nt(kv_ref[here, :HD], query[g]) * (factor * LOG2E)
                keep = key_local >= first[g] - tile * TILE
                if diagonal:
                    keep = keep & (key_local <= query_local + g * GRAIN)
                score = jnp.where(keep, score, NEG)
                score_ref[g, here, :] = score
                new_top = jnp.maximum(top, jnp.max(score, axis=0, keepdims=True))
                weight = jnp.sum(jnp.exp2(score - new_top), axis=0, keepdims=True)
                following.append((new_top, total * jnp.exp2(top - new_top) + weight))
            return tuple(following)

        state = tuple(
            (jnp.full((1, wide), NEG, jnp.float32), jnp.zeros((1, wide), jnp.float32)) for g in streams
        )
        state = lax.fori_loop(low, last, lambda tile, carry: score_tile(tile, carry, False), state)
        state = score_tile(last, state, True)
        lse = [top + jnp.log2(total) for top, total in state]

        def output_tile(tile, carry):
            here = tile_rows(tile)
            value_grad = acc_ref[here, HD:]
            for g in streams:
                prob = jnp.exp2(score_ref[g, here, :] - lse[g])
                score_ref[g, here, :] = prob
                prob = prob.astype(jnp.bfloat16)
                sum_ref[g] += dot_tn(kv_ref[here, HD:], prob)
                value_grad = value_grad + dot_nn(prob, grad[g])
            acc_ref[here, HD:] = value_grad
            return carry

        lax.fori_loop(low, last + 1, output_tile, 0)
        delta = []
        for g in streams:
            turned = sum_ref[g].astype(jnp.bfloat16).astype(jnp.float32)
            delta.append(
                jnp.sum(turned * grad[g].astype(jnp.float32).T, axis=0, keepdims=True)
            )
            out_rows = turned.T.astype(jnp.bfloat16)
            for head, cols in enumerate(heads):
                out_ref[places[g], cols] = out_rows[head * GRAIN : (head + 1) * GRAIN]
        sum_ref[...] = jnp.zeros_like(sum_ref)

        def gradient_tile(tile, carry):
            here = tile_rows(tile)
            key_grad = acc_ref[here, :HD]
            for g in streams:
                dprob = dot_nt(kv_ref[here, HD:], grad[g])
                dscore = (score_ref[g, here, :] * (dprob - delta[g])).astype(jnp.bfloat16)
                key_grad = key_grad + dot_nn(dscore, query[g])
                sum_ref[g] += dot_tn(kv_ref[here, :HD], dscore)
            acc_ref[here, :HD] = key_grad
            return carry

        lax.fori_loop(low, last + 1, gradient_tile, 0)
        for g in streams:
            turned = sum_ref[g] * factor
            dquery = turned.T.astype(jnp.bfloat16)
            for head, cols in enumerate(heads):
                part = slice(head * GRAIN, (head + 1) * GRAIN)
                dq_ref[places[g], cols] = dquery[part]
                bundle_ref[cols, places[g]] = turned[:, part].astype(jnp.bfloat16)
    cols = query_ref.shape[1]
    for distance, blocks in enumerate(
        ((d0,), (bundle_ref.at[cols:, : 2 * HD],), (d2,), (d3, bundle_ref.at[cols:, 2 * HD :]))
    ):
        place = pl.ds((SPAN - distance) * rows, rows)
        key_grad, value_grad = acc_ref[place, :HD] * factor, acc_ref[place, HD:]
        for block in blocks:
            block[:, :HD] = key_grad.astype(block.dtype)
            block[:, HD:] = value_grad.astype(block.dtype)


def attention(first, query, grad, kv_list):
    rows, cols = query.shape
    window = (SPAN + 1) * rows
    low = jax.ShapeDtypeStruct((rows, cols), jnp.bfloat16)
    bundle = jax.ShapeDtypeStruct((cols + rows, rows), jnp.bfloat16)
    own = jax.ShapeDtypeStruct((rows, 2 * HD), jnp.float32)
    sent = jax.ShapeDtypeStruct((rows, 2 * HD), jnp.bfloat16)
    vmem = pl.BlockSpec(memory_space=pltpu.VMEM)
    anywhere = pl.BlockSpec(memory_space=pl.ANY)
    return pl.pallas_call(
        attention_kernel,
        out_shape=(low, low, bundle, own, sent, sent),
        in_specs=[pl.BlockSpec(memory_space=pltpu.SMEM), vmem, vmem] + [anywhere] * (SPAN + 1),
        out_specs=(vmem,) * 6,
        scratch_shapes=[
            pltpu.VMEM((window, 2 * HD), jnp.bfloat16),
            pltpu.VMEM((window, 2 * HD), jnp.float32),
            pltpu.VMEM((TILE // GRAIN, window, GROUP * GRAIN), jnp.float32),
            pltpu.VMEM((TILE // GRAIN, HD, GROUP * GRAIN), jnp.float32),
            pltpu.SemaphoreType.DMA((SPAN + 1,)),
        ],
        compiler_params=pltpu.CompilerParams(vmem_limit_bytes=24 * MIB),
        cost_estimate=pl.CostEstimate(
            flops=6 * 2 * rows * window * cols, bytes_accessed=6 * MIB, transcendentals=0
        ),
        name="attention",
    )(first, query, grad, *kv_list)


def shift(value, axis, steps):
    count = lax.axis_size(axis)
    pairs = [(i, i + steps) for i in range(count) if 0 <= i + steps < count]
    return lax.ppermute(value, axis, pairs)


def swap(value, axis, mask):
    return lax.ppermute(value, axis, [(i, i ^ mask) for i in range(lax.axis_size(axis))])


def rotate(value, axis, steps):
    count = lax.axis_size(axis)
    return lax.ppermute(value, axis, [(i, (i + steps) % count) for i in range(count)])


def body(inputs, query_weight, key_weight, value_weight, out_grad, doc_lengths):
    tok_rows, width = inputs.shape
    n_ctx = lax.axis_size("ctx")
    n_head = lax.axis_size("head")
    chips = n_ctx // 2
    ctx = lax.axis_index("ctx")
    head = lax.axis_index("head")
    q_cols = query_weight.shape[1]
    k_cols = key_weight.shape[1]

    weights = (query_weight, key_weight, value_weight)
    out_width = width // n_head
    piece = out_width // n_ctx
    pieces = cut_rows(weights, n_head, piece)
    pieces, inputs = lax.optimization_barrier((pieces, inputs))
    pieces = [rotate(rows, "head", step) for step, rows in enumerate(pieces, 1)]

    kv_loc = project(inputs, (key_weight, value_weight), "project_kv")
    kv_list = [kv_loc] + [shift(kv_loc, "ctx", distance) for distance in range(1, SPAN + 1)]
    other_inputs = swap(inputs, "ctx", 1)
    late_inputs, other_inputs, kv_loc = lax.optimization_barrier((inputs, other_inputs, kv_loc))
    query = project(late_inputs, (query_weight,), "project_query")
    query, kv_list, pieces = lax.optimization_barrier((query, kv_list, pieces))
    gathered = lax.all_gather(jnp.concatenate(pieces, axis=0), "ctx", axis=0, tiled=True)
    gathered = gathered.reshape(n_ctx, n_head - 1, piece, q_cols + 2 * k_cols)

    granules = tok_rows // GRAIN
    window_start = (ctx - SPAN) * tok_rows
    positions = ctx * tok_rows + GRAIN * jnp.arange(granules, dtype=jnp.int32)
    doc_ends = jnp.cumsum(doc_lengths)
    starts = jnp.sum(
        jnp.where(doc_ends[None, :] <= positions[:, None], doc_lengths[None, :], 0), axis=1
    )
    attn_out, dq_low, bundle, own_grads, mid_grads, far_grads = attention(
        starts - window_start, query, out_grad, kv_list
    )

    other_bundle = swap(bundle, "ctx", 1)
    dq_up = rotate(dq_low, "head", 1)
    dq_down = rotate(dq_low, "head", -1)
    far = lax.ppermute(
        far_grads, "ctx", [(source, source - SPAN) for source in range(0, n_ctx, 2) if source >= SPAN]
    )
    kv_shape = (tok_rows, 2 * k_cols)
    merged, = small_kernel(merge_kernel, [(kv_shape, jnp.bfloat16)], "merge", mid_grads, other_bundle)
    merged, late_bundle = lax.optimization_barrier((merged, other_bundle))
    merged = shift(merged, "ctx", -2)

    q_terms = weight_terms(bundle, late_bundle, q_cols, inputs, other_inputs, n_ctx, "query_terms")
    q_moved = [swap(q_terms[chips - 1], "ctx", 2 * (chips - 1))]
    dq_far = rotate(dq_up, "head", 1)
    far, merged, dq_up, dq_down, dq_low, q_terms = lax.optimization_barrier(
        (far, merged, dq_up, dq_down, dq_low, q_terms)
    )
    dkv_low, dkv_turned = small_kernel(
        combine_kernel, [(kv_shape, jnp.bfloat16), (kv_shape[::-1], jnp.bfloat16)], "combine",
        own_grads, merged, far, other_bundle,
    )
    dkv_all = lax.all_gather(dkv_low, "head", axis=0, tiled=True)
    other_dkv = swap(dkv_turned, "ctx", 1)
    q_moved += [swap(q_terms[chip], "ctx", 2 * chip) for chip in range(1, chips - 1)]
    kv_terms = weight_terms(
        dkv_turned, other_dkv, 2 * k_cols, inputs, other_inputs, n_ctx, "key_terms"
    )
    kv_moved = [swap(term, "ctx", 2 * chip) for chip, term in enumerate(kv_terms) if chip > 0]
    _, dq_low, dq_up, dq_down, dkv_low = lax.optimization_barrier((kv_terms, dq_low, dq_up, dq_down, dkv_low))

    grad_sum = products(
        (
            ((dq_low, 0, q_cols), query_weight),
            ((dq_up, 0, q_cols), (gathered, 1, 0)),
            ((dq_down, 0, q_cols), (gathered, 3, 0)),
            ((dkv_low, 0, k_cols), key_weight),
            ((dkv_low, 1, k_cols), value_weight),
        ),
        None, out_width, n_head, jnp.float32, "products_near",
    )
    grad_sum, q_moved, kv_moved = lax.optimization_barrier((grad_sum, q_moved, kv_moved))
    q_grad, = weight_rows([q_terms[0], *q_moved], (q_cols,), "query_rows")
    k_grad, v_grad = weight_rows([kv_terms[0], *kv_moved], (k_cols, k_cols), "key_rows")
    q_grad, k_grad, v_grad, grad_sum = lax.optimization_barrier((q_grad, k_grad, v_grad, grad_sum))
    input_grad = products(
        (
            ((dq_far, 0, q_cols), (gathered, 2, 0)),
            *(((dkv_all, step), (gathered, step, q_cols)) for step in range(1, n_head)),
        ),
        grad_sum, out_width, n_head, jnp.bfloat16, "products_far",
    )
    return (attn_out, input_grad, q_grad, k_grad, v_grad)


def solution(mesh):
    return jax.shard_map(
        body,
        mesh=mesh,
        in_specs=(
            P("ctx", None),
            P(None, "head"),
            P(None, "head"),
            P(None, "head"),
            P("ctx", "head"),
            P(),
        ),
        out_specs=(P("ctx", "head"),) * 5,
        check_vma=False,
    )
```

```python
from functools import partial

import jax
import jax.numpy as jnp
from jax import lax
from jax.experimental import pallas as pl
from jax.experimental.pallas import tpu as pltpu
from jax.sharding import PartitionSpec as P

HD = 128
GROUP = 4
SPAN = 3
GRAIN = 128
TILE = 256
CHUNK = 512
MIB = 2**20

NEG = -1e30
LOG2E = 1.4426950408889634


def dot_nt(left_mat, right_mat):
    return lax.dot_general(
        left_mat, right_mat, (((1,), (1,)), ((), ())), preferred_element_type=jnp.float32
    )


def dot_tn(left_mat, right_mat):
    return lax.dot_general(
        left_mat, right_mat, (((0,), (0,)), ((), ())), preferred_element_type=jnp.float32
    )


def dot_nn(left_mat, right_mat):
    return jnp.dot(left_mat, right_mat, preferred_element_type=jnp.float32)


def in_hbm(*arrays):
    return [pltpu.with_memory_space_constraint(array, pltpu.HBM) for array in arrays]


def cut_kernel(*refs):
    weight_refs, piece_refs, sems = refs[:3], refs[3:-1], refs[-1]
    head, ctx = lax.axis_index("head"), lax.axis_index("ctx")
    n_head = len(piece_refs) + 1
    piece = piece_refs[0].shape[0]
    copies = []
    for distance, piece_ref in enumerate(piece_refs, 1):
        group = lax.rem(head + distance, n_head)
        first = group * (weight_refs[0].shape[0] // n_head) + ctx * piece
        at = 0
        for number, weight_ref in enumerate(weight_refs):
            cols = weight_ref.shape[1]
            copies.append(
                pltpu.make_async_copy(
                    weight_ref.at[pl.ds(pl.multiple_of(first, piece), piece), :],
                    piece_ref.at[:, pl.ds(at, cols)],
                    sems.at[distance - 1, number],
                )
            )
            at += cols
    for copy in copies:
        copy.start()
    for copy in copies:
        copy.wait()


def cut_rows(weights, n_head, piece):
    cols = sum(weight.shape[1] for weight in weights)
    anywhere = pl.BlockSpec(memory_space=pl.ANY)
    return pl.pallas_call(
        cut_kernel,
        out_shape=(jax.ShapeDtypeStruct((piece, cols), jnp.bfloat16),) * (n_head - 1),
        in_specs=[anywhere] * 3,
        out_specs=(pl.BlockSpec(memory_space=pltpu.VMEM),) * (n_head - 1),
        scratch_shapes=[pltpu.SemaphoreType.DMA((n_head - 1, 3))],
        cost_estimate=pl.CostEstimate(flops=0, bytes_accessed=2 * MIB, transcendentals=0),
        name="cut_rows",
    )(*in_hbm(*weights))


def project_kernel(x_ref, *refs):
    n = len(refs) - 4
    weight_refs, (out_ref, x_here, weight_here, sems) = refs[:n], refs[n:]
    rows = x_ref.shape[0]
    chunks = []
    for step in range(x_ref.shape[1] // CHUNK):
        part = pl.ds(step * CHUNK, CHUNK)
        copies = [pltpu.make_async_copy(x_ref.at[:, part], x_here.at[:, part], sems.at[step, 0])]
        at = 0
        for number, weight_ref in enumerate(weight_refs):
            cols = pl.ds(at, weight_ref.shape[1])
            at += weight_ref.shape[1]
            copies.append(
                pltpu.make_async_copy(
                    weight_ref.at[part, :], weight_here.at[part, cols], sems.at[step, 1 + number]
                )
            )
        for copy in copies:
            copy.start()
        chunks.append((part, copies))
    total = jnp.zeros((rows, weight_here.shape[1]), jnp.float32)
    for part, copies in chunks:
        for copy in copies:
            copy.wait()
        total = total + dot_nn(x_here[:, part], weight_here[part, :])
    out_ref[...] = total.astype(out_ref.dtype)


def project(inputs, weights, name):
    rows, width = inputs.shape
    cols = sum(weight.shape[1] for weight in weights)
    anywhere = pl.BlockSpec(memory_space=pl.ANY)
    return pl.pallas_call(
        project_kernel,
        in_specs=[anywhere] * (len(weights) + 1),
        out_specs=pl.BlockSpec(memory_space=pltpu.VMEM),
        out_shape=jax.ShapeDtypeStruct((rows, cols), jnp.bfloat16),
        scratch_shapes=[
            pltpu.VMEM((rows, width), jnp.bfloat16),
            pltpu.VMEM((width, cols), jnp.bfloat16),
            pltpu.SemaphoreType.DMA((width // CHUNK, len(weights) + 1)),
        ],
        compiler_params=pltpu.CompilerParams(vmem_limit_bytes=24 * MIB),
        cost_estimate=pl.CostEstimate(
            flops=2 * rows * width * cols, bytes_accessed=2 * width * (rows + cols), transcendentals=0
        ),
        name=name,
    )(*in_hbm(inputs, *weights))


def merge_kernel(d2_ref, bundle_ref, out_ref):
    rows, cols = out_ref.shape
    core = lax.axis_index("ctx") % 2
    here = pl.ds(bundle_ref.shape[0] - rows, rows)
    near, far = bundle_ref[here, :cols], bundle_ref[here, cols:]
    other = jnp.where(core == 1, near.astype(jnp.float32), far.astype(jnp.float32))
    out_ref[...] = (d2_ref[...].astype(jnp.float32) + other).astype(out_ref.dtype)


def combine_kernel(own_ref, merged_ref, far_ref, bundle_ref, low_ref, turned_ref):
    rows, cols = own_ref.shape
    core = lax.axis_index("ctx") % 2
    near = bundle_ref[bundle_ref.shape[0] - rows :, :cols].astype(jnp.float32)
    total = own_ref[...] + merged_ref[...].astype(jnp.float32) + far_ref[...].astype(jnp.float32)
    total = total + jnp.where(core == 0, near, 0.0)
    low_ref[...] = total.astype(jnp.bfloat16)
    turned_ref[...] = total.T.astype(jnp.bfloat16)


def small_kernel(kernel, shapes, name, *operands):
    def whole(shape):
        return pl.BlockSpec(shape, lambda i: (0, 0))

    return pl.pallas_call(
        kernel,
        grid=(1,),
        out_shape=tuple(jax.ShapeDtypeStruct(shape, dtype) for shape, dtype in shapes),
        in_specs=[whole(operand.shape) for operand in operands],
        out_specs=tuple(whole(shape) for shape, dtype in shapes),
        compiler_params=pltpu.CompilerParams(vmem_limit_bytes=20 * MIB),
        cost_estimate=pl.CostEstimate(flops=4 * MIB, bytes_accessed=4 * MIB, transcendentals=0),
        name=name,
    )(*operands)


def terms_kernel(chips, turned_ref, other_turned_ref, x_ref, other_x_ref, *refs):
    out_refs, (x_here, sum_here, low_here, in_sems, out_sems) = refs[:chips], refs[chips:]
    cols, kept = out_refs[0].shape
    ctx = lax.axis_index("ctx")
    order = [*range(1, chips), 0]
    coming = {}
    for chip in order:
        first = pl.multiple_of((((ctx // 2) ^ chip) * 2 + ctx % 2) * kept, kept)
        coming[chip] = [
            pltpu.make_async_copy(ref.at[:, pl.ds(first, kept)], x_here.at[chip, side], in_sems.at[chip, side])
            for side, ref in enumerate((x_ref, other_x_ref))
        ]
        for copy in coming[chip]:
            copy.start()
    going = []
    for chip in order:
        for copy in coming[chip]:
            copy.wait()
        term = dot_nn(turned_ref[:cols, :], x_here[chip, 0]) + dot_nn(other_turned_ref[:cols, :], x_here[chip, 1])
        here = sum_here if chip == 0 else low_here.at[chip]
        here[...] = term.astype(here.dtype)
        copy = pltpu.make_async_copy(here, out_refs[chip], out_sems.at[chip])
        copy.start()
        going.append(copy)
    for copy in going:
        copy.wait()


def weight_terms(turned, other_turned, cols, inputs, other_inputs, n_ctx, name):
    rows = turned.shape[1]
    kept = inputs.shape[1] // n_ctx
    chips = n_ctx // 2
    vmem = pl.BlockSpec(memory_space=pltpu.VMEM)
    anywhere = pl.BlockSpec(memory_space=pl.ANY)
    return pl.pallas_call(
        partial(terms_kernel, chips),
        in_specs=[vmem, vmem, anywhere, anywhere],
        out_specs=(anywhere,) * chips,
        out_shape=tuple(
            jax.ShapeDtypeStruct((cols, kept), jnp.float32 if chip == 0 else jnp.bfloat16)
            for chip in range(chips)
        ),
        scratch_shapes=[
            pltpu.VMEM((chips, 2, rows, kept), jnp.bfloat16),
            pltpu.VMEM((cols, kept), jnp.float32),
            pltpu.VMEM((chips, cols, kept), jnp.bfloat16),
            pltpu.SemaphoreType.DMA((chips, 2)),
            pltpu.SemaphoreType.DMA((chips,)),
        ],
        compiler_params=pltpu.CompilerParams(vmem_limit_bytes=24 * MIB),
        cost_estimate=pl.CostEstimate(
            flops=4 * cols * rows * kept * chips, bytes_accessed=10 * MIB, transcendentals=0
        ),
        name=name,
    )(turned, other_turned, *in_hbm(inputs, other_inputs))


def rows_kernel(n_in, *refs):
    in_refs, out_refs = refs[:n_in], refs[n_in:]
    total = in_refs[0][...]
    for in_ref in in_refs[1:]:
        total += in_ref[...].astype(jnp.float32)
    at = 0
    for out_ref in out_refs:
        cols = slice(at, at + out_ref.shape[1])
        at = cols.stop
        out_ref[...] = total[cols, :].T


def weight_rows(terms, widths, name):
    kept = terms[0].shape[1]
    shapes = [((kept, width), jnp.float32) for width in widths]
    return small_kernel(partial(rows_kernel, len(terms)), shapes, name, *terms)


def products_kernel(count, has_base, *refs):
    left_refs, rows_refs, out_ref = refs[:count], refs[count : 2 * count], refs[-1]
    total = refs[2 * count][...] if has_base else None
    for left_ref, rows_ref in zip(left_refs, rows_refs):
        rows = rows_ref[...]
        term = dot_nt(left_ref[...], rows.reshape(-1, rows.shape[-1]))
        total = term if total is None else total + term
    out_ref[...] = total.astype(out_ref.dtype)


def products(pairs, base, out_width, n_head, dtype, name):
    rows = base.shape[0] if base is not None else pairs[0][0][0].shape[0]
    block = 512
    n_blocks = out_width // block
    left_specs, right_specs, lefts, rights = [], [], [], []
    flops = 0
    for (left, *place), right in pairs:
        lefts.append(left)
        if len(place) == 2:
            column, cols = place
            left_specs.append(pl.BlockSpec((rows, cols), partial(lambda column, i: (0, column), column)))
        else:
            cols = left.shape[1]
            left_specs.append(
                pl.BlockSpec(
                    (rows, cols),
                    partial(
                        lambda steps, i: ((lax.axis_index("head") + n_head - steps) % n_head, 0), place[0]
                    ),
                )
            )
        flops += 2 * rows * cols * out_width
        if isinstance(right, tuple):
            lefts[-1:] = in_hbm(left)
            gathered, steps, first = right
            piece = gathered.shape[2]
            rights.append(gathered)
            right_specs.append(
                pl.BlockSpec(
                    (block // piece, 1, piece, cols),
                    partial(lambda step, at, i: (i, step, 0, at), steps - 1, first // cols),
                )
            )
        else:
            rights.append(right)
            right_specs.append(
                pl.BlockSpec((block, cols), lambda i: (lax.axis_index("head") * n_blocks + i, 0))
            )
    part = pl.BlockSpec((rows, block), lambda i: (0, i))
    extra = [] if base is None else [base]
    return pl.pallas_call(
        partial(products_kernel, len(pairs), base is not None),
        grid=(n_blocks,),
        in_specs=left_specs + right_specs + [part] * len(extra),
        out_specs=part,
        out_shape=jax.ShapeDtypeStruct((rows, out_width), dtype),
        compiler_params=pltpu.CompilerParams(vmem_limit_bytes=20 * MIB),
        cost_estimate=pl.CostEstimate(flops=flops, bytes_accessed=8 * MIB, transcendentals=0),
        name=name,
    )(*lefts, *in_hbm(*rights), *extra)


def attention_kernel(
    first_ref, query_ref, grad_ref, kv0, kv1, kv2, kv3,
    out_ref, dq_ref, bundle_ref, d0, d2, d3,
    kv_ref, acc_ref, score_ref, sum_ref, sems,
):
    rows = query_ref.shape[0]
    copies = [
        pltpu.make_async_copy(block, kv_ref.at[pl.ds(slot * rows, rows), :], sems.at[slot])
        for slot, block in enumerate((kv3, kv2, kv1, kv0))
    ]
    for copy in copies:
        copy.start()
    acc_ref[...] = jnp.zeros_like(acc_ref)
    for copy in copies:
        copy.wait()
    factor = HD ** (-0.5)
    wide = GROUP * GRAIN
    streams = range(TILE // GRAIN)
    key_local = lax.broadcasted_iota(jnp.int32, (TILE, wide), 0)
    query_local = lax.broadcasted_iota(jnp.int32, (TILE, wide), 1) % GRAIN
    heads = [slice(h * HD, (h + 1) * HD) for h in range(GROUP)]

    def tile_rows(tile):
        return pl.ds(pl.multiple_of(tile * TILE, TILE), TILE)

    for pair in range(rows // TILE):
        places = [pl.ds(pair * TILE + g * GRAIN, GRAIN) for g in streams]
        query = [jnp.concatenate([query_ref[here, cols] for cols in heads], axis=0) for here in places]
        grad = [jnp.concatenate([grad_ref[here, cols] for cols in heads], axis=0) for here in places]
        first = [first_ref[pair * len(places) + g] for g in streams]
        last = (SPAN * rows) // TILE + pair
        low = first[0] // TILE
        sum_ref[...] = jnp.zeros_like(sum_ref)

        def score_tile(tile, carry, diagonal):
            here = tile_rows(tile)
            following = []
            for g in streams:
                top, total = carry[g]
                score = dot_nt(kv_ref[here, :HD], query[g]) * (factor * LOG2E)
                keep = key_local >= first[g] - tile * TILE
                if diagonal:
                    keep = keep & (key_local <= query_local + g * GRAIN)
                score = jnp.where(keep, score, NEG)
                score_ref[g, here, :] = score
                new_top = jnp.maximum(top, jnp.max(score, axis=0, keepdims=True))
                weight = jnp.sum(jnp.exp2(score - new_top), axis=0, keepdims=True)
                following.append((new_top, total * jnp.exp2(top - new_top) + weight))
            return tuple(following)

        state = tuple(
            (jnp.full((1, wide), NEG, jnp.float32), jnp.zeros((1, wide), jnp.float32)) for g in streams
        )
        state = lax.fori_loop(low, last, lambda tile, carry: score_tile(tile, carry, False), state)
        state = score_tile(last, state, True)
        lse = [top + jnp.log2(total) for top, total in state]

        def output_tile(tile, carry):
            here = tile_rows(tile)
            value_grad = acc_ref[here, HD:]
            for g in streams:
                prob = jnp.exp2(score_ref[g, here, :] - lse[g])
                score_ref[g, here, :] = prob
                prob = prob.astype(jnp.bfloat16)
                sum_ref[g] += dot_tn(kv_ref[here, HD:], prob)
                value_grad = value_grad + dot_nn(prob, grad[g])
            acc_ref[here, HD:] = value_grad
            return carry

        lax.fori_loop(low, last + 1, output_tile, 0)
        delta = []
        for g in streams:
            turned = sum_ref[g].astype(jnp.bfloat16).astype(jnp.float32)
            delta.append(
                jnp.sum(turned * grad[g].astype(jnp.float32).T, axis=0, keepdims=True)
            )
            out_rows = turned.T.astype(jnp.bfloat16)
            for head, cols in enumerate(heads):
                out_ref[places[g], cols] = out_rows[head * GRAIN : (head + 1) * GRAIN]
        sum_ref[...] = jnp.zeros_like(sum_ref)

        def gradient_tile(tile, carry):
            here = tile_rows(tile)
            key_grad = acc_ref[here, :HD]
            for g in streams:
                dprob = dot_nt(kv_ref[here, HD:], grad[g])
                dscore = (score_ref[g, here, :] * (dprob - delta[g])).astype(jnp.bfloat16)
                key_grad = key_grad + dot_nn(dscore, query[g])
                sum_ref[g] += dot_tn(kv_ref[here, :HD], dscore)
            acc_ref[here, :HD] = key_grad
            return carry

        lax.fori_loop(low, last + 1, gradient_tile, 0)
        for g in streams:
            turned = sum_ref[g] * factor
            dquery = turned.T.astype(jnp.bfloat16)
            for head, cols in enumerate(heads):
                part = slice(head * GRAIN, (head + 1) * GRAIN)
                dq_ref[places[g], cols] = dquery[part]
                bundle_ref[cols, places[g]] = turned[:, part].astype(jnp.bfloat16)
    cols = query_ref.shape[1]
    for distance, blocks in enumerate(
        ((d0,), (bundle_ref.at[cols:, : 2 * HD],), (d2,), (d3, bundle_ref.at[cols:, 2 * HD :]))
    ):
        place = pl.ds((SPAN - distance) * rows, rows)
        key_grad, value_grad = acc_ref[place, :HD] * factor, acc_ref[place, HD:]
        for block in blocks:
            block[:, :HD] = key_grad.astype(block.dtype)
            block[:, HD:] = value_grad.astype(block.dtype)


def attention(first, query, grad, kv_list):
    rows, cols = query.shape
    window = (SPAN + 1) * rows
    low = jax.ShapeDtypeStruct((rows, cols), jnp.bfloat16)
    bundle = jax.ShapeDtypeStruct((cols + rows, rows), jnp.bfloat16)
    own = jax.ShapeDtypeStruct((rows, 2 * HD), jnp.float32)
    sent = jax.ShapeDtypeStruct((rows, 2 * HD), jnp.bfloat16)
    vmem = pl.BlockSpec(memory_space=pltpu.VMEM)
    anywhere = pl.BlockSpec(memory_space=pl.ANY)
    return pl.pallas_call(
        attention_kernel,
        out_shape=(low, low, bundle, own, sent, sent),
        in_specs=[pl.BlockSpec(memory_space=pltpu.SMEM), vmem, vmem] + [anywhere] * (SPAN + 1),
        out_specs=(vmem,) * 6,
        scratch_shapes=[
            pltpu.VMEM((window, 2 * HD), jnp.bfloat16),
            pltpu.VMEM((window, 2 * HD), jnp.float32),
            pltpu.VMEM((TILE // GRAIN, window, GROUP * GRAIN), jnp.float32),
            pltpu.VMEM((TILE // GRAIN, HD, GROUP * GRAIN), jnp.float32),
            pltpu.SemaphoreType.DMA((SPAN + 1,)),
        ],
        compiler_params=pltpu.CompilerParams(vmem_limit_bytes=24 * MIB),
        cost_estimate=pl.CostEstimate(
            flops=6 * 2 * rows * window * cols, bytes_accessed=6 * MIB, transcendentals=0
        ),
        name="attention",
    )(first, query, grad, *kv_list)


def shift(value, axis, steps):
    count = lax.axis_size(axis)
    pairs = [(i, i + steps) for i in range(count) if 0 <= i + steps < count]
    return lax.ppermute(value, axis, pairs)


def swap(value, axis, mask):
    return lax.ppermute(value, axis, [(i, i ^ mask) for i in range(lax.axis_size(axis))])


def rotate(value, axis, steps):
    count = lax.axis_size(axis)
    return lax.ppermute(value, axis, [(i, (i + steps) % count) for i in range(count)])


def body(inputs, query_weight, key_weight, value_weight, out_grad, doc_lengths):
    tok_rows, width = inputs.shape
    n_ctx = lax.axis_size("ctx")
    n_head = lax.axis_size("head")
    chips = n_ctx // 2
    ctx = lax.axis_index("ctx")
    head = lax.axis_index("head")
    q_cols = query_weight.shape[1]
    k_cols = key_weight.shape[1]

    weights = (query_weight, key_weight, value_weight)
    out_width = width // n_head
    piece = out_width // n_ctx
    pieces = cut_rows(weights, n_head, piece)
    pieces, inputs = lax.optimization_barrier((pieces, inputs))
    pieces = [rotate(rows, "head", step) for step, rows in enumerate(pieces, 1)]

    kv_loc = project(inputs, (key_weight, value_weight), "project_kv")
    kv_list = [kv_loc] + [shift(kv_loc, "ctx", distance) for distance in range(1, SPAN + 1)]
    other_inputs = swap(inputs, "ctx", 1)
    late_inputs, other_inputs, kv_loc = lax.optimization_barrier((inputs, other_inputs, kv_loc))
    query = project(late_inputs, (query_weight,), "project_query")
    query, kv_list, pieces = lax.optimization_barrier((query, kv_list, pieces))
    gathered = lax.all_gather(jnp.concatenate(pieces, axis=0), "ctx", axis=0, tiled=True)
    gathered = gathered.reshape(n_ctx, n_head - 1, piece, q_cols + 2 * k_cols)

    granules = tok_rows // GRAIN
    window_start = (ctx - SPAN) * tok_rows
    positions = ctx * tok_rows + GRAIN * jnp.arange(granules, dtype=jnp.int32)
    doc_ends = jnp.cumsum(doc_lengths)
    starts = jnp.sum(
        jnp.where(doc_ends[None, :] <= positions[:, None], doc_lengths[None, :], 0), axis=1
    )
    attn_out, dq_low, bundle, own_grads, mid_grads, far_grads = attention(
        starts - window_start, query, out_grad, kv_list
    )

    other_bundle = swap(bundle, "ctx", 1)
    dq_up = rotate(dq_low, "head", 1)
    dq_down = rotate(dq_low, "head", -1)
    far = lax.ppermute(
        far_grads, "ctx", [(source, source - SPAN) for source in range(0, n_ctx, 2) if source >= SPAN]
    )
    kv_shape = (tok_rows, 2 * k_cols)
    merged, = small_kernel(merge_kernel, [(kv_shape, jnp.bfloat16)], "merge", mid_grads, other_bundle)
    merged, late_bundle = lax.optimization_barrier((merged, other_bundle))
    merged = shift(merged, "ctx", -2)

    q_terms = weight_terms(bundle, late_bundle, q_cols, inputs, other_inputs, n_ctx, "query_terms")
    q_moved = [swap(q_terms[chips - 1], "ctx", 2 * (chips - 1))]
    dq_far = rotate(dq_up, "head", 1)
    far, merged, dq_up, dq_down, dq_low, q_terms = lax.optimization_barrier(
        (far, merged, dq_up, dq_down, dq_low, q_terms)
    )
    dkv_low, dkv_turned = small_kernel(
        combine_kernel, [(kv_shape, jnp.bfloat16), (kv_shape[::-1], jnp.bfloat16)], "combine",
        own_grads, merged, far, other_bundle,
    )
    dkv_all = lax.all_gather(dkv_low, "head", axis=0, tiled=True)
    other_dkv = swap(dkv_turned, "ctx", 1)
    q_moved += [swap(q_terms[chip], "ctx", 2 * chip) for chip in range(1, chips - 1)]
    kv_terms = weight_terms(
        dkv_turned, other_dkv, 2 * k_cols, inputs, other_inputs, n_ctx, "key_terms"
    )
    kv_terms, dq_far = lax.optimization_barrier((kv_terms, dq_far))
    kv_moved = [swap(term, "ctx", 2 * chip) for chip, term in enumerate(kv_terms) if chip > 0]
    _, dq_low, dq_up, dq_down, dkv_low = lax.optimization_barrier((kv_terms, dq_low, dq_up, dq_down, dkv_low))

    grad_sum = products(
        (
            ((dq_low, 0, q_cols), query_weight),
            ((dq_up, 0, q_cols), (gathered, 1, 0)),
            ((dq_down, 0, q_cols), (gathered, 3, 0)),
            ((dq_far, 0, q_cols), (gathered, 2, 0)),
            ((dkv_low, 0, k_cols), key_weight),
            ((dkv_low, 1, k_cols), value_weight),
        ),
        None, out_width, n_head, jnp.float32, "products_near",
    )
    grad_sum, q_moved, kv_moved = lax.optimization_barrier((grad_sum, q_moved, kv_moved))
    q_grad, = weight_rows([q_terms[0], *q_moved], (q_cols,), "query_rows")
    k_grad, v_grad = weight_rows([kv_terms[0], *kv_moved], (k_cols, k_cols), "key_rows")
    q_grad, k_grad, v_grad, grad_sum = lax.optimization_barrier((q_grad, k_grad, v_grad, grad_sum))
    input_grad = products(
        (
            *(((dkv_all, step), (gathered, step, q_cols)) for step in range(1, n_head)),
        ),
        grad_sum, out_width, n_head, jnp.bfloat16, "products_far",
    )
    return (attn_out, input_grad, q_grad, k_grad, v_grad)


def solution(mesh):
    return jax.shard_map(
        body,
        mesh=mesh,
        in_specs=(
            P("ctx", None),
            P(None, "head"),
            P(None, "head"),
            P(None, "head"),
            P("ctx", "head"),
            P(),
        ),
        out_specs=(P("ctx", "head"),) * 5,
        check_vma=False,
    )
```

```python
from functools import partial

import jax
import jax.numpy as jnp
from jax import lax
from jax.experimental import pallas as pl
from jax.experimental.pallas import tpu as pltpu
from jax.sharding import PartitionSpec as P

HD = 128
GROUP = 4
SPAN = 3
GRAIN = 128
TILE = 256
CHUNK = 512
MIB = 2**20

NEG = -1e30
LOG2E = 1.4426950408889634


def dot_nt(left_mat, right_mat):
    return lax.dot_general(
        left_mat, right_mat, (((1,), (1,)), ((), ())), preferred_element_type=jnp.float32
    )


def dot_tn(left_mat, right_mat):
    return lax.dot_general(
        left_mat, right_mat, (((0,), (0,)), ((), ())), preferred_element_type=jnp.float32
    )


def dot_nn(left_mat, right_mat):
    return jnp.dot(left_mat, right_mat, preferred_element_type=jnp.float32)


def in_hbm(*arrays):
    return [pltpu.with_memory_space_constraint(array, pltpu.HBM) for array in arrays]


def cut_kernel(*refs):
    weight_refs, piece_refs, sems = refs[:3], refs[3:-1], refs[-1]
    head, ctx = lax.axis_index("head"), lax.axis_index("ctx")
    n_head = len(piece_refs) + 1
    piece = piece_refs[0].shape[0]
    copies = []
    for distance, piece_ref in enumerate(piece_refs, 1):
        group = lax.rem(head + distance, n_head)
        first = group * (weight_refs[0].shape[0] // n_head) + ctx * piece
        at = 0
        for number, weight_ref in enumerate(weight_refs):
            cols = weight_ref.shape[1]
            copies.append(
                pltpu.make_async_copy(
                    weight_ref.at[pl.ds(pl.multiple_of(first, piece), piece), :],
                    piece_ref.at[:, pl.ds(at, cols)],
                    sems.at[distance - 1, number],
                )
            )
            at += cols
    for copy in copies:
        copy.start()
    for copy in copies:
        copy.wait()


def cut_rows(weights, n_head, piece):
    cols = sum(weight.shape[1] for weight in weights)
    anywhere = pl.BlockSpec(memory_space=pl.ANY)
    return pl.pallas_call(
        cut_kernel,
        out_shape=(jax.ShapeDtypeStruct((piece, cols), jnp.bfloat16),) * (n_head - 1),
        in_specs=[anywhere] * 3,
        out_specs=(pl.BlockSpec(memory_space=pltpu.VMEM),) * (n_head - 1),
        scratch_shapes=[pltpu.SemaphoreType.DMA((n_head - 1, 3))],
        cost_estimate=pl.CostEstimate(flops=0, bytes_accessed=2 * MIB, transcendentals=0),
        name="cut_rows",
    )(*in_hbm(*weights))


def project_kernel(x_ref, *refs):
    n = len(refs) - 4
    weight_refs, (out_ref, x_here, weight_here, sems) = refs[:n], refs[n:]
    rows = x_ref.shape[0]
    chunks = []
    for step in range(x_ref.shape[1] // CHUNK):
        part = pl.ds(step * CHUNK, CHUNK)
        copies = [pltpu.make_async_copy(x_ref.at[:, part], x_here.at[:, part], sems.at[step, 0])]
        at = 0
        for number, weight_ref in enumerate(weight_refs):
            cols = pl.ds(at, weight_ref.shape[1])
            at += weight_ref.shape[1]
            copies.append(
                pltpu.make_async_copy(
                    weight_ref.at[part, :], weight_here.at[part, cols], sems.at[step, 1 + number]
                )
            )
        for copy in copies:
            copy.start()
        chunks.append((part, copies))
    total = jnp.zeros((rows, weight_here.shape[1]), jnp.float32)
    for part, copies in chunks:
        for copy in copies:
            copy.wait()
        total = total + dot_nn(x_here[:, part], weight_here[part, :])
    out_ref[...] = total.astype(out_ref.dtype)


def project(inputs, weights, name):
    rows, width = inputs.shape
    cols = sum(weight.shape[1] for weight in weights)
    anywhere = pl.BlockSpec(memory_space=pl.ANY)
    return pl.pallas_call(
        project_kernel,
        in_specs=[anywhere] * (len(weights) + 1),
        out_specs=pl.BlockSpec(memory_space=pltpu.VMEM),
        out_shape=jax.ShapeDtypeStruct((rows, cols), jnp.bfloat16),
        scratch_shapes=[
            pltpu.VMEM((rows, width), jnp.bfloat16),
            pltpu.VMEM((width, cols), jnp.bfloat16),
            pltpu.SemaphoreType.DMA((width // CHUNK, len(weights) + 1)),
        ],
        compiler_params=pltpu.CompilerParams(vmem_limit_bytes=24 * MIB),
        cost_estimate=pl.CostEstimate(
            flops=2 * rows * width * cols, bytes_accessed=2 * width * (rows + cols), transcendentals=0
        ),
        name=name,
    )(*in_hbm(inputs, *weights))


def merge_kernel(d2_ref, bundle_ref, out_ref):
    rows, cols = out_ref.shape
    core = lax.axis_index("ctx") % 2
    here = pl.ds(bundle_ref.shape[0] - rows, rows)
    near, far = bundle_ref[here, :cols], bundle_ref[here, cols:]
    other = jnp.where(core == 1, near.astype(jnp.float32), far.astype(jnp.float32))
    out_ref[...] = (d2_ref[...].astype(jnp.float32) + other).astype(out_ref.dtype)


def combine_kernel(own_ref, merged_ref, far_ref, bundle_ref, low_ref, turned_ref):
    rows, cols = own_ref.shape
    core = lax.axis_index("ctx") % 2
    near = bundle_ref[bundle_ref.shape[0] - rows :, :cols].astype(jnp.float32)
    total = own_ref[...] + merged_ref[...].astype(jnp.float32) + far_ref[...].astype(jnp.float32)
    total = total + jnp.where(core == 0, near, 0.0)
    low_ref[...] = total.astype(jnp.bfloat16)
    turned_ref[...] = total.T.astype(jnp.bfloat16)


def small_kernel(kernel, shapes, name, *operands):
    def whole(shape):
        return pl.BlockSpec(shape, lambda i: (0, 0))

    return pl.pallas_call(
        kernel,
        grid=(1,),
        out_shape=tuple(jax.ShapeDtypeStruct(shape, dtype) for shape, dtype in shapes),
        in_specs=[whole(operand.shape) for operand in operands],
        out_specs=tuple(whole(shape) for shape, dtype in shapes),
        compiler_params=pltpu.CompilerParams(vmem_limit_bytes=20 * MIB),
        cost_estimate=pl.CostEstimate(flops=4 * MIB, bytes_accessed=4 * MIB, transcendentals=0),
        name=name,
    )(*operands)


def terms_kernel(chips, turned_ref, other_turned_ref, x_ref, other_x_ref, *refs):
    out_refs, (x_here, sum_here, low_here, in_sems, out_sems) = refs[:chips], refs[chips:]
    cols, kept = out_refs[0].shape
    ctx = lax.axis_index("ctx")
    order = [*range(1, chips), 0]
    coming = {}
    for chip in order:
        first = pl.multiple_of((((ctx // 2) ^ chip) * 2 + ctx % 2) * kept, kept)
        coming[chip] = [
            pltpu.make_async_copy(ref.at[:, pl.ds(first, kept)], x_here.at[chip, side], in_sems.at[chip, side])
            for side, ref in enumerate((x_ref, other_x_ref))
        ]
        for copy in coming[chip]:
            copy.start()
    going = []
    for chip in order:
        for copy in coming[chip]:
            copy.wait()
        term = dot_nn(turned_ref[:cols, :], x_here[chip, 0]) + dot_nn(other_turned_ref[:cols, :], x_here[chip, 1])
        here = sum_here if chip == 0 else low_here.at[chip]
        here[...] = term.astype(here.dtype)
        copy = pltpu.make_async_copy(here, out_refs[chip], out_sems.at[chip])
        copy.start()
        going.append(copy)
    for copy in going:
        copy.wait()


def weight_terms(turned, other_turned, cols, inputs, other_inputs, n_ctx, name):
    rows = turned.shape[1]
    kept = inputs.shape[1] // n_ctx
    chips = n_ctx // 2
    vmem = pl.BlockSpec(memory_space=pltpu.VMEM)
    anywhere = pl.BlockSpec(memory_space=pl.ANY)
    return pl.pallas_call(
        partial(terms_kernel, chips),
        in_specs=[vmem, vmem, anywhere, anywhere],
        out_specs=(anywhere,) * chips,
        out_shape=tuple(
            jax.ShapeDtypeStruct((cols, kept), jnp.float32 if chip == 0 else jnp.bfloat16)
            for chip in range(chips)
        ),
        scratch_shapes=[
            pltpu.VMEM((chips, 2, rows, kept), jnp.bfloat16),
            pltpu.VMEM((cols, kept), jnp.float32),
            pltpu.VMEM((chips, cols, kept), jnp.bfloat16),
            pltpu.SemaphoreType.DMA((chips, 2)),
            pltpu.SemaphoreType.DMA((chips,)),
        ],
        compiler_params=pltpu.CompilerParams(vmem_limit_bytes=24 * MIB),
        cost_estimate=pl.CostEstimate(
            flops=4 * cols * rows * kept * chips, bytes_accessed=10 * MIB, transcendentals=0
        ),
        name=name,
    )(turned, other_turned, *in_hbm(inputs, other_inputs))


def rows_kernel(n_in, *refs):
    in_refs, out_refs = refs[:n_in], refs[n_in:]
    total = in_refs[0][...]
    for in_ref in in_refs[1:]:
        total += in_ref[...].astype(jnp.float32)
    at = 0
    for out_ref in out_refs:
        cols = slice(at, at + out_ref.shape[1])
        at = cols.stop
        out_ref[...] = total[cols, :].T


def weight_rows(terms, widths, name):
    kept = terms[0].shape[1]
    shapes = [((kept, width), jnp.float32) for width in widths]
    return small_kernel(partial(rows_kernel, len(terms)), shapes, name, *terms)


def products_kernel(count, has_base, *refs):
    left_refs, rows_refs, out_ref = refs[:count], refs[count : 2 * count], refs[-1]
    total = refs[2 * count][...] if has_base else None
    for left_ref, rows_ref in zip(left_refs, rows_refs):
        rows = rows_ref[...]
        term = dot_nt(left_ref[...], rows.reshape(-1, rows.shape[-1]))
        total = term if total is None else total + term
    out_ref[...] = total.astype(out_ref.dtype)


def products(pairs, base, out_width, n_head, dtype, name):
    rows = base.shape[0] if base is not None else pairs[0][0][0].shape[0]
    block = 512
    n_blocks = out_width // block
    left_specs, right_specs, lefts, rights = [], [], [], []
    flops = 0
    for (left, *place), right in pairs:
        lefts.append(left)
        if len(place) == 2:
            column, cols = place
            left_specs.append(pl.BlockSpec((rows, cols), partial(lambda column, i: (0, column), column)))
        else:
            cols = left.shape[1]
            left_specs.append(
                pl.BlockSpec(
                    (rows, cols),
                    partial(
                        lambda steps, i: ((lax.axis_index("head") + n_head - steps) % n_head, 0), place[0]
                    ),
                )
            )
        flops += 2 * rows * cols * out_width
        if isinstance(right, tuple):
            lefts[-1:] = in_hbm(left)
            gathered, steps, first = right
            piece = gathered.shape[2]
            rights.append(gathered)
            right_specs.append(
                pl.BlockSpec(
                    (block // piece, 1, piece, cols),
                    partial(lambda step, at, i: (i, step, 0, at), steps - 1, first // cols),
                )
            )
        else:
            rights.append(right)
            right_specs.append(
                pl.BlockSpec((block, cols), lambda i: (lax.axis_index("head") * n_blocks + i, 0))
            )
    part = pl.BlockSpec((rows, block), lambda i: (0, i))
    extra = [] if base is None else [base]
    return pl.pallas_call(
        partial(products_kernel, len(pairs), base is not None),
        grid=(n_blocks,),
        in_specs=left_specs + right_specs + [part] * len(extra),
        out_specs=part,
        out_shape=jax.ShapeDtypeStruct((rows, out_width), dtype),
        compiler_params=pltpu.CompilerParams(vmem_limit_bytes=20 * MIB),
        cost_estimate=pl.CostEstimate(flops=flops, bytes_accessed=8 * MIB, transcendentals=0),
        name=name,
    )(*lefts, *in_hbm(*rights), *extra)


def attention_kernel(
    first_ref, query_ref, grad_ref, kv0, kv1, kv2, kv3,
    out_ref, dq_ref, bundle_ref, d0, d2, d3,
    kv_ref, acc_ref, score_ref, sum_ref, sems,
):
    rows = query_ref.shape[0]
    copies = [
        pltpu.make_async_copy(block, kv_ref.at[pl.ds(slot * rows, rows), :], sems.at[slot])
        for slot, block in enumerate((kv3, kv2, kv1, kv0))
    ]
    for copy in copies:
        copy.start()
    acc_ref[...] = jnp.zeros_like(acc_ref)
    for copy in copies:
        copy.wait()
    factor = HD ** (-0.5)
    wide = GROUP * GRAIN
    streams = range(TILE // GRAIN)
    key_local = lax.broadcasted_iota(jnp.int32, (TILE, wide), 0)
    query_local = lax.broadcasted_iota(jnp.int32, (TILE, wide), 1) % GRAIN
    heads = [slice(h * HD, (h + 1) * HD) for h in range(GROUP)]

    def tile_rows(tile):
        return pl.ds(pl.multiple_of(tile * TILE, TILE), TILE)

    for pair in range(rows // TILE):
        places = [pl.ds(pair * TILE + g * GRAIN, GRAIN) for g in streams]
        query = [jnp.concatenate([query_ref[here, cols] for cols in heads], axis=0) for here in places]
        grad = [jnp.concatenate([grad_ref[here, cols] for cols in heads], axis=0) for here in places]
        first = [first_ref[pair * len(places) + g] for g in streams]
        last = (SPAN * rows) // TILE + pair
        low = first[0] // TILE
        sum_ref[...] = jnp.zeros_like(sum_ref)

        def score_tile(tile, carry, diagonal):
            here = tile_rows(tile)
            following = []
            for g in streams:
                top, total = carry[g]
                score = dot_nt(kv_ref[here, :HD], query[g]) * (factor * LOG2E)
                keep = key_local >= first[g] - tile * TILE
                if diagonal:
                    keep = keep & (key_local <= query_local + g * GRAIN)
                score = jnp.where(keep, score, NEG)
                score_ref[g, here, :] = score
                new_top = jnp.maximum(top, jnp.max(score, axis=0, keepdims=True))
                weight = jnp.sum(jnp.exp2(score - new_top), axis=0, keepdims=True)
                following.append((new_top, total * jnp.exp2(top - new_top) + weight))
            return tuple(following)

        state = tuple(
            (jnp.full((1, wide), NEG, jnp.float32), jnp.zeros((1, wide), jnp.float32)) for g in streams
        )
        state = lax.fori_loop(low, last, lambda tile, carry: score_tile(tile, carry, False), state)
        state = score_tile(last, state, True)
        lse = [top + jnp.log2(total) for top, total in state]

        def output_tile(tile, carry):
            here = tile_rows(tile)
            value_grad = acc_ref[here, HD:]
            for g in streams:
                prob = jnp.exp2(score_ref[g, here, :] - lse[g])
                score_ref[g, here, :] = prob
                prob = prob.astype(jnp.bfloat16)
                sum_ref[g] += dot_tn(kv_ref[here, HD:], prob)
                value_grad = value_grad + dot_nn(prob, grad[g])
            acc_ref[here, HD:] = value_grad
            return carry

        lax.fori_loop(low, last + 1, output_tile, 0)
        delta = []
        for g in streams:
            turned = sum_ref[g].astype(jnp.bfloat16).astype(jnp.float32)
            delta.append(
                jnp.sum(turned * grad[g].astype(jnp.float32).T, axis=0, keepdims=True)
            )
            out_rows = turned.T.astype(jnp.bfloat16)
            for head, cols in enumerate(heads):
                out_ref[places[g], cols] = out_rows[head * GRAIN : (head + 1) * GRAIN]
        sum_ref[...] = jnp.zeros_like(sum_ref)

        def gradient_tile(tile, carry):
            here = tile_rows(tile)
            key_grad = acc_ref[here, :HD]
            for g in streams:
                dprob = dot_nt(kv_ref[here, HD:], grad[g])
                dscore = (score_ref[g, here, :] * (dprob - delta[g])).astype(jnp.bfloat16)
                key_grad = key_grad + dot_nn(dscore, query[g])
                sum_ref[g] += dot_tn(kv_ref[here, :HD], dscore)
            acc_ref[here, :HD] = key_grad
            return carry

        lax.fori_loop(low, last + 1, gradient_tile, 0)
        for g in streams:
            turned = sum_ref[g] * factor
            dquery = turned.T.astype(jnp.bfloat16)
            for head, cols in enumerate(heads):
                part = slice(head * GRAIN, (head + 1) * GRAIN)
                dq_ref[places[g], cols] = dquery[part]
                bundle_ref[cols, places[g]] = turned[:, part].astype(jnp.bfloat16)
    cols = query_ref.shape[1]
    for distance, blocks in enumerate(
        ((d0,), (bundle_ref.at[cols:, : 2 * HD],), (d2,), (d3, bundle_ref.at[cols:, 2 * HD :]))
    ):
        place = pl.ds((SPAN - distance) * rows, rows)
        key_grad, value_grad = acc_ref[place, :HD] * factor, acc_ref[place, HD:]
        for block in blocks:
            block[:, :HD] = key_grad.astype(block.dtype)
            block[:, HD:] = value_grad.astype(block.dtype)


def attention(first, query, grad, kv_list):
    rows, cols = query.shape
    window = (SPAN + 1) * rows
    low = jax.ShapeDtypeStruct((rows, cols), jnp.bfloat16)
    bundle = jax.ShapeDtypeStruct((cols + rows, rows), jnp.bfloat16)
    own = jax.ShapeDtypeStruct((rows, 2 * HD), jnp.float32)
    sent = jax.ShapeDtypeStruct((rows, 2 * HD), jnp.bfloat16)
    vmem = pl.BlockSpec(memory_space=pltpu.VMEM)
    anywhere = pl.BlockSpec(memory_space=pl.ANY)
    return pl.pallas_call(
        attention_kernel,
        out_shape=(low, low, bundle, own, sent, sent),
        in_specs=[pl.BlockSpec(memory_space=pltpu.SMEM), vmem, vmem] + [anywhere] * (SPAN + 1),
        out_specs=(vmem,) * 6,
        scratch_shapes=[
            pltpu.VMEM((window, 2 * HD), jnp.bfloat16),
            pltpu.VMEM((window, 2 * HD), jnp.float32),
            pltpu.VMEM((TILE // GRAIN, window, GROUP * GRAIN), jnp.float32),
            pltpu.VMEM((TILE // GRAIN, HD, GROUP * GRAIN), jnp.float32),
            pltpu.SemaphoreType.DMA((SPAN + 1,)),
        ],
        compiler_params=pltpu.CompilerParams(vmem_limit_bytes=24 * MIB),
        cost_estimate=pl.CostEstimate(
            flops=6 * 2 * rows * window * cols, bytes_accessed=6 * MIB, transcendentals=0
        ),
        name="attention",
    )(first, query, grad, *kv_list)


def shift(value, axis, steps):
    count = lax.axis_size(axis)
    pairs = [(i, i + steps) for i in range(count) if 0 <= i + steps < count]
    return lax.ppermute(value, axis, pairs)


def swap(value, axis, mask):
    return lax.ppermute(value, axis, [(i, i ^ mask) for i in range(lax.axis_size(axis))])


def rotate(value, axis, steps):
    count = lax.axis_size(axis)
    return lax.ppermute(value, axis, [(i, (i + steps) % count) for i in range(count)])


def body(inputs, query_weight, key_weight, value_weight, out_grad, doc_lengths):
    tok_rows, width = inputs.shape
    n_ctx = lax.axis_size("ctx")
    n_head = lax.axis_size("head")
    chips = n_ctx // 2
    ctx = lax.axis_index("ctx")
    head = lax.axis_index("head")
    q_cols = query_weight.shape[1]
    k_cols = key_weight.shape[1]

    weights = (query_weight, key_weight, value_weight)
    out_width = width // n_head
    piece = out_width // n_ctx
    pieces = cut_rows(weights, n_head, piece)
    pieces, inputs = lax.optimization_barrier((pieces, inputs))
    pieces = [rotate(rows, "head", step) for step, rows in enumerate(pieces, 1)]

    kv_loc = project(inputs, (key_weight, value_weight), "project_kv")
    kv_list = [kv_loc] + [shift(kv_loc, "ctx", distance) for distance in range(1, SPAN + 1)]
    other_inputs = swap(inputs, "ctx", 1)
    late_inputs, other_inputs, kv_loc = lax.optimization_barrier((inputs, other_inputs, kv_loc))
    query = project(late_inputs, (query_weight,), "project_query")
    query, kv_list, pieces = lax.optimization_barrier((query, kv_list, pieces))
    gathered = lax.all_gather(jnp.concatenate(pieces, axis=0), "ctx", axis=0, tiled=True)
    gathered = gathered.reshape(n_ctx, n_head - 1, piece, q_cols + 2 * k_cols)

    granules = tok_rows // GRAIN
    window_start = (ctx - SPAN) * tok_rows
    positions = ctx * tok_rows + GRAIN * jnp.arange(granules, dtype=jnp.int32)
    doc_ends = jnp.cumsum(doc_lengths)
    starts = jnp.sum(
        jnp.where(doc_ends[None, :] <= positions[:, None], doc_lengths[None, :], 0), axis=1
    )
    attn_out, dq_low, bundle, own_grads, mid_grads, far_grads = attention(
        starts - window_start, query, out_grad, kv_list
    )

    other_bundle = swap(bundle, "ctx", 1)
    dq_up = rotate(dq_low, "head", 1)
    dq_down = rotate(dq_low, "head", -1)
    far = lax.ppermute(
        far_grads, "ctx", [(source, source - SPAN) for source in range(0, n_ctx, 2) if source >= SPAN]
    )
    kv_shape = (tok_rows, 2 * k_cols)
    merged, = small_kernel(merge_kernel, [(kv_shape, jnp.bfloat16)], "merge", mid_grads, other_bundle)
    merged, late_bundle = lax.optimization_barrier((merged, other_bundle))
    merged = shift(merged, "ctx", -2)

    q_terms = weight_terms(bundle, late_bundle, q_cols, inputs, other_inputs, n_ctx, "query_terms")
    q_moved = [swap(q_terms[chips - 1], "ctx", 2 * (chips - 1))]
    dq_far = rotate(dq_up, "head", 1)
    far, merged, dq_up, dq_down, dq_low, q_terms = lax.optimization_barrier(
        (far, merged, dq_up, dq_down, dq_low, q_terms)
    )
    dkv_low, dkv_turned = small_kernel(
        combine_kernel, [(kv_shape, jnp.bfloat16), (kv_shape[::-1], jnp.bfloat16)], "combine",
        own_grads, merged, far, other_bundle,
    )
    dkv_all = lax.all_gather(dkv_low, "head", axis=0, tiled=True)
    other_dkv = swap(dkv_turned, "ctx", 1)
    q_moved += [swap(q_terms[chip], "ctx", 2 * chip) for chip in range(1, chips - 1)]
    kv_terms = weight_terms(
        dkv_turned, other_dkv, 2 * k_cols, inputs, other_inputs, n_ctx, "key_terms"
    )
    kv_terms, dq_far = lax.optimization_barrier((kv_terms, dq_far))
    kv_moved = [swap(term, "ctx", 2 * chip) for chip, term in enumerate(kv_terms) if chip > 0]
    _, dq_low, dq_up, dq_down, dkv_low = lax.optimization_barrier((kv_terms, dq_low, dq_up, dq_down, dkv_low))

    grad_sum = products(
        (
            ((dq_low, 0, q_cols), query_weight),
            ((dq_up, 0, q_cols), (gathered, 1, 0)),
            ((dq_down, 0, q_cols), (gathered, 3, 0)),
            ((dq_far, 0, q_cols), (gathered, 2, 0)),
            ((dkv_low, 0, k_cols), key_weight),
            ((dkv_low, 1, k_cols), value_weight),
        ),
        None, out_width, n_head, jnp.float32, "products_near",
    )
    grad_sum, q_moved = lax.optimization_barrier((grad_sum, q_moved))
    q_grad, = weight_rows([q_terms[0], *q_moved], (q_cols,), "query_rows")
    q_grad, grad_sum = lax.optimization_barrier((q_grad, grad_sum))
    input_grad = products(
        [((dkv_all, step), (gathered, step, q_cols)) for step in range(1, n_head)],
        grad_sum, out_width, n_head, jnp.bfloat16, "products_far",
    )
    input_grad, kv_moved = lax.optimization_barrier((input_grad, kv_moved))
    k_grad, v_grad = weight_rows([kv_terms[0], *kv_moved], (k_cols, k_cols), "key_rows")
    return (attn_out, input_grad, q_grad, k_grad, v_grad)


def solution(mesh):
    return jax.shard_map(
        body,
        mesh=mesh,
        in_specs=(
            P("ctx", None),
            P(None, "head"),
            P(None, "head"),
            P(None, "head"),
            P("ctx", "head"),
            P(),
        ),
        out_specs=(P("ctx", "head"),) * 5,
        check_vma=False,
    )
```

```python
from functools import partial

import jax
import jax.numpy as jnp
from jax import lax
from jax.experimental import pallas as pl
from jax.experimental.pallas import tpu as pltpu
from jax.sharding import PartitionSpec as P

HD = 128
GROUP = 4
SPAN = 3
GRAIN = 128
TILE = 256
CHUNK = 512
MIB = 2**20

NEG = -1e30
LOG2E = 1.4426950408889634


def dot_nt(left_mat, right_mat):
    return lax.dot_general(
        left_mat, right_mat, (((1,), (1,)), ((), ())), preferred_element_type=jnp.float32
    )


def dot_tn(left_mat, right_mat):
    return lax.dot_general(
        left_mat, right_mat, (((0,), (0,)), ((), ())), preferred_element_type=jnp.float32
    )


def dot_nn(left_mat, right_mat):
    return jnp.dot(left_mat, right_mat, preferred_element_type=jnp.float32)


def in_hbm(*arrays):
    return [pltpu.with_memory_space_constraint(array, pltpu.HBM) for array in arrays]


def cut_kernel(*refs):
    weight_refs, piece_refs, sems = refs[:3], refs[3:-1], refs[-1]
    head, ctx = lax.axis_index("head"), lax.axis_index("ctx")
    n_head = len(piece_refs) + 1
    piece = piece_refs[0].shape[0]
    copies = []
    for distance, piece_ref in enumerate(piece_refs, 1):
        group = lax.rem(head + distance, n_head)
        first = group * (weight_refs[0].shape[0] // n_head) + ctx * piece
        at = 0
        for number, weight_ref in enumerate(weight_refs):
            cols = weight_ref.shape[1]
            copies.append(
                pltpu.make_async_copy(
                    weight_ref.at[pl.ds(pl.multiple_of(first, piece), piece), :],
                    piece_ref.at[:, pl.ds(at, cols)],
                    sems.at[distance - 1, number],
                )
            )
            at += cols
    for copy in copies:
        copy.start()
    for copy in copies:
        copy.wait()


def cut_rows(weights, n_head, piece):
    cols = sum(weight.shape[1] for weight in weights)
    anywhere = pl.BlockSpec(memory_space=pl.ANY)
    return pl.pallas_call(
        cut_kernel,
        out_shape=(jax.ShapeDtypeStruct((piece, cols), jnp.bfloat16),) * (n_head - 1),
        in_specs=[anywhere] * 3,
        out_specs=(pl.BlockSpec(memory_space=pltpu.VMEM),) * (n_head - 1),
        scratch_shapes=[pltpu.SemaphoreType.DMA((n_head - 1, 3))],
        cost_estimate=pl.CostEstimate(flops=0, bytes_accessed=2 * MIB, transcendentals=0),
        name="cut_rows",
    )(*in_hbm(*weights))


def project_kernel(x_ref, *refs):
    n = len(refs) - 4
    weight_refs, (out_ref, x_here, weight_here, sems) = refs[:n], refs[n:]
    rows = x_ref.shape[0]
    chunks = []
    for step in range(x_ref.shape[1] // CHUNK):
        part = pl.ds(step * CHUNK, CHUNK)
        copies = [pltpu.make_async_copy(x_ref.at[:, part], x_here.at[:, part], sems.at[step, 0])]
        at = 0
        for number, weight_ref in enumerate(weight_refs):
            cols = pl.ds(at, weight_ref.shape[1])
            at += weight_ref.shape[1]
            copies.append(
                pltpu.make_async_copy(
                    weight_ref.at[part, :], weight_here.at[part, cols], sems.at[step, 1 + number]
                )
            )
        for copy in copies:
            copy.start()
        chunks.append((part, copies))
    total = jnp.zeros((rows, weight_here.shape[1]), jnp.float32)
    for part, copies in chunks:
        for copy in copies:
            copy.wait()
        total = total + dot_nn(x_here[:, part], weight_here[part, :])
    out_ref[...] = total.astype(out_ref.dtype)


def project(inputs, weights, name):
    rows, width = inputs.shape
    cols = sum(weight.shape[1] for weight in weights)
    anywhere = pl.BlockSpec(memory_space=pl.ANY)
    return pl.pallas_call(
        project_kernel,
        in_specs=[anywhere] * (len(weights) + 1),
        out_specs=pl.BlockSpec(memory_space=pltpu.VMEM),
        out_shape=jax.ShapeDtypeStruct((rows, cols), jnp.bfloat16),
        scratch_shapes=[
            pltpu.VMEM((rows, width), jnp.bfloat16),
            pltpu.VMEM((width, cols), jnp.bfloat16),
            pltpu.SemaphoreType.DMA((width // CHUNK, len(weights) + 1)),
        ],
        compiler_params=pltpu.CompilerParams(vmem_limit_bytes=24 * MIB),
        cost_estimate=pl.CostEstimate(
            flops=2 * rows * width * cols, bytes_accessed=2 * width * (rows + cols), transcendentals=0
        ),
        name=name,
    )(*in_hbm(inputs, *weights))


def merge_kernel(d2_ref, bundle_ref, out_ref):
    rows, cols = out_ref.shape
    core = lax.axis_index("ctx") % 2
    here = pl.ds(bundle_ref.shape[0] - rows, rows)
    near, far = bundle_ref[here, :cols], bundle_ref[here, cols:]
    other = jnp.where(core == 1, near.astype(jnp.float32), far.astype(jnp.float32))
    out_ref[...] = (d2_ref[...].astype(jnp.float32) + other).astype(out_ref.dtype)


def combine_kernel(own_ref, merged_ref, far_ref, bundle_ref, low_ref, turned_ref):
    rows, cols = own_ref.shape
    core = lax.axis_index("ctx") % 2
    near = bundle_ref[bundle_ref.shape[0] - rows :, :cols].astype(jnp.float32)
    total = own_ref[...] + merged_ref[...].astype(jnp.float32) + far_ref[...].astype(jnp.float32)
    total = total + jnp.where(core == 0, near, 0.0)
    low_ref[...] = total.astype(jnp.bfloat16)
    turned_ref[...] = total.T.astype(jnp.bfloat16)


def small_kernel(kernel, shapes, name, *operands):
    def whole(shape):
        return pl.BlockSpec(shape, lambda i: (0, 0))

    return pl.pallas_call(
        kernel,
        grid=(1,),
        out_shape=tuple(jax.ShapeDtypeStruct(shape, dtype) for shape, dtype in shapes),
        in_specs=[whole(operand.shape) for operand in operands],
        out_specs=tuple(whole(shape) for shape, dtype in shapes),
        compiler_params=pltpu.CompilerParams(vmem_limit_bytes=20 * MIB),
        cost_estimate=pl.CostEstimate(flops=4 * MIB, bytes_accessed=4 * MIB, transcendentals=0),
        name=name,
    )(*operands)


def terms_kernel(chips, turned_ref, other_turned_ref, x_ref, other_x_ref, *refs):
    out_refs, (x_here, sum_here, low_here, in_sems, out_sems) = refs[:chips], refs[chips:]
    cols, kept = out_refs[0].shape
    ctx = lax.axis_index("ctx")
    order = [*range(1, chips), 0]
    coming = {}
    for chip in order:
        first = pl.multiple_of((((ctx // 2) ^ chip) * 2 + ctx % 2) * kept, kept)
        coming[chip] = [
            pltpu.make_async_copy(ref.at[:, pl.ds(first, kept)], x_here.at[chip, side], in_sems.at[chip, side])
            for side, ref in enumerate((x_ref, other_x_ref))
        ]
        for copy in coming[chip]:
            copy.start()
    going = []
    for chip in order:
        for copy in coming[chip]:
            copy.wait()
        term = dot_nn(turned_ref[:cols, :], x_here[chip, 0]) + dot_nn(other_turned_ref[:cols, :], x_here[chip, 1])
        here = sum_here if chip == 0 else low_here.at[chip]
        here[...] = term.astype(here.dtype)
        copy = pltpu.make_async_copy(here, out_refs[chip], out_sems.at[chip])
        copy.start()
        going.append(copy)
    for copy in going:
        copy.wait()


def weight_terms(turned, other_turned, cols, inputs, other_inputs, n_ctx, name):
    rows = turned.shape[1]
    kept = inputs.shape[1] // n_ctx
    chips = n_ctx // 2
    vmem = pl.BlockSpec(memory_space=pltpu.VMEM)
    anywhere = pl.BlockSpec(memory_space=pl.ANY)
    return pl.pallas_call(
        partial(terms_kernel, chips),
        in_specs=[vmem, vmem, anywhere, anywhere],
        out_specs=(anywhere,) * chips,
        out_shape=tuple(
            jax.ShapeDtypeStruct((cols, kept), jnp.float32 if chip == 0 else jnp.bfloat16)
            for chip in range(chips)
        ),
        scratch_shapes=[
            pltpu.VMEM((chips, 2, rows, kept), jnp.bfloat16),
            pltpu.VMEM((cols, kept), jnp.float32),
            pltpu.VMEM((chips, cols, kept), jnp.bfloat16),
            pltpu.SemaphoreType.DMA((chips, 2)),
            pltpu.SemaphoreType.DMA((chips,)),
        ],
        compiler_params=pltpu.CompilerParams(vmem_limit_bytes=24 * MIB),
        cost_estimate=pl.CostEstimate(
            flops=4 * cols * rows * kept * chips, bytes_accessed=10 * MIB, transcendentals=0
        ),
        name=name,
    )(turned, other_turned, *in_hbm(inputs, other_inputs))


def rows_kernel(n_in, *refs):
    in_refs, out_refs = refs[:n_in], refs[n_in:]
    total = in_refs[0][...]
    for in_ref in in_refs[1:]:
        total += in_ref[...].astype(jnp.float32)
    at = 0
    for out_ref in out_refs:
        cols = slice(at, at + out_ref.shape[1])
        at = cols.stop
        out_ref[...] = total[cols, :].T


def weight_rows(terms, widths, name):
    kept = terms[0].shape[1]
    shapes = [((kept, width), jnp.float32) for width in widths]
    return small_kernel(partial(rows_kernel, len(terms)), shapes, name, *terms)


def products_kernel(count, has_base, *refs):
    left_refs, rows_refs, out_ref = refs[:count], refs[count : 2 * count], refs[-1]
    total = refs[2 * count][...] if has_base else None
    for left_ref, rows_ref in zip(left_refs, rows_refs):
        rows = rows_ref[...]
        term = dot_nt(left_ref[...], rows.reshape(-1, rows.shape[-1]))
        total = term if total is None else total + term
    out_ref[...] = total.astype(out_ref.dtype)


def products(pairs, base, out_width, n_head, dtype, name):
    rows = base.shape[0] if base is not None else pairs[0][0][0].shape[0]
    block = 512
    n_blocks = out_width // block
    left_specs, right_specs, lefts, rights = [], [], [], []
    flops = 0
    for (left, *place), right in pairs:
        lefts.append(left)
        if len(place) == 2:
            column, cols = place
            left_specs.append(pl.BlockSpec((rows, cols), partial(lambda column, i: (0, column), column)))
        else:
            cols = left.shape[1]
            left_specs.append(
                pl.BlockSpec(
                    (rows, cols),
                    partial(
                        lambda steps, i: ((lax.axis_index("head") + n_head - steps) % n_head, 0), place[0]
                    ),
                )
            )
        flops += 2 * rows * cols * out_width
        if isinstance(right, tuple):
            lefts[-1:] = in_hbm(left)
            gathered, steps, first = right
            piece = gathered.shape[2]
            rights.append(gathered)
            right_specs.append(
                pl.BlockSpec(
                    (block // piece, 1, piece, cols),
                    partial(lambda step, at, i: (i, step, 0, at), steps - 1, first // cols),
                )
            )
        else:
            rights.append(right)
            right_specs.append(
                pl.BlockSpec((block, cols), lambda i: (lax.axis_index("head") * n_blocks + i, 0))
            )
    part = pl.BlockSpec((rows, block), lambda i: (0, i))
    extra = [] if base is None else [base]
    return pl.pallas_call(
        partial(products_kernel, len(pairs), base is not None),
        grid=(n_blocks,),
        in_specs=left_specs + right_specs + [part] * len(extra),
        out_specs=part,
        out_shape=jax.ShapeDtypeStruct((rows, out_width), dtype),
        compiler_params=pltpu.CompilerParams(vmem_limit_bytes=20 * MIB),
        cost_estimate=pl.CostEstimate(flops=flops, bytes_accessed=8 * MIB, transcendentals=0),
        name=name,
    )(*lefts, *in_hbm(*rights), *extra)


def attention_kernel(
    first_ref, query_ref, grad_ref, kv0, kv1, kv2, kv3,
    out_ref, dq_ref, bundle_ref, d0, d2, d3,
    kv_ref, acc_ref, score_ref, sum_ref, sems,
):
    rows = query_ref.shape[0]
    copies = [
        pltpu.make_async_copy(block, kv_ref.at[pl.ds(slot * rows, rows), :], sems.at[slot])
        for slot, block in enumerate((kv3, kv2, kv1, kv0))
    ]
    for copy in copies:
        copy.start()
    acc_ref[...] = jnp.zeros_like(acc_ref)
    for copy in copies:
        copy.wait()
    factor = HD ** (-0.5)
    wide = GROUP * GRAIN
    streams = range(TILE // GRAIN)
    key_local = lax.broadcasted_iota(jnp.int32, (TILE, wide), 0)
    query_local = lax.broadcasted_iota(jnp.int32, (TILE, wide), 1) % GRAIN
    heads = [slice(h * HD, (h + 1) * HD) for h in range(GROUP)]

    def tile_rows(tile):
        return pl.ds(pl.multiple_of(tile * TILE, TILE), TILE)

    for pair in range(rows // TILE):
        places = [pl.ds(pair * TILE + g * GRAIN, GRAIN) for g in streams]
        query = [jnp.concatenate([query_ref[here, cols] for cols in heads], axis=0) for here in places]
        grad = [jnp.concatenate([grad_ref[here, cols] for cols in heads], axis=0) for here in places]
        first = [first_ref[pair * len(places) + g] for g in streams]
        last = (SPAN * rows) // TILE + pair
        low = first[0] // TILE
        sum_ref[...] = jnp.zeros_like(sum_ref)

        def score_tile(tile, carry, diagonal):
            here = tile_rows(tile)
            following = []
            for g in streams:
                top, total = carry[g]
                score = dot_nt(kv_ref[here, :HD], query[g]) * (factor * LOG2E)
                keep = key_local >= first[g] - tile * TILE
                if diagonal:
                    keep = keep & (key_local <= query_local + g * GRAIN)
                score = jnp.where(keep, score, NEG)
                score_ref[g, here, :] = score
                new_top = jnp.maximum(top, jnp.max(score, axis=0, keepdims=True))
                weight = jnp.sum(jnp.exp2(score - new_top), axis=0, keepdims=True)
                following.append((new_top, total * jnp.exp2(top - new_top) + weight))
            return tuple(following)

        state = tuple(
            (jnp.full((1, wide), NEG, jnp.float32), jnp.zeros((1, wide), jnp.float32)) for g in streams
        )
        state = lax.fori_loop(low, last, lambda tile, carry: score_tile(tile, carry, False), state)
        state = score_tile(last, state, True)
        lse = [top + jnp.log2(total) for top, total in state]

        def output_tile(tile, carry):
            here = tile_rows(tile)
            value_grad = acc_ref[here, HD:]
            for g in streams:
                prob = jnp.exp2(score_ref[g, here, :] - lse[g])
                score_ref[g, here, :] = prob
                prob = prob.astype(jnp.bfloat16)
                sum_ref[g] += dot_tn(kv_ref[here, HD:], prob)
                value_grad = value_grad + dot_nn(prob, grad[g])
            acc_ref[here, HD:] = value_grad
            return carry

        lax.fori_loop(low, last + 1, output_tile, 0)
        delta = []
        for g in streams:
            turned = sum_ref[g].astype(jnp.bfloat16).astype(jnp.float32)
            delta.append(
                jnp.sum(turned * grad[g].astype(jnp.float32).T, axis=0, keepdims=True)
            )
            out_rows = turned.T.astype(jnp.bfloat16)
            for head, cols in enumerate(heads):
                out_ref[places[g], cols] = out_rows[head * GRAIN : (head + 1) * GRAIN]
        sum_ref[...] = jnp.zeros_like(sum_ref)

        def gradient_tile(tile, carry):
            here = tile_rows(tile)
            key_grad = acc_ref[here, :HD]
            for g in streams:
                dprob = dot_nt(kv_ref[here, HD:], grad[g])
                dscore = (score_ref[g, here, :] * (dprob - delta[g])).astype(jnp.bfloat16)
                key_grad = key_grad + dot_nn(dscore, query[g])
                sum_ref[g] += dot_tn(kv_ref[here, :HD], dscore)
            acc_ref[here, :HD] = key_grad
            return carry

        lax.fori_loop(low, last + 1, gradient_tile, 0)
        for g in streams:
            turned = sum_ref[g] * factor
            dquery = turned.T.astype(jnp.bfloat16)
            for head, cols in enumerate(heads):
                part = slice(head * GRAIN, (head + 1) * GRAIN)
                dq_ref[places[g], cols] = dquery[part]
                bundle_ref[cols, places[g]] = turned[:, part].astype(jnp.bfloat16)
    cols = query_ref.shape[1]
    for distance, blocks in enumerate(
        ((d0,), (bundle_ref.at[cols:, : 2 * HD],), (d2,), (d3, bundle_ref.at[cols:, 2 * HD :]))
    ):
        place = pl.ds((SPAN - distance) * rows, rows)
        key_grad, value_grad = acc_ref[place, :HD] * factor, acc_ref[place, HD:]
        for block in blocks:
            block[:, :HD] = key_grad.astype(block.dtype)
            block[:, HD:] = value_grad.astype(block.dtype)


def attention(first, query, grad, kv_list):
    rows, cols = query.shape
    window = (SPAN + 1) * rows
    low = jax.ShapeDtypeStruct((rows, cols), jnp.bfloat16)
    bundle = jax.ShapeDtypeStruct((cols + rows, rows), jnp.bfloat16)
    own = jax.ShapeDtypeStruct((rows, 2 * HD), jnp.float32)
    sent = jax.ShapeDtypeStruct((rows, 2 * HD), jnp.bfloat16)
    vmem = pl.BlockSpec(memory_space=pltpu.VMEM)
    anywhere = pl.BlockSpec(memory_space=pl.ANY)
    return pl.pallas_call(
        attention_kernel,
        out_shape=(low, low, bundle, own, sent, sent),
        in_specs=[pl.BlockSpec(memory_space=pltpu.SMEM), vmem, vmem] + [anywhere] * (SPAN + 1),
        out_specs=(vmem,) * 6,
        scratch_shapes=[
            pltpu.VMEM((window, 2 * HD), jnp.bfloat16),
            pltpu.VMEM((window, 2 * HD), jnp.float32),
            pltpu.VMEM((TILE // GRAIN, window, GROUP * GRAIN), jnp.float32),
            pltpu.VMEM((TILE // GRAIN, HD, GROUP * GRAIN), jnp.float32),
            pltpu.SemaphoreType.DMA((SPAN + 1,)),
        ],
        compiler_params=pltpu.CompilerParams(vmem_limit_bytes=24 * MIB),
        cost_estimate=pl.CostEstimate(
            flops=6 * 2 * rows * window * cols, bytes_accessed=6 * MIB, transcendentals=0
        ),
        name="attention",
    )(first, query, grad, *kv_list)


def shift(value, axis, steps):
    count = lax.axis_size(axis)
    pairs = [(i, i + steps) for i in range(count) if 0 <= i + steps < count]
    return lax.ppermute(value, axis, pairs)


def swap(value, axis, mask):
    return lax.ppermute(value, axis, [(i, i ^ mask) for i in range(lax.axis_size(axis))])


def rotate(value, axis, steps):
    count = lax.axis_size(axis)
    return lax.ppermute(value, axis, [(i, (i + steps) % count) for i in range(count)])


def body(inputs, query_weight, key_weight, value_weight, out_grad, doc_lengths):
    tok_rows, width = inputs.shape
    n_ctx = lax.axis_size("ctx")
    n_head = lax.axis_size("head")
    chips = n_ctx // 2
    ctx = lax.axis_index("ctx")
    head = lax.axis_index("head")
    q_cols = query_weight.shape[1]
    k_cols = key_weight.shape[1]

    weights = (query_weight, key_weight, value_weight)
    out_width = width // n_head
    piece = out_width // n_ctx
    pieces = cut_rows(weights, n_head, piece)
    pieces, inputs = lax.optimization_barrier((pieces, inputs))
    order = sorted(range(1, n_head), key=lambda step: -min(step, n_head - step))
    moved_pieces = {step: rotate(pieces[step - 1], "head", step) for step in order}

    kv_loc = project(inputs, (key_weight, value_weight), "project_kv")
    kv_list = [kv_loc] + [shift(kv_loc, "ctx", distance) for distance in range(1, SPAN + 1)]
    other_inputs = swap(inputs, "ctx", 1)
    late_inputs, other_inputs, kv_loc = lax.optimization_barrier((inputs, other_inputs, kv_loc))
    query = project(late_inputs, (query_weight,), "project_query")
    pieces = [moved_pieces[step] for step in order]
    query, kv_list, pieces = lax.optimization_barrier((query, kv_list, pieces))
    pieces = [pieces[order.index(step)] for step in range(1, n_head)]
    gathered = lax.all_gather(jnp.concatenate(pieces, axis=0), "ctx", axis=0, tiled=True)
    gathered = gathered.reshape(n_ctx, n_head - 1, piece, q_cols + 2 * k_cols)

    granules = tok_rows // GRAIN
    window_start = (ctx - SPAN) * tok_rows
    positions = ctx * tok_rows + GRAIN * jnp.arange(granules, dtype=jnp.int32)
    doc_ends = jnp.cumsum(doc_lengths)
    starts = jnp.sum(
        jnp.where(doc_ends[None, :] <= positions[:, None], doc_lengths[None, :], 0), axis=1
    )
    attn_out, dq_low, bundle, own_grads, mid_grads, far_grads = attention(
        starts - window_start, query, out_grad, kv_list
    )

    other_bundle = swap(bundle, "ctx", 1)
    dq_up = rotate(dq_low, "head", 1)
    dq_down = rotate(dq_low, "head", -1)
    far = lax.ppermute(
        far_grads, "ctx", [(source, source - SPAN) for source in range(0, n_ctx, 2) if source >= SPAN]
    )
    kv_shape = (tok_rows, 2 * k_cols)
    merged, = small_kernel(merge_kernel, [(kv_shape, jnp.bfloat16)], "merge", mid_grads, other_bundle)
    merged, late_bundle = lax.optimization_barrier((merged, other_bundle))
    merged = shift(merged, "ctx", -2)

    q_terms = weight_terms(bundle, late_bundle, q_cols, inputs, other_inputs, n_ctx, "query_terms")
    q_moved = [swap(q_terms[chips - 1], "ctx", 2 * (chips - 1))]
    dq_far = rotate(dq_up, "head", 1)
    far, merged, dq_up, dq_down, dq_low, q_terms = lax.optimization_barrier(
        (far, merged, dq_up, dq_down, dq_low, q_terms)
    )
    dkv_low, dkv_turned = small_kernel(
        combine_kernel, [(kv_shape, jnp.bfloat16), (kv_shape[::-1], jnp.bfloat16)], "combine",
        own_grads, merged, far, other_bundle,
    )
    dkv_all = lax.all_gather(dkv_low, "head", axis=0, tiled=True)
    other_dkv = swap(dkv_turned, "ctx", 1)
    q_moved += [swap(q_terms[chip], "ctx", 2 * chip) for chip in range(1, chips - 1)]
    kv_terms = weight_terms(
        dkv_turned, other_dkv, 2 * k_cols, inputs, other_inputs, n_ctx, "key_terms"
    )
    kv_terms, dq_far = lax.optimization_barrier((kv_terms, dq_far))
    kv_moved = [swap(term, "ctx", 2 * chip) for chip, term in enumerate(kv_terms) if chip > 0]
    _, dq_low, dq_up, dq_down, dkv_low = lax.optimization_barrier((kv_terms, dq_low, dq_up, dq_down, dkv_low))

    grad_sum = products(
        (
            ((dq_low, 0, q_cols), query_weight),
            ((dq_up, 0, q_cols), (gathered, 1, 0)),
            ((dq_down, 0, q_cols), (gathered, 3, 0)),
            ((dq_far, 0, q_cols), (gathered, 2, 0)),
            ((dkv_low, 0, k_cols), key_weight),
            ((dkv_low, 1, k_cols), value_weight),
        ),
        None, out_width, n_head, jnp.float32, "products_near",
    )
    grad_sum, q_moved = lax.optimization_barrier((grad_sum, q_moved))
    q_grad, = weight_rows([q_terms[0], *q_moved], (q_cols,), "query_rows")
    q_grad, grad_sum = lax.optimization_barrier((q_grad, grad_sum))
    input_grad = products(
        [((dkv_all, step), (gathered, step, q_cols)) for step in range(1, n_head)],
        grad_sum, out_width, n_head, jnp.bfloat16, "products_far",
    )
    input_grad, kv_moved = lax.optimization_barrier((input_grad, kv_moved))
    k_grad, v_grad = weight_rows([kv_terms[0], *kv_moved], (k_cols, k_cols), "key_rows")
    return (attn_out, input_grad, q_grad, k_grad, v_grad)


def solution(mesh):
    return jax.shard_map(
        body,
        mesh=mesh,
        in_specs=(
            P("ctx", None),
            P(None, "head"),
            P(None, "head"),
            P(None, "head"),
            P("ctx", "head"),
            P(),
        ),
        out_specs=(P("ctx", "head"),) * 5,
        check_vma=False,
    )
```

```python
from functools import partial

import jax
import jax.numpy as jnp
from jax import lax
from jax.experimental import pallas as pl
from jax.experimental.pallas import tpu as pltpu
from jax.sharding import PartitionSpec as P

HD = 128
GROUP = 4
SPAN = 3
GRAIN = 128
TILE = 256
CHUNK = 512
MIB = 2**20

NEG = -1e30
LOG2E = 1.4426950408889634


def dot_nt(left_mat, right_mat):
    return lax.dot_general(
        left_mat, right_mat, (((1,), (1,)), ((), ())), preferred_element_type=jnp.float32
    )


def dot_tn(left_mat, right_mat):
    return lax.dot_general(
        left_mat, right_mat, (((0,), (0,)), ((), ())), preferred_element_type=jnp.float32
    )


def dot_nn(left_mat, right_mat):
    return jnp.dot(left_mat, right_mat, preferred_element_type=jnp.float32)


def in_hbm(*arrays):
    return [pltpu.with_memory_space_constraint(array, pltpu.HBM) for array in arrays]


def cut_kernel(*refs):
    weight_refs, piece_refs, sems = refs[:3], refs[3:-1], refs[-1]
    head, ctx = lax.axis_index("head"), lax.axis_index("ctx")
    n_head = len(piece_refs) + 1
    piece = piece_refs[0].shape[0]
    copies = []
    for distance, piece_ref in enumerate(piece_refs, 1):
        group = lax.rem(head + distance, n_head)
        first = group * (weight_refs[0].shape[0] // n_head) + ctx * piece
        at = 0
        for number, weight_ref in enumerate(weight_refs):
            cols = weight_ref.shape[1]
            copies.append(
                pltpu.make_async_copy(
                    weight_ref.at[pl.ds(pl.multiple_of(first, piece), piece), :],
                    piece_ref.at[:, pl.ds(at, cols)],
                    sems.at[distance - 1, number],
                )
            )
            at += cols
    for copy in copies:
        copy.start()
    for copy in copies:
        copy.wait()


def cut_rows(weights, n_head, piece):
    cols = sum(weight.shape[1] for weight in weights)
    anywhere = pl.BlockSpec(memory_space=pl.ANY)
    return pl.pallas_call(
        cut_kernel,
        out_shape=(jax.ShapeDtypeStruct((piece, cols), jnp.bfloat16),) * (n_head - 1),
        in_specs=[anywhere] * 3,
        out_specs=(pl.BlockSpec(memory_space=pltpu.VMEM),) * (n_head - 1),
        scratch_shapes=[pltpu.SemaphoreType.DMA((n_head - 1, 3))],
        cost_estimate=pl.CostEstimate(flops=0, bytes_accessed=2 * MIB, transcendentals=0),
        name="cut_rows",
    )(*in_hbm(*weights))


def project_kernel(x_ref, *refs):
    n = len(refs) - 4
    weight_refs, (out_ref, x_here, weight_here, sems) = refs[:n], refs[n:]
    rows = x_ref.shape[0]
    chunks = []
    for step in range(x_ref.shape[1] // CHUNK):
        part = pl.ds(step * CHUNK, CHUNK)
        copies = [pltpu.make_async_copy(x_ref.at[:, part], x_here.at[:, part], sems.at[step, 0])]
        at = 0
        for number, weight_ref in enumerate(weight_refs):
            cols = pl.ds(at, weight_ref.shape[1])
            at += weight_ref.shape[1]
            copies.append(
                pltpu.make_async_copy(
                    weight_ref.at[part, :], weight_here.at[part, cols], sems.at[step, 1 + number]
                )
            )
        for copy in copies:
            copy.start()
        chunks.append((part, copies))
    total = jnp.zeros((rows, weight_here.shape[1]), jnp.float32)
    for part, copies in chunks:
        for copy in copies:
            copy.wait()
        total = total + dot_nn(x_here[:, part], weight_here[part, :])
    out_ref[...] = total.astype(out_ref.dtype)


def project(inputs, weights, name):
    rows, width = inputs.shape
    cols = sum(weight.shape[1] for weight in weights)
    anywhere = pl.BlockSpec(memory_space=pl.ANY)
    return pl.pallas_call(
        project_kernel,
        in_specs=[anywhere] * (len(weights) + 1),
        out_specs=pl.BlockSpec(memory_space=pltpu.VMEM),
        out_shape=jax.ShapeDtypeStruct((rows, cols), jnp.bfloat16),
        scratch_shapes=[
            pltpu.VMEM((rows, width), jnp.bfloat16),
            pltpu.VMEM((width, cols), jnp.bfloat16),
            pltpu.SemaphoreType.DMA((width // CHUNK, len(weights) + 1)),
        ],
        compiler_params=pltpu.CompilerParams(vmem_limit_bytes=24 * MIB),
        cost_estimate=pl.CostEstimate(
            flops=2 * rows * width * cols, bytes_accessed=2 * width * (rows + cols), transcendentals=0
        ),
        name=name,
    )(*in_hbm(inputs, *weights))


def merge_kernel(d2_ref, bundle_ref, out_ref):
    rows, cols = out_ref.shape
    core = lax.axis_index("ctx") % 2
    here = pl.ds(bundle_ref.shape[0] - rows, rows)
    near, far = bundle_ref[here, :cols], bundle_ref[here, cols:]
    other = jnp.where(core == 1, near.astype(jnp.float32), far.astype(jnp.float32))
    out_ref[...] = (d2_ref[...].astype(jnp.float32) + other).astype(out_ref.dtype)


def combine_kernel(own_ref, merged_ref, far_ref, bundle_ref, low_ref, turned_ref):
    rows, cols = own_ref.shape
    core = lax.axis_index("ctx") % 2
    near = bundle_ref[bundle_ref.shape[0] - rows :, :cols].astype(jnp.float32)
    total = own_ref[...] + merged_ref[...].astype(jnp.float32) + far_ref[...].astype(jnp.float32)
    total = total + jnp.where(core == 0, near, 0.0)
    low_ref[...] = total.astype(jnp.bfloat16)
    turned_ref[...] = total.T.astype(jnp.bfloat16)


def small_kernel(kernel, shapes, name, *operands):
    def whole(shape):
        return pl.BlockSpec(shape, lambda i: (0, 0))

    return pl.pallas_call(
        kernel,
        grid=(1,),
        out_shape=tuple(jax.ShapeDtypeStruct(shape, dtype) for shape, dtype in shapes),
        in_specs=[whole(operand.shape) for operand in operands],
        out_specs=tuple(whole(shape) for shape, dtype in shapes),
        compiler_params=pltpu.CompilerParams(vmem_limit_bytes=20 * MIB),
        cost_estimate=pl.CostEstimate(flops=4 * MIB, bytes_accessed=4 * MIB, transcendentals=0),
        name=name,
    )(*operands)


def terms_kernel(chips, turned_ref, other_turned_ref, x_ref, other_x_ref, *refs):
    out_refs, (x_here, sum_here, low_here, in_sems, out_sems) = refs[:chips], refs[chips:]
    cols, kept = out_refs[0].shape
    ctx = lax.axis_index("ctx")
    order = [*range(1, chips), 0]
    coming = {}
    for chip in order:
        first = pl.multiple_of((((ctx // 2) ^ chip) * 2 + ctx % 2) * kept, kept)
        coming[chip] = [
            pltpu.make_async_copy(ref.at[:, pl.ds(first, kept)], x_here.at[chip, side], in_sems.at[chip, side])
            for side, ref in enumerate((x_ref, other_x_ref))
        ]
        for copy in coming[chip]:
            copy.start()
    going = []
    for chip in order:
        for copy in coming[chip]:
            copy.wait()
        term = dot_nn(turned_ref[:cols, :], x_here[chip, 0]) + dot_nn(other_turned_ref[:cols, :], x_here[chip, 1])
        here = sum_here if chip == 0 else low_here.at[chip]
        here[...] = term.astype(here.dtype)
        copy = pltpu.make_async_copy(here, out_refs[chip], out_sems.at[chip])
        copy.start()
        going.append(copy)
    for copy in going:
        copy.wait()


def weight_terms(turned, other_turned, cols, inputs, other_inputs, n_ctx, name):
    rows = turned.shape[1]
    kept = inputs.shape[1] // n_ctx
    chips = n_ctx // 2
    vmem = pl.BlockSpec(memory_space=pltpu.VMEM)
    anywhere = pl.BlockSpec(memory_space=pl.ANY)
    return pl.pallas_call(
        partial(terms_kernel, chips),
        in_specs=[vmem, vmem, anywhere, anywhere],
        out_specs=(anywhere,) * chips,
        out_shape=tuple(
            jax.ShapeDtypeStruct((cols, kept), jnp.float32 if chip == 0 else jnp.bfloat16)
            for chip in range(chips)
        ),
        scratch_shapes=[
            pltpu.VMEM((chips, 2, rows, kept), jnp.bfloat16),
            pltpu.VMEM((cols, kept), jnp.float32),
            pltpu.VMEM((chips, cols, kept), jnp.bfloat16),
            pltpu.SemaphoreType.DMA((chips, 2)),
            pltpu.SemaphoreType.DMA((chips,)),
        ],
        compiler_params=pltpu.CompilerParams(vmem_limit_bytes=24 * MIB),
        cost_estimate=pl.CostEstimate(
            flops=4 * cols * rows * kept * chips, bytes_accessed=10 * MIB, transcendentals=0
        ),
        name=name,
    )(turned, other_turned, *in_hbm(inputs, other_inputs))


def rows_kernel(n_in, *refs):
    in_refs, out_refs = refs[:n_in], refs[n_in:]
    total = in_refs[0][...]
    for in_ref in in_refs[1:]:
        total += in_ref[...].astype(jnp.float32)
    at = 0
    for out_ref in out_refs:
        cols = slice(at, at + out_ref.shape[1])
        at = cols.stop
        out_ref[...] = total[cols, :].T


def weight_rows(terms, widths, name):
    kept = terms[0].shape[1]
    shapes = [((kept, width), jnp.float32) for width in widths]
    return small_kernel(partial(rows_kernel, len(terms)), shapes, name, *terms)


def products_kernel(count, has_base, *refs):
    left_refs, rows_refs, out_ref = refs[:count], refs[count : 2 * count], refs[-1]
    total = refs[2 * count][...] if has_base else None
    for left_ref, rows_ref in zip(left_refs, rows_refs):
        rows = rows_ref[...]
        term = dot_nt(left_ref[...], rows.reshape(-1, rows.shape[-1]))
        total = term if total is None else total + term
    out_ref[...] = total.astype(out_ref.dtype)


def products(pairs, base, out_width, n_head, dtype, name):
    rows = base.shape[0] if base is not None else pairs[0][0][0].shape[0]
    block = 512
    n_blocks = out_width // block
    left_specs, right_specs, lefts, rights = [], [], [], []
    flops = 0
    for (left, *place), right in pairs:
        lefts.append(left)
        if len(place) == 2:
            column, cols = place
            left_specs.append(pl.BlockSpec((rows, cols), partial(lambda column, i: (0, column), column)))
        else:
            cols = left.shape[1]
            left_specs.append(
                pl.BlockSpec(
                    (rows, cols),
                    partial(
                        lambda steps, i: ((lax.axis_index("head") + n_head - steps) % n_head, 0), place[0]
                    ),
                )
            )
        flops += 2 * rows * cols * out_width
        if isinstance(right, tuple):
            lefts[-1:] = in_hbm(left)
            gathered, steps, first = right
            piece = gathered.shape[2]
            rights.append(gathered)
            right_specs.append(
                pl.BlockSpec(
                    (block // piece, 1, piece, cols),
                    partial(lambda step, at, i: (i, step, 0, at), steps - 1, first // cols),
                )
            )
        else:
            rights.append(right)
            right_specs.append(
                pl.BlockSpec((block, cols), lambda i: (lax.axis_index("head") * n_blocks + i, 0))
            )
    part = pl.BlockSpec((rows, block), lambda i: (0, i))
    extra = [] if base is None else [base]
    return pl.pallas_call(
        partial(products_kernel, len(pairs), base is not None),
        grid=(n_blocks,),
        in_specs=left_specs + right_specs + [part] * len(extra),
        out_specs=part,
        out_shape=jax.ShapeDtypeStruct((rows, out_width), dtype),
        compiler_params=pltpu.CompilerParams(vmem_limit_bytes=20 * MIB),
        cost_estimate=pl.CostEstimate(flops=flops, bytes_accessed=8 * MIB, transcendentals=0),
        name=name,
    )(*lefts, *in_hbm(*rights), *extra)


def attention_kernel(
    first_ref, query_ref, grad_ref, kv0, kv1, kv2, kv3,
    out_ref, dq_ref, bundle_ref, d0, d2, d3,
    kv_ref, acc_ref, score_ref, sum_ref, sems,
):
    rows = query_ref.shape[0]
    copies = [
        pltpu.make_async_copy(block, kv_ref.at[pl.ds(slot * rows, rows), :], sems.at[slot])
        for slot, block in enumerate((kv3, kv2, kv1, kv0))
    ]
    for copy in copies:
        copy.start()
    acc_ref[...] = jnp.zeros_like(acc_ref)
    for copy in copies:
        copy.wait()
    factor = HD ** (-0.5)
    wide = GROUP * GRAIN
    streams = range(TILE // GRAIN)
    key_local = lax.broadcasted_iota(jnp.int32, (TILE, wide), 0)
    query_local = lax.broadcasted_iota(jnp.int32, (TILE, wide), 1) % GRAIN
    heads = [slice(h * HD, (h + 1) * HD) for h in range(GROUP)]

    def tile_rows(tile):
        return pl.ds(pl.multiple_of(tile * TILE, TILE), TILE)

    for pair in range(rows // TILE):
        places = [pl.ds(pair * TILE + g * GRAIN, GRAIN) for g in streams]
        query = [jnp.concatenate([query_ref[here, cols] for cols in heads], axis=0) for here in places]
        grad = [jnp.concatenate([grad_ref[here, cols] for cols in heads], axis=0) for here in places]
        first = [first_ref[pair * len(places) + g] for g in streams]
        last = (SPAN * rows) // TILE + pair
        low = first[0] // TILE
        sum_ref[...] = jnp.zeros_like(sum_ref)

        def score_tile(tile, carry, diagonal):
            here = tile_rows(tile)
            following = []
            for g in streams:
                top, total = carry[g]
                score = dot_nt(kv_ref[here, :HD], query[g]) * (factor * LOG2E)
                keep = key_local >= first[g] - tile * TILE
                if diagonal:
                    keep = keep & (key_local <= query_local + g * GRAIN)
                score = jnp.where(keep, score, NEG)
                score_ref[g, here, :] = score
                new_top = jnp.maximum(top, jnp.max(score, axis=0, keepdims=True))
                weight = jnp.sum(jnp.exp2(score - new_top), axis=0, keepdims=True)
                following.append((new_top, total * jnp.exp2(top - new_top) + weight))
            return tuple(following)

        state = tuple(
            (jnp.full((1, wide), NEG, jnp.float32), jnp.zeros((1, wide), jnp.float32)) for g in streams
        )
        state = lax.fori_loop(low, last, lambda tile, carry: score_tile(tile, carry, False), state)
        state = score_tile(last, state, True)
        lse = [top + jnp.log2(total) for top, total in state]

        def output_tile(tile, carry):
            here = tile_rows(tile)
            value_grad = acc_ref[here, HD:]
            for g in streams:
                prob = jnp.exp2(score_ref[g, here, :] - lse[g])
                score_ref[g, here, :] = prob
                prob = prob.astype(jnp.bfloat16)
                sum_ref[g] += dot_tn(kv_ref[here, HD:], prob)
                value_grad = value_grad + dot_nn(prob, grad[g])
            acc_ref[here, HD:] = value_grad
            return carry

        lax.fori_loop(low, last + 1, output_tile, 0)
        delta = []
        for g in streams:
            turned = sum_ref[g].astype(jnp.bfloat16).astype(jnp.float32)
            delta.append(
                jnp.sum(turned * grad[g].astype(jnp.float32).T, axis=0, keepdims=True)
            )
            out_rows = turned.T.astype(jnp.bfloat16)
            for head, cols in enumerate(heads):
                out_ref[places[g], cols] = out_rows[head * GRAIN : (head + 1) * GRAIN]
        sum_ref[...] = jnp.zeros_like(sum_ref)

        def gradient_tile(tile, carry):
            here = tile_rows(tile)
            key_grad = acc_ref[here, :HD]
            for g in streams:
                dprob = dot_nt(kv_ref[here, HD:], grad[g])
                dscore = (score_ref[g, here, :] * (dprob - delta[g])).astype(jnp.bfloat16)
                key_grad = key_grad + dot_nn(dscore, query[g])
                sum_ref[g] += dot_tn(kv_ref[here, :HD], dscore)
            acc_ref[here, :HD] = key_grad
            return carry

        lax.fori_loop(low, last + 1, gradient_tile, 0)
        for g in streams:
            turned = sum_ref[g] * factor
            dquery = turned.T.astype(jnp.bfloat16)
            for head, cols in enumerate(heads):
                part = slice(head * GRAIN, (head + 1) * GRAIN)
                dq_ref[places[g], cols] = dquery[part]
                bundle_ref[cols, places[g]] = turned[:, part].astype(jnp.bfloat16)
    cols = query_ref.shape[1]
    for distance, blocks in enumerate(
        ((d0,), (bundle_ref.at[cols:, : 2 * HD],), (d2,), (d3, bundle_ref.at[cols:, 2 * HD :]))
    ):
        place = pl.ds((SPAN - distance) * rows, rows)
        key_grad, value_grad = acc_ref[place, :HD] * factor, acc_ref[place, HD:]
        for block in blocks:
            block[:, :HD] = key_grad.astype(block.dtype)
            block[:, HD:] = value_grad.astype(block.dtype)


def attention(first, query, grad, kv_list):
    rows, cols = query.shape
    window = (SPAN + 1) * rows
    low = jax.ShapeDtypeStruct((rows, cols), jnp.bfloat16)
    bundle = jax.ShapeDtypeStruct((cols + rows, rows), jnp.bfloat16)
    own = jax.ShapeDtypeStruct((rows, 2 * HD), jnp.float32)
    sent = jax.ShapeDtypeStruct((rows, 2 * HD), jnp.bfloat16)
    vmem = pl.BlockSpec(memory_space=pltpu.VMEM)
    anywhere = pl.BlockSpec(memory_space=pl.ANY)
    return pl.pallas_call(
        attention_kernel,
        out_shape=(low, low, bundle, own, sent, sent),
        in_specs=[pl.BlockSpec(memory_space=pltpu.SMEM), vmem, vmem] + [anywhere] * (SPAN + 1),
        out_specs=(vmem,) * 6,
        scratch_shapes=[
            pltpu.VMEM((window, 2 * HD), jnp.bfloat16),
            pltpu.VMEM((window, 2 * HD), jnp.float32),
            pltpu.VMEM((TILE // GRAIN, window, GROUP * GRAIN), jnp.float32),
            pltpu.VMEM((TILE // GRAIN, HD, GROUP * GRAIN), jnp.float32),
            pltpu.SemaphoreType.DMA((SPAN + 1,)),
        ],
        compiler_params=pltpu.CompilerParams(vmem_limit_bytes=24 * MIB),
        cost_estimate=pl.CostEstimate(
            flops=6 * 2 * rows * window * cols, bytes_accessed=6 * MIB, transcendentals=0
        ),
        name="attention",
    )(first, query, grad, *kv_list)


def shift(value, axis, steps):
    count = lax.axis_size(axis)
    pairs = [(i, i + steps) for i in range(count) if 0 <= i + steps < count]
    return lax.ppermute(value, axis, pairs)


def swap(value, axis, mask):
    return lax.ppermute(value, axis, [(i, i ^ mask) for i in range(lax.axis_size(axis))])


def rotate(value, axis, steps):
    count = lax.axis_size(axis)
    return lax.ppermute(value, axis, [(i, (i + steps) % count) for i in range(count)])


def body(inputs, query_weight, key_weight, value_weight, out_grad, doc_lengths):
    tok_rows, width = inputs.shape
    n_ctx = lax.axis_size("ctx")
    n_head = lax.axis_size("head")
    chips = n_ctx // 2
    ctx = lax.axis_index("ctx")
    head = lax.axis_index("head")
    q_cols = query_weight.shape[1]
    k_cols = key_weight.shape[1]

    weights = (query_weight, key_weight, value_weight)
    out_width = width // n_head
    piece = out_width // n_ctx
    pieces = cut_rows(weights, n_head, piece)
    pieces, inputs = lax.optimization_barrier((pieces, inputs))
    order = sorted(range(1, n_head), key=lambda step: -min(step, n_head - step))
    moved_pieces = {step: rotate(pieces[step - 1], "head", step) for step in order}

    kv_loc = project(inputs, (key_weight, value_weight), "project_kv")
    kv_list = [kv_loc] + [shift(kv_loc, "ctx", distance) for distance in range(1, SPAN + 1)]
    other_inputs = swap(inputs, "ctx", 1)
    late_inputs, other_inputs, kv_loc = lax.optimization_barrier((inputs, other_inputs, kv_loc))
    query = project(late_inputs, (query_weight,), "project_query")
    pieces = [moved_pieces[step] for step in order]
    query, kv_list, pieces = lax.optimization_barrier((query, kv_list, pieces))
    pieces = [pieces[order.index(step)] for step in range(1, n_head)]
    gathered = lax.all_gather(jnp.concatenate(pieces, axis=0), "ctx", axis=0, tiled=True)
    gathered = gathered.reshape(n_ctx, n_head - 1, piece, q_cols + 2 * k_cols)

    granules = tok_rows // GRAIN
    window_start = (ctx - SPAN) * tok_rows
    positions = ctx * tok_rows + GRAIN * jnp.arange(granules, dtype=jnp.int32)
    doc_ends = jnp.cumsum(doc_lengths)
    starts = jnp.sum(
        jnp.where(doc_ends[None, :] <= positions[:, None], doc_lengths[None, :], 0), axis=1
    )
    attn_out, dq_low, bundle, own_grads, mid_grads, far_grads = attention(
        starts - window_start, query, out_grad, kv_list
    )

    other_bundle = swap(bundle, "ctx", 1)
    dq_up = rotate(dq_low, "head", 1)
    dq_down = rotate(dq_low, "head", -1)
    far = lax.ppermute(
        far_grads, "ctx", [(source, source - SPAN) for source in range(0, n_ctx, 2) if source >= SPAN]
    )
    kv_shape = (tok_rows, 2 * k_cols)
    merged, = small_kernel(merge_kernel, [(kv_shape, jnp.bfloat16)], "merge", mid_grads, other_bundle)
    merged, late_bundle = lax.optimization_barrier((merged, other_bundle))
    merged = shift(merged, "ctx", -2)

    q_terms = weight_terms(bundle, late_bundle, q_cols, inputs, other_inputs, n_ctx, "query_terms")
    q_moved = [swap(q_terms[chips - 1], "ctx", 2 * (chips - 1))]
    dq_far = rotate(dq_up, "head", 1)
    far, merged, dq_up, dq_down, dq_low, q_terms = lax.optimization_barrier(
        (far, merged, dq_up, dq_down, dq_low, q_terms)
    )
    dkv_low, dkv_turned = small_kernel(
        combine_kernel, [(kv_shape, jnp.bfloat16), (kv_shape[::-1], jnp.bfloat16)], "combine",
        own_grads, merged, far, other_bundle,
    )
    dkv_all = lax.all_gather(dkv_low, "head", axis=0, tiled=True)
    other_dkv = swap(dkv_turned, "ctx", 1)
    q_terms, other_dkv = lax.optimization_barrier((q_terms, other_dkv))
    q_moved += [swap(q_terms[chip], "ctx", 2 * chip) for chip in range(1, chips - 1)]
    kv_terms = weight_terms(
        dkv_turned, other_dkv, 2 * k_cols, inputs, other_inputs, n_ctx, "key_terms"
    )
    kv_terms, dq_far = lax.optimization_barrier((kv_terms, dq_far))
    kv_moved = [swap(term, "ctx", 2 * chip) for chip, term in enumerate(kv_terms) if chip > 0]
    _, dq_low, dq_up, dq_down, dkv_low = lax.optimization_barrier((kv_terms, dq_low, dq_up, dq_down, dkv_low))

    grad_sum = products(
        (
            ((dq_low, 0, q_cols), query_weight),
            ((dq_up, 0, q_cols), (gathered, 1, 0)),
            ((dq_down, 0, q_cols), (gathered, 3, 0)),
            ((dq_far, 0, q_cols), (gathered, 2, 0)),
            ((dkv_low, 0, k_cols), key_weight),
            ((dkv_low, 1, k_cols), value_weight),
        ),
        None, out_width, n_head, jnp.float32, "products_near",
    )
    grad_sum, q_moved = lax.optimization_barrier((grad_sum, q_moved))
    q_grad, = weight_rows([q_terms[0], *q_moved], (q_cols,), "query_rows")
    q_grad, grad_sum = lax.optimization_barrier((q_grad, grad_sum))
    input_grad = products(
        [((dkv_all, step), (gathered, step, q_cols)) for step in range(1, n_head)],
        grad_sum, out_width, n_head, jnp.bfloat16, "products_far",
    )
    input_grad, kv_moved = lax.optimization_barrier((input_grad, kv_moved))
    k_grad, v_grad = weight_rows([kv_terms[0], *kv_moved], (k_cols, k_cols), "key_rows")
    return (attn_out, input_grad, q_grad, k_grad, v_grad)


def solution(mesh):
    return jax.shard_map(
        body,
        mesh=mesh,
        in_specs=(
            P("ctx", None),
            P(None, "head"),
            P(None, "head"),
            P(None, "head"),
            P("ctx", "head"),
            P(),
        ),
        out_specs=(P("ctx", "head"),) * 5,
        check_vma=False,
    )
```
